32 devices in a mesh: tab: 8 (over y, x, core), blk: 4 (over z).
Axes of the slice: x: 2, y: 2, z: 4, core: 2. Of those that a mesh axis runs over, the one named last changes fastest.
Arguments:
- cells: bfloat16 [8, 1024, 3, 512], P('tab', 'blk'), may hold values from -6 to 6
- missing: int32 [8, 1024, 3], P('tab', 'blk'), may hold values 0 or 1
- context: int32 [8, 1024], P('tab', 'blk'), may hold values from 0 to 1, as said below
- cotangent: bfloat16 [8, 1024, 3, 512], P('tab', 'blk'), may hold values from -6 to 6
- miss_embed: bfloat16 [512], replicated, may hold values from -4 to 4
- norm1_gain: bfloat16 [512], replicated, may hold values from 0.5 to 1.5
- norm1_shift: bfloat16 [512], replicated, may hold values from -2 to 2
- feat_qkv: bfloat16 [512, 1536], replicated, may hold values from -0.375 to 0.375
- feat_out: bfloat16 [512, 512], replicated, may hold values from -0.25 to 0.25
- norm2_gain: bfloat16 [512], replicated, may hold values from 0.5 to 1.5
- norm2_shift: bfloat16 [512], replicated, may hold values from -2 to 2
- row_qkv: bfloat16 [512, 1536], replicated, may hold values from -0.375 to 0.375
- row_out: bfloat16 [512, 512], replicated, may hold values from -2 to 2
- norm3_gain: bfloat16 [512], replicated, may hold values from 0.5 to 1.5
- norm3_shift: bfloat16 [512], replicated, may hold values from -2 to 2
- ff_in: bfloat16 [512, 2048], replicated, may hold values from -0.25 to 0.25
- ff_in_bias: bfloat16 [2048], replicated, may hold values from -2 to 2
- ff_out: bfloat16 [2048, 512], replicated, may hold values from -0.1875 to 0.1875
- ff_out_bias: bfloat16 [512], replicated, may hold values from -2 to 2
Outputs:
- activations: bfloat16 [8, 1024, 3, 512], P('tab', 'blk')
- input_grad: float32 [8, 1024, 3, 512], P('tab', 'blk')
- grad_miss_embed: float32 [512], replicated
- grad_norm1_gain: float32 [512], replicated
- grad_norm1_shift: float32 [512], replicated
- grad_feat_qkv: float32 [512, 1536], replicated
- grad_feat_out: float32 [512, 512], replicated
- grad_norm2_gain: float32 [512], replicated
- grad_norm2_shift: float32 [512], replicated
- grad_row_qkv: float32 [512, 1536], replicated
- grad_row_out: float32 [512, 512], replicated
- grad_norm3_gain: float32 [512], replicated
- grad_norm3_shift: float32 [512], replicated
- grad_ff_in: float32 [512, 2048], replicated
- grad_ff_in_bias: float32 [2048], replicated
- grad_ff_out: float32 [2048, 512], replicated
- grad_ff_out_bias: float32 [512], replicated
The draws below stay inside these ranges and needn't reach their ends.
Inputs may be any that keep to these rules, and one draw needn't show every extreme that they name: Row 0 of every table is a context row.
All inputs are finite; a program needn't handle non-finite values. No bound on the sum of `missing` on one device may be relied on, other than what follows from the above.
Results may differ from the reference program's by a relative error of at most 0.023.
The reference program's roundings to bfloat16 on the way count: a program that leaves them out, or rounds other values in their place, can miss the bound.
Values may be sent and summed in bfloat16 or wider, within the bound.
A program may use at most 128 MiB of HBM per device.

```python
import math
import jax
import jax.numpy as jnp
from jax import lax

D = 512
HEADS = 4
HEAD = 128
FF = 2048
COLS = 3
TABLES = 8
ROWS = 1024


def draw_context(key, part):
    key = jax.random.fold_in(key, 7)
    level_key, roll_key = jax.random.split(key)
    share_level = jax.random.randint(level_key, (TABLES, 1), 40, 91)
    rolled = jax.random.randint(roll_key, (TABLES, ROWS), 0, 100)
    context_flags = (rolled < share_level).astype(jnp.int32)
    return context_flags.at[:, 0].set(1)


def set_ends(entries, rng, smallest, largest):
    spot = [jax.random.randint(jax.random.fold_in(rng, axis), (), 0, length) for axis, length in enumerate(entries.shape)]
    widest = entries.shape.index(max(entries.shape))
    neighbour = spot[:widest] + [(spot[widest] + 1) % entries.shape[widest]] + spot[widest + 1:]
    return entries.at[tuple(spot)].set(smallest).at[tuple(neighbour)].set(largest)


def shard_levels(own_key, dims, cuts, least, largest):
    level = 1.0
    for position, shards_of in cuts:
        draws = jax.random.uniform(jax.random.fold_in(jax.random.fold_in(own_key, 6), position), (shards_of,), jnp.float32, least / len(cuts), largest / len(cuts))
        level = level * jnp.repeat(jnp.exp(draws), dims[position] // shards_of).reshape((-1,) + (1,) * (len(dims) - 1 - position))
    return level


def centred(key, shape, deviation, reach, shards=(), dtype=jnp.bfloat16):
    drawn = jax.random.normal(key, shape, jnp.float32) * deviation
    if len(shards) > 0:
        drawn = shard_levels(key, shape, shards, -0.22, 0.18) * drawn
    return jnp.clip(drawn, min=-reach, max=reach).astype(dtype)


def setup_inputs(seed: int = 0) -> dict:
    key_of = jax.random.split(jax.random.key(seed), 20)
    cells = centred(key_of[0], (TABLES, ROWS, COLS, D), 1.0, 6.0, ((0, 8), (1, 4)))
    missing = set_ends((jax.random.randint(key_of[1], (TABLES, ROWS, COLS), 0, 5) < 1).astype(jnp.int32), jax.random.fold_in(key_of[1], 1), 0, 1)
    context = draw_context(jax.random.fold_in(key_of[19], 71), 0)
    cotangent = centred(key_of[3], (TABLES, ROWS, COLS, D), 1.0, 6.0, ((0, 8), (1, 4)))
    miss_embed = centred(key_of[4], (D,), 1.0, 4.0)
    norm1_gain = jnp.clip(1.0 + 0.1 * jax.random.normal(key_of[5], (D,), jnp.float32), 0.5, 1.5).astype(jnp.bfloat16)
    norm1_shift = centred(key_of[6], (D,), 0.3, 2.0)
    feat_qkv = centred(key_of[7], (D, 3 * D), (D // 2) ** -0.5, 0.375)
    feat_out = centred(key_of[8], (D, D), D ** -0.5, 0.25)
    norm2_gain = jnp.clip(1.0 + 0.1 * jax.random.normal(key_of[9], (D,), jnp.float32), 0.5, 1.5).astype(jnp.bfloat16)
    norm2_shift = centred(key_of[10], (D,), 0.3, 2.0)
    row_qkv = centred(key_of[11], (D, 3 * D), (D // 2) ** -0.5, 0.375)
    row_out = centred(key_of[12], (D, D), (max(D * 16 // ROWS, 1)) ** -0.5, 2.0)
    norm3_gain = jnp.clip(1.0 + 0.1 * jax.random.normal(key_of[13], (D,), jnp.float32), 0.5, 1.5).astype(jnp.bfloat16)
    norm3_shift = centred(key_of[14], (D,), 0.3, 2.0)
    ff_in = centred(key_of[15], (D, FF), D ** -0.5, 0.25)
    ff_in_bias = centred(key_of[16], (FF,), 0.3, 2.0)
    ff_out = centred(key_of[17], (FF, D), (FF // 2) ** -0.5, 0.1875)
    ff_out_bias = centred(key_of[18], (D,), 0.3, 2.0)
    return {"cells": cells, "missing": missing, "context": context, "cotangent": cotangent, "miss_embed": miss_embed, "norm1_gain": norm1_gain, "norm1_shift": norm1_shift, "feat_qkv": feat_qkv, "feat_out": feat_out, "norm2_gain": norm2_gain, "norm2_shift": norm2_shift, "row_qkv": row_qkv, "row_out": row_out, "norm3_gain": norm3_gain, "norm3_shift": norm3_shift, "ff_in": ff_in, "ff_in_bias": ff_in_bias, "ff_out": ff_out, "ff_out_bias": ff_out_bias}


@jax.custom_vjp
def low(v):
    return lax.optimization_barrier(v.astype(jnp.bfloat16)).astype(jnp.float32)

@jax.custom_vjp
def low_back(v):
    return v

def low_keep(v):
    return (low(v), None)

def low_pass(kept, grad):
    return (grad,)

def back_keep(v):
    return (v, None)

def back_low(kept, grad):
    return (low(grad),)
low.defvjp(low_keep, low_pass)
low_back.defvjp(back_keep, back_low)
highest = lax.Precision.HIGHEST
epsilon = 1e-05
masked_score = -1e+30

def normalize(inputs, scales, shifts):
    center = inputs - lax.optimization_barrier(jnp.mean(inputs, axis=-1, keepdims=True))
    spread = lax.optimization_barrier(jnp.mean(center * center, axis=-1, keepdims=True))
    return center * lax.rsqrt(spread + epsilon) * scales + shifts

def project(inputs, weight):
    return jnp.einsum('...d,df->...f', inputs, weight, precision=highest)

def split_heads(packed):
    pieces = packed.reshape(packed.shape[:-1] + (3, HEADS, HEAD))
    return (pieces[..., 0, :, :], pieces[..., 1, :, :], pieces[..., 2, :, :])

def table_forward(table_cells, embedding, params, missing_table, context_table):
    gain_one, shift_one, feat_qkv, feat_out, gain_two, shift_two, row_qkv, row_out, gain_three, shift_three, ff_in, ff_in_bias, ff_out, ff_out_bias = params
    score_scale = 1.0 / math.sqrt(HEAD)
    base_cells = jnp.where(missing_table[..., None] > 0, embedding, table_cells)
    normed = low(normalize(base_cells, gain_one, shift_one))
    queries, key_heads, values = split_heads(low_back(low(project(normed, feat_qkv))))
    scores = low_back(jnp.einsum('rihe,rjhe->rhij', queries, key_heads, precision=highest) * score_scale)
    weights = low(jax.nn.softmax(scores, axis=-1))
    attended = low_back(low(jnp.einsum('rhij,rjhe->rihe', weights, values, precision=highest)))
    after_feat = base_cells + low_back(project(attended.reshape(base_cells.shape), feat_out))
    normed = low(normalize(after_feat, gain_two, shift_two))
    queries, key_heads, values = split_heads(low_back(low(project(normed, row_qkv))))
    scores = low_back(jnp.einsum('iche,jche->chij', queries, key_heads, precision=highest) * score_scale)
    scores = jnp.where(context_table[None, None, None, :] > 0, scores, masked_score)
    weights = low(jax.nn.softmax(scores, axis=-1))
    attended = low_back(low(jnp.einsum('chij,jche->iche', weights, values, precision=highest)))
    after_rows = after_feat + low_back(project(attended.reshape(after_feat.shape), row_out))
    normed = low(normalize(after_rows, gain_three, shift_three))
    inner_act = low_back(project(normed, ff_in) + ff_in_bias)
    hidden = low(jax.nn.gelu(inner_act))
    return after_rows + low_back(project(hidden, ff_out) + ff_out_bias)

def reference(cells, missing, context, cotangent, miss_embed, norm1_gain, norm1_shift, feat_qkv, feat_out, norm2_gain, norm2_shift, row_qkv, row_out, norm3_gain, norm3_shift, ff_in, ff_in_bias, ff_out, ff_out_bias):
    params = tuple((weight.astype(jnp.float32) for weight in (norm1_gain, norm1_shift, feat_qkv, feat_out, norm2_gain, norm2_shift, row_qkv, row_out, norm3_gain, norm3_shift, ff_in, ff_in_bias, ff_out, ff_out_bias)))
    embedding = miss_embed.astype(jnp.float32)

    def per_table(totals, table_item):
        table_cells, missing_table, context_table, table_cot = table_item

        def forward_fn(inputs, embed_vec, weights_in):
            return table_forward(inputs, embed_vec, weights_in, missing_table, context_table)
        result, pullback = jax.vjp(forward_fn, table_cells.astype(jnp.float32), embedding, params)
        grad_cells, grad_embed, grad_params = pullback(table_cot.astype(jnp.float32))
        totals = jax.tree.map(jnp.add, totals, (grad_embed, grad_params))
        return (totals, (result.astype(jnp.bfloat16), grad_cells))
    zero_totals = jax.tree.map(jnp.zeros_like, (embedding, params))
    totals, (results, grads_in) = lax.scan(per_table, zero_totals, (cells, missing, context, cotangent))
    grad_embed, grad_params = totals
    g_gain_one, g_shift_one, g_feat_qkv, g_feat_out, g_gain_two, g_shift_two, g_row_qkv, g_row_out, g_gain_three, g_shift_three, g_ff_in, g_ff_in_bias, g_ff_out, g_ff_out_bias = grad_params
    return (results, grads_in, grad_embed, g_gain_one, g_shift_one, g_feat_qkv, g_feat_out, g_gain_two, g_shift_two, g_row_qkv, g_row_out, g_gain_three, g_shift_three, g_ff_in, g_ff_in_bias, g_ff_out, g_ff_out_bias)
```

```python
import functools
import math

import jax
import jax.numpy as jnp
from jax import lax
from jax.experimental import pallas as pl
from jax.experimental.pallas import tpu as pltpu
from jax.sharding import PartitionSpec as P

HEADS = 4
HEAD = 128
EPS = 1e-05
SCALE = 1.0 / math.sqrt(HEAD)
MESH = pl.DeviceIdType.MESH
F32 = jnp.float32
BF16 = jnp.bfloat16
EMBED, GAIN1, SHIFT1, GAIN2, SHIFT2, GAIN3, SHIFT3, OUT_BIAS, IN_BIAS = range(9)
B_FF_OUT, B_FF_IN, B_ROW_OUT, B_ROW_QKV, B_FEAT_OUT, B_FEAT_QKV = 0, 4, 8, 9, 12, 13
BLOCKS = 16
CHUNK = 64


def dot(a, b):
    return jnp.dot(a, b, preferred_element_type=F32)


def dot_rt(a, b):
    return lax.dot_general(a, b, (((1,), (1,)), ((), ())), preferred_element_type=F32)


def dot_lt(a, b):
    return lax.dot_general(a, b, (((0,), (0,)), ((), ())), preferred_element_type=F32)


def stats(x):
    center = x - jnp.mean(x, axis=-1, keepdims=True)
    rstd = lax.rsqrt(jnp.mean(center * center, axis=-1, keepdims=True) + EPS)
    return center * rstd, rstd


def norm_back(x, gain, dy):
    xhat, rstd = stats(x)
    dxh = dy * gain
    dx = rstd * (
        dxh
        - jnp.mean(dxh, axis=-1, keepdims=True)
        - xhat * jnp.mean(dxh * xhat, axis=-1, keepdims=True)
    )
    dgain = jnp.sum(dy * xhat, axis=0, keepdims=True)
    dshift = jnp.sum(dy, axis=0, keepdims=True)
    return dx, dgain, dshift


def layer_kernel(
    nb,
    cells_h,
    cot_h,
    absent,
    ctx,
    vec,
    wfqkv_h,
    wfout_h,
    wrqkv_h,
    wrout_h,
    wfin_h,
    wfdn_h,
    act_h,
    igrad_h,
    grads_h,
    gvec,
    cells,
    cot,
    wfqkv,
    wfout,
    wrqkv,
    wrout,
    wfin,
    wfdn,
    wkvt,
    af,
    n1,
    fqkv,
    fp,
    fo,
    n2,
    rss,
    rsr,
    g2,
    hid,
    gin,
    n3,
    ro,
    gy2,
    accq,
    ctxa,
    act,
    dn2,
    load_sem,
    out_sem,
    ctx_send,
    ctx_recv,
    ag_send,
    ag_recv,
    fwd_send,
    rs_send,
    rs_recv,
):
    cols, rows, width = cells.shape
    seg = width
    ff_blocks = wfdn.shape[0] // seg
    t = lax.axis_index("tab")
    z = lax.axis_index("blk")

    loads = [
        pltpu.make_async_copy(src, dst, load_sem.at[i])
        for i, (src, dst) in enumerate(
            [
                (cells_h, cells),
                (wfqkv_h, wfqkv),
                (wfout_h, wfout),
                (wrqkv_h, wrqkv),
                (wrout_h, wrout),
                (wfin_h, wfin),
                (wfdn_h, wfdn),
                (cot_h, cot),
            ]
        )
    ]
    for load in loads:
        load.start()

    barrier = pltpu.get_barrier_semaphore()
    for d in range(1, nb):
        pl.semaphore_signal(
            barrier, inc=1, device_id=(t, lax.rem(z + d, nb)), device_id_type=MESH
        )
    pl.semaphore_wait(barrier, nb - 1)

    ctxa[z] = ctx[...]
    ctx_copies = [
        pltpu.make_async_remote_copy(
            src_ref=ctxa.at[z],
            dst_ref=ctxa.at[z],
            send_sem=ctx_send.at[d],
            recv_sem=ctx_recv.at[z],
            device_id=(t, lax.rem(z + d, nb)),
            device_id_type=MESH,
        )
        for d in range(1, nb)
    ]
    for copy in ctx_copies:
        copy.start()

    def own_send(c, d):
        return pltpu.make_async_remote_copy(
            src_ref=n2.at[c, z],
            dst_ref=n2.at[c, z],
            send_sem=ag_send.at[c, d + 2],
            recv_sem=ag_recv.at[c, z],
            device_id=(t, z + d),
            device_id_type=MESH,
        )

    def each_near(act_on):
        for d in (-1, 1, -2, 2):

            @pl.when(jnp.logical_and(z + d >= 0, z + d < nb))
            def _():
                act_on(d)

    def start_gather(c):
        each_near(lambda d: own_send(c, d).start())

    def forward(c, far):
        return pltpu.make_async_remote_copy(
            src_ref=n2.at[c, far],
            dst_ref=n2.at[c, far],
            send_sem=fwd_send.at[c],
            recv_sem=ag_recv.at[c, far],
            device_id=(t, nb - 1 - far),
            device_id_type=MESH,
        )

    def await_block(c, s):
        pltpu.make_async_copy(n2.at[c, s], n2.at[c, s], ag_recv.at[c, s]).wait()

    def at_middle(run):
        for mid in (1, nb - 2):

            @pl.when(z == mid)
            def _():
                run(nb - 1 if mid == 1 else 0)

    def start_forward(c):
        def go(far):
            await_block(c, far)
            forward(c, far).start()

        at_middle(go)

    def await_gather(c):
        for s in range(nb):
            skip = z == s
            if s == 0:
                skip = jnp.logical_or(skip, z == nb - 2)
            if s == nb - 1:
                skip = jnp.logical_or(skip, z == 1)

            @pl.when(jnp.logical_not(skip))
            def _():
                await_block(c, s)

    def row(i):
        return vec[i : i + 1, :]

    def base_of(c, r):
        return jnp.where(
            absent[c, pl.ds(r, CHUNK), :] > 0, row(EMBED), cells[c, pl.ds(r, CHUNK), :].astype(F32)
        )

    ones = (
        lax.broadcasted_iota(jnp.int32, (width, HEAD), 0) // HEAD
        == lax.broadcasted_iota(jnp.int32, (width, HEAD), 1)
    ).astype(BF16)
    ones_t = (
        lax.broadcasted_iota(jnp.int32, (HEAD, width), 1) // HEAD
        == lax.broadcasted_iota(jnp.int32, (HEAD, width), 0)
    ).astype(BF16)

    gvec[...] = jnp.zeros_like(gvec)
    loads[0].wait()
    for c in range(cols):
        for r in range(0, rows, CHUNK):
            xhat, _ = stats(base_of(c, r))
            n1[c, pl.ds(r, CHUNK), :] = (xhat * row(GAIN1) + row(SHIFT1)).astype(BF16)
    loads[1].wait()
    n1_all = n1[...].reshape(cols * rows, width)
    for b in range(3):
        fqkv[b] = (
            dot(n1_all, wfqkv[:, b * seg : (b + 1) * seg]).astype(BF16).reshape(cols, rows, width)
        )

    def feature_forward(hi, lo, spread):
        for i in range(cols):
            for j in range(cols):
                for r in range(0, rows, CHUNK):
                    prod = fqkv[0, i, pl.ds(r, CHUNK), :].astype(F32) * fqkv[
                        1, j, pl.ds(r, CHUNK), :
                    ].astype(F32)
                    top = prod.astype(BF16)
                    hi[pl.ds(j * rows + r, CHUNK), :] = top
                    lo[pl.ds(j * rows + r, CHUNK), :] = (prod - top.astype(F32)).astype(BF16)
            scores = (dot(hi[...], ones) + dot(lo[...], ones)) * SCALE
            parts = [scores[j * rows : (j + 1) * rows] for j in range(cols)]
            top = functools.reduce(jnp.maximum, parts)
            parts = [jnp.exp(part - top) for part in parts]
            inv = 1.0 / functools.reduce(jnp.add, parts)
            for j in range(cols):
                fp[i, j] = parts[j] * inv
            spread[...] = dot(
                fp[i].reshape(cols * rows, HEAD).astype(BF16), ones_t
            )
            for r in range(0, rows, CHUNK):
                total = functools.reduce(
                    jnp.add,
                    [
                        spread[pl.ds(j * rows + r, CHUNK), :]
                        * fqkv[2, j, pl.ds(r, CHUNK), :].astype(F32)
                        for j in range(cols)
                    ],
                )
                fo[i, pl.ds(r, CHUNK), :] = total.astype(BF16)
            if i == 0:
                loads[2].wait()
            spread[0:rows, :] = dot(fo[i], wfout[...])
            for r in range(0, rows, CHUNK):
                after = base_of(i, r) + spread[pl.ds(r, CHUNK), :]
                af[i, pl.ds(r, CHUNK), :] = after
                xhat, _ = stats(after)
                n2[i, z, pl.ds(r, CHUNK), :] = (xhat * row(GAIN2) + row(SHIFT2)).astype(BF16)
            if i == 0:
                start_gather(0)

    pl.run_scoped(
        feature_forward,
        pltpu.VMEM((cols * rows, width), BF16),
        pltpu.VMEM((cols * rows, width), BF16),
        pltpu.VMEM((cols * rows, width), F32),
    )

    loads[3].wait()
    for b in range(2):
        wkvt[b] = (
            wrqkv[:, (b + 1) * seg : (b + 2) * seg].astype(F32).T.astype(BF16)
        )
    for load in loads[4:]:
        load.wait()
    for s in range(nb):

        @pl.when(z != s)
        def _():
            pltpu.make_async_copy(ctxa.at[s], ctxa.at[s], ctx_recv.at[s]).wait()

    accq[...] = jnp.zeros_like(accq)

    def rs_copy(c, owner, dest, slot, k):
        return pltpu.make_async_remote_copy(
            src_ref=rss.at[c, owner],
            dst_ref=rsr.at[c, slot],
            send_sem=rs_send.at[c, k],
            recv_sem=rs_recv.at[c, slot],
            device_id=(t, dest),
            device_id_type=MESH,
        )

    def rs_plan(me):
        plan = []
        for owner in range(nb):
            distance = abs(owner - me)
            if distance == 0 or (distance == 2 and 0 < me < nb - 1 and owner in (0, nb - 1)):
                continue
            if distance == 3:
                dest = 1 if me == 0 else nb - 2
                plan.insert(0, (owner, dest, dest))
            else:
                plan.append((owner, owner, me))
        return plan

    def start_scatter(c):
        for me in range(nb):

            @pl.when(z == me)
            def _():
                for k, (owner, dest, slot) in enumerate(rs_plan(me)):
                    rs_copy(c, owner, dest, slot, k).start()

    def await_slot(c, s):
        pltpu.make_async_copy(rsr.at[c, s], rsr.at[c, s], rs_recv.at[c, s]).wait()

    def combine(c):
        for me in (1, nb - 2):

            @pl.when(z == me)
            def _():
                owner = nb - 1 if me == 1 else 0
                await_slot(c, me)
                rss[c, owner] = (
                    rss[c, owner].astype(F32) + rsr[c, me].astype(F32)
                ).astype(BF16)
                rs_copy(c, owner, owner, me, 3).start()

    def columns_stage(bias, q, kv, kvt, dkv, p, ot, dgel, ar, dq):
        for s in range(nb):
            b = (ctxa[s].astype(F32) - 1.0) * 1e30
            for lane in range(0, rows, HEAD):
                bias[pl.ds(s * rows, rows), lane : lane + HEAD] = b

        def column(c, _):
            start_forward(c)

            @pl.when(c + 1 < cols)
            def _():
                start_gather(c + 1)

            await_gather(c)
            x = n2[c].reshape(nb * rows, width)
            own = n2[c, z]
            q[...] = dot(own, wrqkv[:, 0:seg]).astype(BF16)
            kv[0] = dot(x, wrqkv[:, seg : 2 * seg]).astype(BF16)
            kvt[1] = dot_rt(wkvt[1], x).astype(BF16)
            for h in range(HEADS):
                hs = slice(h * HEAD, (h + 1) * HEAD)
                s = dot_rt(kv[0, :, hs], q[:, hs]) + bias[...]
                top = jnp.max(s, axis=0, keepdims=True)
                e = jnp.exp((s - top) * SCALE)
                p[h] = (e * (1.0 / jnp.sum(e, axis=0, keepdims=True))).astype(BF16)
                ot[hs, :] = dot(kvt[1, hs, :], p[h])
            ro[c] = ot[...].T.astype(BF16)
            kv[1] = dot(x, wrqkv[:, 2 * seg : 3 * seg]).astype(BF16)
            kvt[0] = dot_rt(wkvt[0], x).astype(BF16)

            ar[...] = dot(ro[c], wrout[...])
            for r in range(0, rows, CHUNK):
                rr = pl.ds(r, CHUNK)
                after = af[c, rr, :] + ar[rr, :]
                ar[rr, :] = after
                xhat, _ = stats(after)
                n3[c, rr, :] = (xhat * row(GAIN3) + row(SHIFT3)).astype(BF16)
            for f in range(ff_blocks):
                fs = slice(f * seg, (f + 1) * seg)
                dgel[f] = dot(n3[c], wfin[:, fs])
                for r in range(0, rows, CHUNK):
                    rr = pl.ds(r, CHUNK)
                    u = dgel[f, rr, :] + row(IN_BIAS + f)
                    c0 = math.sqrt(2.0 / math.pi)
                    sq = u * u
                    th = jnp.tanh(u * (c0 + (c0 * 0.044715) * sq))
                    half = 0.5 * (1.0 + th)
                    hid[c, rr, fs] = (u * half).astype(BF16)
                    dgel[f, rr, :] = half + 0.5 * u * (1.0 - th * th) * (
                        c0 + (3.0 * c0 * 0.044715) * sq
                    )
            act[c] = (ar[...] + dot(hid[c], wfdn[...]) + row(OUT_BIAS)).astype(BF16)
            pltpu.make_async_copy(act.at[c], act_h.at[c], out_sem.at[c]).start()
            for f in range(ff_blocks):
                fs = slice(f * seg, (f + 1) * seg)
                gi = (dot_rt(cot[c], wfdn[fs, :]) * dgel[f]).astype(BF16)
                gin[c, :, fs] = gi
                gvec[IN_BIAS + f : IN_BIAS + f + 1, :] += jnp.sum(
                    gi.astype(F32), axis=0, keepdims=True
                )
            dgel[0] = dot_rt(gin[c], wfin[...])
            for r in range(0, rows, CHUNK):
                rr = pl.ds(r, CHUNK)
                dx, dgain, dshift = norm_back(ar[rr, :], row(GAIN3), dgel[0, rr, :])
                g3 = cot[c, rr, :].astype(F32)
                g = g3 + dx
                g2[c, rr, :] = g
                gy2[c, rr, :] = g.astype(BF16)
                gvec[GAIN3 : GAIN3 + 1, :] += dgain
                gvec[SHIFT3 : SHIFT3 + 1, :] += dshift
                gvec[OUT_BIAS : OUT_BIAS + 1, :] += jnp.sum(g3, axis=0, keepdims=True)
            ar[...] = dot_rt(gy2[c], wrout[...])
            gro = ar[...].astype(BF16)
            for h in range(HEADS):
                hs = slice(h * HEAD, (h + 1) * HEAD)
                dp = dot_rt(kv[1, :, hs], gro[:, hs])
                pr = p[h].astype(F32)
                ds = (pr * (dp - jnp.sum(pr * dp, axis=0, keepdims=True))).astype(BF16)
                dkv[0, :, hs] = (dot(ds, q[:, hs]) * SCALE).astype(BF16)
                dkv[1, :, hs] = dot(p[h], gro[:, hs]).astype(BF16)
                ot[hs, :] = dot(kvt[0, hs, :], ds)
            dq[...] = (ot[...].T * SCALE).astype(BF16)
            for o in range(nb):
                os = slice(o * rows, (o + 1) * rows)
                rss[c, o] = (
                    dot_rt(dkv[0, os, :], wrqkv[:, seg : 2 * seg])
                    + dot_rt(dkv[1, os, :], wrqkv[:, 2 * seg : 3 * seg])
                ).astype(BF16)
            start_scatter(c)

            @pl.when(c > 0)
            def _():
                combine(c - 1)

            af_part = dot_rt(dq[...], wrqkv[:, 0:seg])
            dn2[c] = af_part
            accq[0] += dot_lt(own, dq[...])
            accq[1] += dot_lt(x, dkv[0])
            accq[2] += dot_lt(x, dkv[1])
            return 0

        lax.fori_loop(0, cols, column, 0)

    pl.run_scoped(
        columns_stage,
        pltpu.VMEM((nb * rows, rows), F32),
        pltpu.VMEM((rows, width), BF16),
        pltpu.VMEM((2, nb * rows, width), BF16),
        pltpu.VMEM((2, width, nb * rows), BF16),
        pltpu.VMEM((2, nb * rows, width), BF16),
        pltpu.VMEM((HEADS, nb * rows, rows), BF16),
        pltpu.VMEM((width, rows), F32),
        pltpu.VMEM((ff_blocks, rows, width), F32),
        pltpu.VMEM((rows, width), F32),
        pltpu.VMEM((rows, width), BF16),
    )

    def weights_stage(gb):
        def flat(ref):
            return ref[...].reshape(cols * rows, ref.shape[-1])

        for f in range(ff_blocks):
            fs = slice(f * seg, (f + 1) * seg)
            gb[B_FF_OUT + f] = dot_lt(hid[:, :, fs].reshape(cols * rows, seg), flat(cot)).astype(BF16)
            gb[B_FF_IN + f] = dot_lt(flat(n3), gin[:, :, fs].reshape(cols * rows, seg)).astype(BF16)
        gb[B_ROW_OUT] = dot_lt(flat(ro), flat(gy2)).astype(BF16)
        for b in range(3):
            gb[B_ROW_QKV + b] = accq[b].astype(BF16)

    def weigh(spread, source, part, dest, dest_part, i, scale):
        for r in range(0, rows, CHUNK):
            rr = pl.ds(r, CHUNK)
            total = functools.reduce(
                jnp.add,
                [
                    spread[pl.ds(j * rows + r, CHUNK), :]
                    * (source[j, rr, :] if part is None else source[part, j, rr, :]).astype(F32)
                    for j in range(cols)
                ],
            )
            dest[dest_part, i, rr, :] = (total * scale).astype(BF16)

    def feature_backward(gb, hi, lo, spread, gfo, dqkv, dsl):
        for c in range(cols):
            for s in range(nb):
                skip = z == s
                if s in (0, nb - 1):
                    skip = jnp.logical_or(skip, z == nb - 1 - s)

                @pl.when(jnp.logical_not(skip))
                def _():
                    await_slot(c, s)
                    dn2[c] += rsr[c, s].astype(F32)

            for r in range(0, rows, CHUNK):
                rr = pl.ds(r, CHUNK)
                dy = dn2[c, rr, :] + rss[c, z, rr, :].astype(F32)
                dx, dgain, dshift = norm_back(af[c, rr, :], row(GAIN2), dy)
                g = g2[c, rr, :] + dx
                g2[c, rr, :] = g
                gy2[c, rr, :] = g.astype(BF16)
                gvec[GAIN2 : GAIN2 + 1, :] += dgain
                gvec[SHIFT2 : SHIFT2 + 1, :] += dshift
        gy1 = gy2[...].reshape(cols * rows, width)
        gfo[...] = dot_rt(gy1, wfout[...]).astype(BF16).reshape(cols, rows, width)
        gb[B_FEAT_OUT] = dot_lt(fo[...].reshape(cols * rows, width), gy1).astype(BF16)
        for i in range(cols):
            for j in range(cols):
                for r in range(0, rows, CHUNK):
                    prod = gfo[i, pl.ds(r, CHUNK), :].astype(F32) * fqkv[
                        2, j, pl.ds(r, CHUNK), :
                    ].astype(F32)
                    top = prod.astype(BF16)
                    hi[pl.ds(j * rows + r, CHUNK), :] = top
                    lo[pl.ds(j * rows + r, CHUNK), :] = (prod - top.astype(F32)).astype(BF16)
            dp = dot(hi[...], ones) + dot(lo[...], ones)
            parts = [dp[j * rows : (j + 1) * rows] for j in range(cols)]
            mean = functools.reduce(jnp.add, [fp[i, j] * parts[j] for j in range(cols)])
            for j in range(cols):
                dsl[i, j] = (fp[i, j] * (parts[j] - mean)).astype(BF16)
        for i in range(cols):
            spread[...] = dot(dsl[i].reshape(cols * rows, HEAD), ones_t)
            weigh(spread, fqkv, 1, dqkv, 0, i, SCALE)
            spread[...] = dot(jnp.concatenate([dsl[j, i] for j in range(cols)], axis=0), ones_t)
            weigh(spread, fqkv, 0, dqkv, 1, i, SCALE)
            spread[...] = dot(
                jnp.concatenate([fp[j, i].astype(BF16) for j in range(cols)], axis=0), ones_t
            )
            weigh(spread, gfo, None, dqkv, 2, i, 1.0)
        n1_flat = n1[...].reshape(cols * rows, width)
        for b in range(3):
            gb[B_FEAT_QKV + b] = dot_lt(
                n1_flat, dqkv[b].reshape(cols * rows, width)
            ).astype(BF16)
        spread[...] = functools.reduce(
            jnp.add,
            [
                dot_rt(
                    dqkv[b].reshape(cols * rows, width), wfqkv[:, b * seg : (b + 1) * seg]
                )
                for b in range(3)
            ],
        )
        for c in range(cols):
            for r in range(0, rows, CHUNK):
                rr = pl.ds(r, CHUNK)
                dx, dgain, dshift = norm_back(
                    base_of(c, r), row(GAIN1), spread[pl.ds(c * rows + r, CHUNK), :]
                )
                g = g2[c, rr, :] + dx
                gone = absent[c, rr, :] > 0
                g2[c, rr, :] = jnp.where(gone, 0.0, g)
                gvec[GAIN1 : GAIN1 + 1, :] += dgain
                gvec[SHIFT1 : SHIFT1 + 1, :] += dshift
                gvec[EMBED : EMBED + 1, :] += jnp.sum(
                    jnp.where(gone, g, 0.0), axis=0, keepdims=True
                )

    def tail_stage(gb):
        weights_stage(gb)
        combine(cols - 1)
        pl.run_scoped(
            functools.partial(feature_backward, gb),
            pltpu.VMEM((cols * rows, width), BF16),
            pltpu.VMEM((cols * rows, width), BF16),
            pltpu.VMEM((cols * rows, width), F32),
            pltpu.VMEM((cols, rows, width), BF16),
            pltpu.VMEM((3, cols, rows, width), BF16),
            pltpu.VMEM((cols, cols, rows, HEAD), BF16),
        )
        grads_copy = pltpu.make_async_copy(gb, grads_h, out_sem.at[cols + 1])
        grads_copy.start()
        grads_copy.wait()

    pl.run_scoped(tail_stage, pltpu.VMEM((BLOCKS, width, width), BF16))

    igrad_copy = pltpu.make_async_copy(g2, igrad_h, out_sem.at[cols])
    igrad_copy.start()
    for c in range(cols):
        pltpu.make_async_copy(act.at[c], act_h.at[c], out_sem.at[c]).wait()
        each_near(lambda d: own_send(c, d).wait_send())
        at_middle(lambda far: forward(c, far).wait_send())
        for me in range(nb):

            @pl.when(z == me)
            def _():
                plan = rs_plan(me)
                for k, (owner, dest, slot) in enumerate(plan):
                    rs_copy(c, owner, dest, slot, k).wait_send()
                if 0 < me < nb - 1:
                    owner = nb - 1 if me == 1 else 0
                    rs_copy(c, owner, owner, me, 3).wait_send()

    for copy in ctx_copies:
        copy.wait_send()
    igrad_copy.wait()


def per_device(
    cells,
    missing,
    context,
    cotangent,
    miss_embed,
    norm1_gain,
    norm1_shift,
    feat_qkv,
    feat_out,
    norm2_gain,
    norm2_shift,
    row_qkv,
    row_out,
    norm3_gain,
    norm3_shift,
    ff_in,
    ff_in_bias,
    ff_out,
    ff_out_bias,
):
    _, rows, cols, width = cells.shape
    nb = lax.axis_size("blk")
    ff = ff_in.shape[1]
    ff_blocks = ff // width

    cells_t = jnp.transpose(cells[0], (1, 0, 2))
    cot_t = jnp.transpose(cotangent[0], (1, 0, 2))
    absent = jnp.transpose(missing[0], (1, 0))[:, :, None].astype(F32)
    ctx = jnp.broadcast_to(context[0][:, None].astype(BF16), (rows, HEAD))
    vec = jnp.concatenate(
        [
            jnp.stack(
                [
                    miss_embed,
                    norm1_gain,
                    norm1_shift,
                    norm2_gain,
                    norm2_shift,
                    norm3_gain,
                    norm3_shift,
                    ff_out_bias,
                ]
            ),
            ff_in_bias.reshape(ff_blocks, width),
            jnp.zeros((8 - ff_blocks, width), BF16),
        ]
    ).astype(F32)

    any_spec = pl.BlockSpec(memory_space=pl.ANY)
    vmem_spec = pl.BlockSpec(memory_space=pltpu.VMEM)
    token = (cols, rows, width)
    vm = pltpu.VMEM
    act, igrad, grads, gvec = pl.pallas_call(
        functools.partial(layer_kernel, nb),
        out_shape=(
            jax.ShapeDtypeStruct(token, BF16),
            jax.ShapeDtypeStruct(token, F32),
            jax.ShapeDtypeStruct((BLOCKS, width, width), BF16),
            jax.ShapeDtypeStruct((16, width), F32),
        ),
        in_specs=[any_spec] * 2 + [vmem_spec] * 3 + [any_spec] * 6,
        out_specs=(any_spec, any_spec, any_spec, vmem_spec),
        scratch_shapes=[
            vm(token, BF16),
            vm(token, BF16),
            vm(feat_qkv.shape, BF16),
            vm(feat_out.shape, BF16),
            vm(row_qkv.shape, BF16),
            vm(row_out.shape, BF16),
            vm(ff_in.shape, BF16),
            vm(ff_out.shape, BF16),
            vm((2, width, width), BF16),
            vm(token, F32),
            vm(token, BF16),
            vm((3,) + token, BF16),
            vm((cols, cols, rows, HEAD), F32),
            vm(token, BF16),
            vm((cols, nb, rows, width), BF16),
            vm((cols, nb, rows, width), BF16),
            vm((cols, nb, rows, width), BF16),
            vm(token, F32),
            vm((cols, rows, ff), BF16),
            vm((cols, rows, ff), BF16),
            vm(token, BF16),
            vm(token, BF16),
            vm(token, BF16),
            vm((3, width, width), F32),
            vm((nb, rows, HEAD), BF16),
            vm(token, BF16),
            vm(token, F32),
            pltpu.SemaphoreType.DMA((8,)),
            pltpu.SemaphoreType.DMA((cols + 2,)),
            pltpu.SemaphoreType.DMA((nb,)),
            pltpu.SemaphoreType.DMA((nb,)),
            pltpu.SemaphoreType.DMA((cols, 5)),
            pltpu.SemaphoreType.DMA((cols, nb)),
            pltpu.SemaphoreType.DMA((cols,)),
            pltpu.SemaphoreType.DMA((cols, nb)),
            pltpu.SemaphoreType.DMA((cols, nb)),
        ],
        compiler_params=pltpu.CompilerParams(
            collective_id=0, has_side_effects=True, vmem_limit_bytes=64 * 1024 * 1024
        ),
    )(
        cells_t,
        cot_t,
        absent,
        ctx,
        vec,
        feat_qkv,
        feat_out,
        row_qkv,
        row_out,
        ff_in,
        ff_out,
    )
    grads, gvec = lax.psum((grads.astype(F32), gvec), ("tab", "blk"))

    def side(first, count):
        return jnp.concatenate([grads[first + b] for b in range(count)], axis=1)

    return (
        jnp.transpose(act, (1, 0, 2))[None],
        jnp.transpose(igrad, (1, 0, 2))[None],
        gvec[EMBED],
        gvec[GAIN1],
        gvec[SHIFT1],
        side(B_FEAT_QKV, 3),
        grads[B_FEAT_OUT],
        gvec[GAIN2],
        gvec[SHIFT2],
        side(B_ROW_QKV, 3),
        grads[B_ROW_OUT],
        gvec[GAIN3],
        gvec[SHIFT3],
        side(B_FF_IN, ff_blocks),
        gvec[IN_BIAS : IN_BIAS + ff_blocks].reshape(ff),
        grads[B_FF_OUT : B_FF_OUT + ff_blocks].reshape(ff, width),
        gvec[OUT_BIAS],
    )


def solution(mesh):
    split = (
        P("tab", "blk", None, None),
        P("tab", "blk", None),
        P("tab", "blk"),
        P("tab", "blk", None, None),
    )
    return jax.shard_map(
        per_device,
        mesh=mesh,
        in_specs=split + (P(),) * 15,
        out_specs=(P("tab", "blk", None, None),) * 2 + (P(),) * 15,
        check_vma=False,
    )
```

```python
import functools
import math

import jax
import jax.numpy as jnp
from jax import lax
from jax.experimental import pallas as pl
from jax.experimental.pallas import tpu as pltpu
from jax.sharding import PartitionSpec as P

HEADS = 4
HEAD = 128
EPS = 1e-05
SCALE = 1.0 / math.sqrt(HEAD)
MESH = pl.DeviceIdType.MESH
F32 = jnp.float32
BF16 = jnp.bfloat16
EMBED, GAIN1, SHIFT1, GAIN2, SHIFT2, GAIN3, SHIFT3, OUT_BIAS, IN_BIAS = range(9)
CHUNK = 64
HALF = 256
STAGES = 8


def dot(a, b):
    return jnp.dot(a, b, preferred_element_type=F32)


def dot_rt(a, b):
    return lax.dot_general(a, b, (((1,), (1,)), ((), ())), preferred_element_type=F32)


def dot_lt(a, b):
    return lax.dot_general(a, b, (((0,), (0,)), ((), ())), preferred_element_type=F32)


def stats(x):
    center = x - jnp.mean(x, axis=-1, keepdims=True)
    rstd = lax.rsqrt(jnp.mean(center * center, axis=-1, keepdims=True) + EPS)
    return center * rstd, rstd


def norm_back(x, gain, dy):
    xhat, rstd = stats(x)
    dxh = dy * gain
    dx = rstd * (
        dxh
        - jnp.mean(dxh, axis=-1, keepdims=True)
        - xhat * jnp.mean(dxh * xhat, axis=-1, keepdims=True)
    )
    dgain = jnp.sum(dy * xhat, axis=0, keepdims=True)
    dshift = jnp.sum(dy, axis=0, keepdims=True)
    return dx, dgain, dshift


def layer_kernel(
    nb,
    fused,
    cells_h,
    cot_h,
    missing,
    context,
    vec,
    wfqkv_h,
    wfout_h,
    wrqkv_h,
    wrout_h,
    wfin_h,
    wfdn_h,
    act_h,
    igrad_h,
    gfqkv_h,
    gfout_h,
    grqkv_h,
    grout_h,
    gfin_h,
    gfdn_h,
    gvec,
    n1_h,
    fqkv_h,
    fp_h,
    fo_h,
    cot,
    wrqkv,
    wrout,
    wfin,
    wfdn,
    wkvt,
    absent,
    af,
    n2,
    rss,
    rsr,
    g2,
    hid,
    gin,
    nro,
    gy2,
    accq,
    ctxa,
    act,
    dn2,
    gb,
    vland,
    load_sem,
    feat_sem,
    stash_sem,
    out_sem,
    ctx_send,
    ctx_recv,
    ag_send,
    ag_recv,
    fwd_send,
    rs_send,
    rs_recv,
    ar_send,
    ar_recv,
    vec_send,
    vec_recv,
    ready,
    free,
):
    cols, rows, width = g2.shape
    seg = width
    ff_blocks = wfin.shape[1] // seg
    quarter = rows // CHUNK
    ro_at = cols
    t = lax.axis_index("tab")
    z = lax.axis_index("blk")
    core, xbit, ybit = lax.rem(t, 2), lax.rem(lax.div(t, 2), 2), lax.rem(lax.div(t, 4), 2)
    on_core = (t + 1 - 2 * core, z)
    on_x = (t + 2 - 4 * xbit, z)
    on_y = (t + 4 - 8 * ybit, z)
    along = [(t, lax.rem(z + d, nb)) for d in range(1, nb)]
    partners = along + ([on_core, on_x, on_y] if fused else [])

    def load_all(pairs, sem):
        copies = [
            pltpu.make_async_copy(a, b, sem.at[i]) for i, (a, b) in enumerate(pairs)
        ]
        for copy in copies:
            copy.start()
        return copies

    def signal_all(sem):
        for device in partners:
            pl.semaphore_signal(sem, inc=1, device_id=device, device_id_type=MESH)

    def await_all(sem):
        pl.semaphore_wait(sem, len(partners))

    def remote(source, dest, send, recv, device):
        return pltpu.make_async_remote_copy(
            src_ref=source,
            dst_ref=dest,
            send_sem=send,
            recv_sem=recv,
            device_id=device,
            device_id_type=MESH,
        )

    def block(c, s):
        return n2.at[c * (nb // 2) + s // 2, pl.ds(pl.multiple_of((s % 2) * rows, rows), rows)]

    own_hi, own_lo = lax.div(z, 2), pl.multiple_of(lax.rem(z, 2) * rows, rows)

    def own_block(c):
        return n2.at[c * (nb // 2) + own_hi, pl.ds(own_lo, rows)]

    def own_send(c, d):
        return remote(
            own_block(c), own_block(c), ag_send.at[c, d + 2], ag_recv.at[c, z], (t, z + d)
        )

    def each_near(run):
        for d in (-1, 1, -2, 2):

            @pl.when(jnp.logical_and(z + d >= 0, z + d < nb))
            def _():
                run(d)

    def start_gather(c):
        each_near(lambda d: own_send(c, d).start())

    def forward(c, far):
        return remote(
            block(c, far), block(c, far), fwd_send.at[c], ag_recv.at[c, far], (t, nb - 1 - far)
        )

    def await_block(c, s):
        pltpu.make_async_copy(block(c, s), block(c, s), ag_recv.at[c, s]).wait()

    def at_middle(run):
        for mid in (1, nb - 2):

            @pl.when(z == mid)
            def _():
                run(nb - 1 if mid == 1 else 0)

    def start_forward(c):
        def go(far):
            await_block(c, far)
            forward(c, far).start()

        at_middle(go)

    def await_gather(c):
        for s in range(nb):
            skip = z == s
            if s == 0:
                skip = jnp.logical_or(skip, z == nb - 2)
            if s == nb - 1:
                skip = jnp.logical_or(skip, z == 1)

            @pl.when(jnp.logical_not(skip))
            def _():
                await_block(c, s)

    def rs_copy(c, owner, dest, slot, k):
        return remote(
            rss.at[c, owner], rsr.at[c, slot], rs_send.at[c, k], rs_recv.at[c, slot], (t, dest)
        )

    def rs_plan(me):
        plan = []
        for owner in range(nb):
            distance = abs(owner - me)
            if distance == 0 or (distance == 2 and 0 < me < nb - 1 and owner in (0, nb - 1)):
                continue
            if distance == 3:
                dest = 1 if me == 0 else nb - 2
                plan.insert(0, (owner, dest, dest))
            else:
                plan.append((owner, owner, me))
        return plan

    def start_scatter(c):
        for me in range(nb):

            @pl.when(z == me)
            def _():
                for k, (owner, dest, slot) in enumerate(rs_plan(me)):
                    rs_copy(c, owner, dest, slot, k).start()

    def await_slot(c, s):
        pltpu.make_async_copy(rsr.at[c, s], rsr.at[c, s], rs_recv.at[c, s]).wait()

    def combine(c):
        for me in (1, nb - 2):

            @pl.when(z == me)
            def _():
                owner = nb - 1 if me == 1 else 0
                await_slot(c, me)
                rss[c, owner] = (
                    rss[c, owner].astype(F32) + rsr[c, me].astype(F32)
                ).astype(BF16)
                rs_copy(c, owner, owner, me, 3).start()

    groups = [
        (gb, 0, 4, 0, (hid, 0)),
        (gb, 4, 5, 4, (hid, 4)),
        (gb, 9, 3, 9, (hid, 9)),
        (n2, 0, 4, 12, (nro, 0)),
    ]
    lanes_a, lanes_b = pl.ds(0, HALF), pl.ds(HALF, HALF)

    def at16(v):
        return pl.multiple_of(v, 16)

    row_core = core * 256
    paths = [(lanes_a, xbit, ybit, on_x, on_y), (lanes_b, ybit, xbit, on_y, on_x)]

    def landing(g, stage):
        _, _, n, place, (land, land_at) = groups[g]
        if stage == 0:
            return land, pl.ds(land_at, n)
        if stage == 1:
            return wfdn, pl.ds(place, n)
        return gin, pl.ds(place + (16 if stage == 3 else 0), n)

    def sum_copies(g, stage):
        ref, base, n, _, _ = groups[g]
        whole = pl.ds(0, width)

        def final(row, count, lanes):
            return ref.at[pl.ds(base, n), pl.ds(at16(row), count), lanes]

        out = []
        if stage < 4:
            land, at = landing(g, stage)
            if stage > 0:
                last, last_at = landing(g, stage - 1)
        if stage == 0:
            out.append((final((1 - core) * 256, 256, whole), land.at[at], on_core))
        elif stage == 1:
            for lanes, bit, _, device, _ in paths:
                away = last.at[last_at, pl.ds(at16((1 - bit) * 128), 128), lanes]
                out.append((away, land.at[at, :, lanes], device))
        elif stage == 2:
            for lanes, _, bit, _, device in paths:
                away = last.at[last_at, pl.ds(at16((1 - bit) * 64), 64), lanes]
                out.append((away, land.at[at, :, lanes], device))
        elif stage == 3:
            for d in range(1, nb):
                away = last.at[last_at, pl.ds(at16(lax.rem(z + d, nb) * 16), 16), :]
                out.append((away, land.at[at, pl.ds((d - 1) * 16, 16), :], along[d - 1]))
        elif stage == 4:
            last, last_at = landing(g, 3)
            for d in range(1, nb):
                for lanes, bit1, bit2, _, _ in paths:
                    row = row_core + bit1 * 128 + bit2 * 64 + z * 16
                    mine = last.at[last_at, pl.ds(0, 16), lanes]
                    out.append((mine, final(row, 16, lanes), along[d - 1]))
        elif stage == 5:
            for lanes, bit1, bit2, _, device in paths:
                mine = final(row_core + bit1 * 128 + bit2 * 64, 64, lanes)
                out.append((mine, mine, device))
        elif stage == 6:
            for lanes, bit1, _, device, _ in paths:
                mine = final(row_core + bit1 * 128, 128, lanes)
                out.append((mine, mine, device))
        else:
            mine = final(row_core, 256, whole)
            out.append((mine, mine, on_core))
        first = (0, 1, 3, 5, 8, 14, 16, 18)[stage]
        return [
            remote(a, b, ar_send.at[g, first + i], ar_recv.at[g, first + i], device)
            for i, (a, b, device) in enumerate(out)
        ]

    def start_sum(g, stage=0):
        if fused:
            if stage == STAGES - 1:
                pl.semaphore_wait(free.at[g], 1)
            for copy in sum_copies(g, stage):
                copy.start()

    def add_landed(g, stage):
        ref, base, n, _, _ = groups[g]
        blocks = pl.ds(base, n)
        land, at = landing(g, stage)
        if stage == 0:
            mine = ref[blocks, pl.ds(at16(row_core), 256), :]
            land[at] = (mine.astype(F32) + land[at].astype(F32)).astype(BF16)
            return
        last, last_at = landing(g, stage - 1)
        if stage == 3:
            total = last[last_at, pl.ds(at16(z * 16), 16), :].astype(F32)
            for d in range(1, nb):
                total = total + land[at, pl.ds((d - 1) * 16, 16), :].astype(F32)
            total = total.astype(BF16)
            land[at, pl.ds(0, 16), :] = total
            for i, (lanes, bit1, bit2, _, _) in enumerate(paths):
                row = at16(row_core + bit1 * 128 + bit2 * 64 + z * 16)
                ref[blocks, pl.ds(row, 16), lanes] = total[:, :, i * HALF : (i + 1) * HALF]
            return
        count = 128 if stage == 1 else 64
        for lanes, bit1, bit2, _, _ in paths:
            row = at16((bit1 if stage == 1 else bit2) * count)
            mine = last[last_at, pl.ds(row, count), lanes]
            land[at, :, lanes] = (
                mine.astype(F32) + land[at, :, lanes].astype(F32)
            ).astype(BF16)

    def next_sum(g, stage):
        if not fused:
            return
        for copy in sum_copies(g, stage):
            copy.wait_recv()
        if stage < 4:
            add_landed(g, stage)
        if stage == 0:
            for copy in sum_copies(g, stage):
                copy.wait_send()
            pl.semaphore_signal(free.at[g], inc=1, device_id=on_core, device_id_type=MESH)
        if stage + 1 < STAGES:
            start_sum(g, stage + 1)

    def out_copies(g):
        if g == 0:
            pairs = [
                (gb.at[f], gfdn_h.at[pl.ds(f * seg, seg)]) for f in range(ff_blocks)
            ]
            first = 0
        elif g == 1:
            pairs = [
                (gb.at[4 + f], gfin_h.at[:, pl.ds(f * seg, seg)]) for f in range(ff_blocks)
            ] + [(gb.at[8], grout_h)]
            first = 4
        elif g == 2:
            pairs = [(gb.at[9 + b], grqkv_h.at[:, pl.ds(b * seg, seg)]) for b in range(3)]
            first = 9
        else:
            pairs = [(n2.at[0], gfout_h)] + [
                (n2.at[1 + b], gfqkv_h.at[:, pl.ds(b * seg, seg)]) for b in range(3)
            ]
            first = 12
        return [
            pltpu.make_async_copy(a, b, out_sem.at[first + i]) for i, (a, b) in enumerate(pairs)
        ]

    def start_out(g):
        for copy in out_copies(g):
            copy.start()

    barrier = pltpu.get_barrier_semaphore()
    signal_all(barrier)
    loads = load_all(
        [(wrqkv_h, wrqkv), (wrout_h, wrout), (wfin_h, wfin), (wfdn_h, wfdn), (cot_h, cot)],
        load_sem,
    )
    marks = jnp.concatenate(
        [missing[...].astype(F32), jnp.zeros((8 - cols, rows), F32)], axis=0
    ).T
    for c in range(cols):
        absent[c] = marks[:, c : c + 1]
    ctxa[z] = jnp.broadcast_to(context[...].astype(F32), (HEAD, rows)).T.astype(BF16)
    gvec[...] = jnp.zeros_like(gvec)

    def row(i):
        return vec[i : i + 1, :]

    ones = (
        lax.broadcasted_iota(jnp.int32, (width, HEAD), 0) // HEAD
        == lax.broadcasted_iota(jnp.int32, (width, HEAD), 1)
    ).astype(BF16)
    ones_t = (
        lax.broadcasted_iota(jnp.int32, (HEAD, width), 1) // HEAD
        == lax.broadcasted_iota(jnp.int32, (HEAD, width), 0)
    ).astype(BF16)

    def base_of(cells, c, r):
        return jnp.where(
            absent[c, pl.ds(r, CHUNK), :] > 0, row(EMBED), cells[c, pl.ds(r, CHUNK), :].astype(F32)
        )

    ctx_copies = [
        remote(ctxa.at[z], ctxa.at[z], ctx_send.at[d], ctx_recv.at[z], along[d])
        for d in range(nb - 1)
    ]

    def feature_forward(cells, wfqkv, wfout, n1, fqkv, fp, fo, hi, lo, spread):
        feat_loads = load_all(
            [(cells_h, cells), (wfqkv_h, wfqkv), (wfout_h, wfout)], feat_sem
        )
        feat_loads[0].wait()
        for c in range(cols):
            for r in range(0, rows, CHUNK):
                xhat, _ = stats(base_of(cells, c, r))
                n1[c, pl.ds(r, CHUNK), :] = (xhat * row(GAIN1) + row(SHIFT1)).astype(BF16)
        await_all(barrier)
        for copy in ctx_copies:
            copy.start()
        feat_loads[1].wait()
        n1_all = n1[...].reshape(cols * rows, width)
        for b in range(3):
            fqkv[b] = (
                dot(n1_all, wfqkv[:, b * seg : (b + 1) * seg])
                .astype(BF16)
                .reshape(cols, rows, width)
            )
        stash = [(n1, n1_h), (fqkv, fqkv_h)]
        for i in range(cols):
            for j in range(cols):
                for r in range(0, rows, CHUNK):
                    prod = fqkv[0, i, pl.ds(r, CHUNK), :].astype(F32) * fqkv[
                        1, j, pl.ds(r, CHUNK), :
                    ].astype(F32)
                    top = prod.astype(BF16)
                    hi[pl.ds(j * rows + r, CHUNK), :] = top
                    lo[pl.ds(j * rows + r, CHUNK), :] = (prod - top.astype(F32)).astype(BF16)
            scores = (dot(hi[...], ones) + dot(lo[...], ones)) * SCALE
            parts = [scores[j * rows : (j + 1) * rows] for j in range(cols)]
            top = functools.reduce(jnp.maximum, parts)
            parts = [jnp.exp(part - top) for part in parts]
            inv = 1.0 / functools.reduce(jnp.add, parts)
            for j in range(cols):
                fp[i, j] = parts[j] * inv
            spread[...] = dot(fp[i].reshape(cols * rows, HEAD).astype(BF16), ones_t)
            weigh(spread, fqkv, 2, fo, None, i, 1.0)
            if i == 0:
                feat_loads[2].wait()
            spread[0:rows, :] = dot(fo[i], wfout[...])
            for r in range(0, rows, CHUNK):
                after = base_of(cells, i, r) + spread[pl.ds(r, CHUNK), :]
                af[i, pl.ds(r, CHUNK), :] = after
                xhat, _ = stats(after)
                n2[i * (nb // 2) + own_hi, pl.ds(pl.multiple_of(own_lo + r, CHUNK), CHUNK), :] = (
                    xhat * row(GAIN2) + row(SHIFT2)
                ).astype(BF16)
            if i == 0:
                start_gather(0)
        for copy in load_all(stash + [(fp, fp_h), (fo, fo_h)], stash_sem):
            copy.wait()

    def weigh(spread, source, part, dest, dest_part, i, scale):
        for r in range(0, rows, CHUNK):
            rr = pl.ds(r, CHUNK)
            total = functools.reduce(
                jnp.add,
                [
                    spread[pl.ds(j * rows + r, CHUNK), :]
                    * (source[j, rr, :] if part is None else source[part, j, rr, :]).astype(F32)
                    for j in range(cols)
                ],
            )
            total = (total * scale).astype(BF16)
            if dest_part is None:
                dest[i, rr, :] = total
            else:
                dest[dest_part, i, rr, :] = total

    token = (cols, rows, width)
    vm = pltpu.VMEM
    feature_scratch = [
        vm(token, BF16),
        vm(wfqkv_h.shape, BF16),
        vm(wfout_h.shape, BF16),
        vm(token, BF16),
        vm((3,) + token, BF16),
        vm((cols, cols, rows, HEAD), F32),
        vm(token, BF16),
        vm((cols * rows, width), BF16),
        vm((cols * rows, width), BF16),
        vm((cols * rows, width), F32),
    ]
    pl.run_scoped(feature_forward, *feature_scratch)

    loads[0].wait()
    for b in range(2):
        wkvt[b] = wrqkv[:, (b + 1) * seg : (b + 2) * seg].astype(F32).T.astype(BF16)
    for load in loads[1:]:
        load.wait()
    for s in range(nb):

        @pl.when(z != s)
        def _():
            pltpu.make_async_copy(ctxa.at[s], ctxa.at[s], ctx_recv.at[s]).wait()

    accq[...] = jnp.zeros_like(accq)

    def ff_weight(f):
        return wfdn[pl.ds(f * (seg // 128), seg // 128)].reshape(seg, width)

    def gin_block(c, f):
        return pl.ds((c * ff_blocks + f) * quarter, quarter)

    def ff_weights():
        cot_all = cot[...].reshape(cols * rows, width)
        n3_all = nro[0:cols].reshape(cols * rows, width)
        for f in range(ff_blocks):
            hid_all = jnp.concatenate([hid[c * ff_blocks + f] for c in range(cols)], axis=0)
            gb[f] = dot_lt(hid_all, cot_all).astype(BF16)
            gin_all = jnp.concatenate(
                [gin[gin_block(c, f)].reshape(rows, seg) for c in range(cols)], axis=0
            )
            gb[ff_blocks + f] = dot_lt(n3_all, gin_all).astype(BF16)
        gb[2 * ff_blocks] = dot_lt(
            nro[ro_at : ro_at + cols].reshape(cols * rows, width),
            gy2[...].reshape(cols * rows, width),
        ).astype(BF16)
        if fused:
            signal_all(ready)
            await_all(ready)
        start_sum(0)
        start_sum(1)

    def columns_stage(bias, q, kv, kvt, dkv, p, ot, dgel, ar, dq):
        for s in range(nb):
            b = (ctxa[s].astype(F32) - 1.0) * 1e30
            for lane in range(0, rows, HEAD):
                bias[pl.ds(s * rows, rows), lane : lane + HEAD] = b

        def column(c, _):
            start_forward(c)

            @pl.when(c + 1 < cols)
            def _():
                start_gather(c + 1)

            await_gather(c)
            x = n2[pl.ds(c * (nb // 2), nb // 2)].reshape(nb * rows, width)
            own = n2[c * (nb // 2) + own_hi, pl.ds(own_lo, rows), :]
            q[...] = dot(own, wrqkv[:, 0:seg]).astype(BF16)
            kv[0] = dot(x, wrqkv[:, seg : 2 * seg]).astype(BF16)
            kvt[1] = dot_rt(wkvt[1], x).astype(BF16)
            for h in range(HEADS):
                hs = slice(h * HEAD, (h + 1) * HEAD)
                s = dot_rt(kv[0, :, hs], q[:, hs]) + bias[...]
                top = jnp.max(s, axis=0, keepdims=True)
                e = jnp.exp((s - top) * SCALE)
                p[h] = (e * (1.0 / jnp.sum(e, axis=0, keepdims=True))).astype(BF16)
                ot[hs, :] = dot(kvt[1, hs, :], p[h])
            nro[ro_at + c] = ot[...].T.astype(BF16)
            kv[1] = dot(x, wrqkv[:, 2 * seg : 3 * seg]).astype(BF16)
            kvt[0] = dot_rt(wkvt[0], x).astype(BF16)

            ar[...] = dot(nro[ro_at + c], wrout[...])
            for r in range(0, rows, CHUNK):
                rr = pl.ds(r, CHUNK)
                after = af[c, rr, :] + ar[rr, :]
                ar[rr, :] = after
                xhat, _ = stats(after)
                nro[c, rr, :] = (xhat * row(GAIN3) + row(SHIFT3)).astype(BF16)
            for f in range(ff_blocks):
                fs = slice(f * seg, (f + 1) * seg)
                dgel[f] = dot(nro[c], wfin[:, fs])
                for r in range(0, rows, CHUNK):
                    rr = pl.ds(r, CHUNK)
                    u = dgel[f, rr, :] + row(IN_BIAS + f)
                    c0 = math.sqrt(2.0 / math.pi)
                    sq = u * u
                    th = jnp.tanh(u * (c0 + (c0 * 0.044715) * sq))
                    half = 0.5 * (1.0 + th)
                    hid[c * ff_blocks + f, rr, :] = (u * half).astype(BF16)
                    dgel[f, rr, :] = half + 0.5 * u * (1.0 - th * th) * (
                        c0 + (3.0 * c0 * 0.044715) * sq
                    )
            total = ar[...] + row(OUT_BIAS)
            for f in range(ff_blocks):
                total = total + dot(hid[c * ff_blocks + f], ff_weight(f))
            act[c] = total.astype(BF16)
            pltpu.make_async_copy(act.at[c], act_h.at[c], stash_sem.at[c]).start()
            back = jnp.zeros((rows, width), F32)
            for f in range(ff_blocks):
                fs = slice(f * seg, (f + 1) * seg)
                gi = (dot_rt(cot[c], ff_weight(f)) * dgel[f]).astype(BF16)
                gin[gin_block(c, f)] = gi.reshape(quarter, CHUNK, seg)
                gvec[IN_BIAS + f : IN_BIAS + f + 1, :] += jnp.sum(
                    gi.astype(F32), axis=0, keepdims=True
                )
                back = back + dot_rt(gi, wfin[:, fs])
            dgel[0] = back
            for r in range(0, rows, CHUNK):
                rr = pl.ds(r, CHUNK)
                dx, dgain, dshift = norm_back(ar[rr, :], row(GAIN3), dgel[0, rr, :])
                g3 = cot[c, rr, :].astype(F32)
                g = g3 + dx
                g2[c, rr, :] = g
                gy2[c, rr, :] = g.astype(BF16)
                gvec[GAIN3 : GAIN3 + 1, :] += dgain
                gvec[SHIFT3 : SHIFT3 + 1, :] += dshift
                gvec[OUT_BIAS : OUT_BIAS + 1, :] += jnp.sum(g3, axis=0, keepdims=True)

            ar[...] = dot_rt(gy2[c], wrout[...])

            @pl.when(c == cols - 1)
            def _():
                ff_weights()

            gro = ar[...].astype(BF16)
            for h in range(HEADS):
                hs = slice(h * HEAD, (h + 1) * HEAD)
                dp = dot_rt(kv[1, :, hs], gro[:, hs])
                pr = p[h].astype(F32)
                ds = (pr * (dp - jnp.sum(pr * dp, axis=0, keepdims=True))).astype(BF16)
                dkv[0, :, hs] = (dot(ds, q[:, hs]) * SCALE).astype(BF16)
                dkv[1, :, hs] = dot(p[h], gro[:, hs]).astype(BF16)
                ot[hs, :] = dot(kvt[0, hs, :], ds)
            dq[...] = (ot[...].T * SCALE).astype(BF16)
            for o in range(nb):
                os = slice(o * rows, (o + 1) * rows)
                rss[c, o] = (
                    dot_rt(dkv[0, os, :], wrqkv[:, seg : 2 * seg])
                    + dot_rt(dkv[1, os, :], wrqkv[:, 2 * seg : 3 * seg])
                ).astype(BF16)
            start_scatter(c)

            @pl.when(c > 0)
            def _():
                combine(c - 1)

            @pl.when(c == cols - 1)
            def _():
                next_sum(0, 0)
                next_sum(1, 0)

            dn2[c] = dot_rt(dq[...], wrqkv[:, 0:seg])
            accq[0] += dot_lt(own, dq[...])
            accq[1] += dot_lt(x, dkv[0])
            accq[2] += dot_lt(x, dkv[1])
            return 0

        lax.fori_loop(0, cols, column, 0)

    pl.run_scoped(
        columns_stage,
        vm((nb * rows, rows), F32),
        vm((rows, width), BF16),
        vm((2, nb * rows, width), BF16),
        vm((2, width, nb * rows), BF16),
        vm((2, nb * rows, width), BF16),
        vm((HEADS, nb * rows, rows), BF16),
        vm((width, rows), F32),
        vm((ff_blocks, rows, width), F32),
        vm((rows, width), F32),
        vm((rows, width), BF16),
    )

    def feature_backward(cells, wfqkv, wfout, n1, fqkv, fp, fo, hi, lo, spread, gfo, dqkv, dsl):
        again = load_all(
            [
                (cells_h, cells),
                (wfqkv_h, wfqkv),
                (wfout_h, wfout),
                (n1_h, n1),
                (fqkv_h, fqkv),
                (fp_h, fp),
                (fo_h, fo),
            ],
            feat_sem,
        )
        for b in range(3):
            gb[9 + b] = accq[b].astype(BF16)
        start_sum(2)
        next_sum(0, 1)
        combine(cols - 1)
        for c in range(cols):
            each_near(lambda d: own_send(c, d).wait_send())
            at_middle(lambda far: forward(c, far).wait_send())
        next_sum(1, 1)
        next_sum(0, 2)
        next_sum(2, 0)
        for c in range(cols):
            for s in range(nb):
                skip = z == s
                if s in (0, nb - 1):
                    skip = jnp.logical_or(skip, z == nb - 1 - s)

                @pl.when(jnp.logical_not(skip))
                def _():
                    await_slot(c, s)
                    dn2[c] += rsr[c, s].astype(F32)

            for r in range(0, rows, CHUNK):
                rr = pl.ds(r, CHUNK)
                dy = dn2[c, rr, :] + rss[c, z, rr, :].astype(F32)
                dx, dgain, dshift = norm_back(af[c, rr, :], row(GAIN2), dy)
                g = g2[c, rr, :] + dx
                g2[c, rr, :] = g
                gy2[c, rr, :] = g.astype(BF16)
                gvec[GAIN2 : GAIN2 + 1, :] += dgain
                gvec[SHIFT2 : SHIFT2 + 1, :] += dshift
        for copy in again:
            copy.wait()
        next_sum(1, 2)
        next_sum(0, 3)
        gy1 = gy2[...].reshape(cols * rows, width)
        gfo[...] = dot_rt(gy1, wfout[...]).astype(BF16).reshape(cols, rows, width)
        n2[0] = dot_lt(fo[...].reshape(cols * rows, width), gy1).astype(BF16)
        next_sum(2, 1)
        for i in range(cols):
            for j in range(cols):
                for r in range(0, rows, CHUNK):
                    prod = gfo[i, pl.ds(r, CHUNK), :].astype(F32) * fqkv[
                        2, j, pl.ds(r, CHUNK), :
                    ].astype(F32)
                    top = prod.astype(BF16)
                    hi[pl.ds(j * rows + r, CHUNK), :] = top
                    lo[pl.ds(j * rows + r, CHUNK), :] = (prod - top.astype(F32)).astype(BF16)
            dp = dot(hi[...], ones) + dot(lo[...], ones)
            parts = [dp[j * rows : (j + 1) * rows] for j in range(cols)]
            mean = functools.reduce(jnp.add, [fp[i, j] * parts[j] for j in range(cols)])
            for j in range(cols):
                dsl[i, j] = (fp[i, j] * (parts[j] - mean)).astype(BF16)
        next_sum(1, 3)
        next_sum(0, 4)
        next_sum(2, 2)
        for i in range(cols):
            spread[...] = dot(dsl[i].reshape(cols * rows, HEAD), ones_t)
            weigh(spread, fqkv, 1, dqkv, 0, i, SCALE)
            spread[...] = dot(jnp.concatenate([dsl[j, i] for j in range(cols)], axis=0), ones_t)
            weigh(spread, fqkv, 0, dqkv, 1, i, SCALE)
            spread[...] = dot(
                jnp.concatenate([fp[j, i].astype(BF16) for j in range(cols)], axis=0), ones_t
            )
            weigh(spread, gfo, None, dqkv, 2, i, 1.0)
        n1_flat = n1[...].reshape(cols * rows, width)
        for b in range(3):
            n2[1 + b] = dot_lt(n1_flat, dqkv[b].reshape(cols * rows, width)).astype(BF16)
        start_sum(3)
        next_sum(0, 5)
        next_sum(1, 4)
        next_sum(2, 3)
        spread[...] = functools.reduce(
            jnp.add,
            [
                dot_rt(dqkv[b].reshape(cols * rows, width), wfqkv[:, b * seg : (b + 1) * seg])
                for b in range(3)
            ],
        )
        next_sum(3, 0)
        next_sum(1, 5)
        next_sum(0, 6)
        next_sum(2, 4)
        for c in range(cols):
            for r in range(0, rows, CHUNK):
                rr = pl.ds(r, CHUNK)
                dx, dgain, dshift = norm_back(
                    base_of(cells, c, r), row(GAIN1), spread[pl.ds(c * rows + r, CHUNK), :]
                )
                g = g2[c, rr, :] + dx
                gone = absent[c, rr, :] > 0
                g2[c, rr, :] = jnp.where(gone, 0.0, g)
                gvec[GAIN1 : GAIN1 + 1, :] += dgain
                gvec[SHIFT1 : SHIFT1 + 1, :] += dshift
                gvec[EMBED : EMBED + 1, :] += jnp.sum(
                    jnp.where(gone, g, 0.0), axis=0, keepdims=True
                )

    pl.run_scoped(
        feature_backward,
        *feature_scratch,
        vm(token, BF16),
        vm((3,) + token, BF16),
        vm((cols, cols, rows, HEAD), BF16),
    )
    igrad_copy = pltpu.make_async_copy(g2, igrad_h, stash_sem.at[cols])
    igrad_copy.start()

    vec_copies = []

    def vec_step(k, devices):
        copies = [
            remote(
                vland.at[k],
                vland.at[4 + k + i],
                vec_send.at[k + i],
                vec_recv.at[k + i],
                device,
            )
            for i, device in enumerate(devices)
        ]
        vland[k] = gvec[...]
        for copy in copies:
            copy.start()
        vec_copies.extend(copies)
        return copies

    def vec_add(copies, k):
        for copy in copies:
            copy.wait_recv()
        if len(copies) == 1:
            gvec[...] = gvec[...] + vland[4 + k]
        else:
            vland[4 + k + nb - 1] = gvec[...]
            total = jnp.zeros_like(gvec)
            for s in range(nb):
                total = total + vland[4 + k + lax.rem(z + nb - s + nb - 1, nb)]
            gvec[...] = total

    if fused:
        step = vec_step(0, [on_core])
        next_sum(3, 1)
        vec_add(step, 0)
        step = vec_step(1, [on_x])
        next_sum(1, 6)
        next_sum(2, 5)
        vec_add(step, 1)
        step = vec_step(2, [on_y])
        next_sum(0, 7)
        start_out(0)
        next_sum(3, 2)
        vec_add(step, 2)
        step = vec_step(3, along)
        next_sum(2, 6)
        next_sum(1, 7)
        start_out(1)
        next_sum(3, 3)
        vec_add(step, 3)
        next_sum(2, 7)
        start_out(2)
        for stage in range(4, STAGES):
            next_sum(3, stage)
        start_out(3)
    else:
        for g in range(4):
            start_out(g)

    for c in range(cols):
        pltpu.make_async_copy(act.at[c], act_h.at[c], stash_sem.at[c]).wait()
        for me in range(nb):

            @pl.when(z == me)
            def _():
                for k, (owner, dest, slot) in enumerate(rs_plan(me)):
                    rs_copy(c, owner, dest, slot, k).wait_send()
                if 0 < me < nb - 1:
                    owner = nb - 1 if me == 1 else 0
                    rs_copy(c, owner, owner, me, 3).wait_send()

    for copy in ctx_copies + vec_copies:
        copy.wait_send()
    if fused:
        for g in range(4):
            for stage in range(1, STAGES):
                for copy in sum_copies(g, stage):
                    copy.wait_send()
    igrad_copy.wait()
    for g in range(4):
        for copy in out_copies(g):
            copy.wait()


def per_device(
    cells,
    missing,
    context,
    cotangent,
    miss_embed,
    norm1_gain,
    norm1_shift,
    feat_qkv,
    feat_out,
    norm2_gain,
    norm2_shift,
    row_qkv,
    row_out,
    norm3_gain,
    norm3_shift,
    ff_in,
    ff_in_bias,
    ff_out,
    ff_out_bias,
):
    _, rows, cols, width = cells.shape
    nb = lax.axis_size("blk")
    fused = lax.axis_size("tab") == 8
    ff = ff_in.shape[1]
    ff_blocks = ff // width

    cells_t = jnp.transpose(cells[0], (1, 0, 2))
    cot_t = jnp.transpose(cotangent[0], (1, 0, 2))
    vec = jnp.concatenate(
        [
            miss_embed,
            norm1_gain,
            norm1_shift,
            norm2_gain,
            norm2_shift,
            norm3_gain,
            norm3_shift,
            ff_out_bias,
            ff_in_bias,
        ]
    ).astype(F32)
    vec = vec.reshape(8 + ff_blocks, width)

    any_spec = pl.BlockSpec(memory_space=pl.ANY)
    vmem_spec = pl.BlockSpec(memory_space=pltpu.VMEM)
    token = (cols, rows, width)
    vm = pltpu.VMEM
    dma = pltpu.SemaphoreType.DMA
    shape = jax.ShapeDtypeStruct
    results = pl.pallas_call(
        functools.partial(layer_kernel, nb, fused),
        out_shape=(
            shape(token, BF16),
            shape(token, F32),
            shape(feat_qkv.shape, BF16),
            shape(feat_out.shape, BF16),
            shape(row_qkv.shape, BF16),
            shape(row_out.shape, BF16),
            shape(ff_in.shape, BF16),
            shape(ff_out.shape, BF16),
            shape((16, width), F32),
            shape(token, BF16),
            shape((3,) + token, BF16),
            shape((cols, cols, rows, HEAD), F32),
            shape(token, BF16),
        ),
        in_specs=[any_spec] * 2 + [vmem_spec] * 3 + [any_spec] * 6,
        out_specs=(any_spec,) * 8 + (vmem_spec,) + (any_spec,) * 4,
        scratch_shapes=[
            vm(token, BF16),
            vm(row_qkv.shape, BF16),
            vm(row_out.shape, BF16),
            vm(ff_in.shape, BF16),
            vm((ff // 128, 128, width), BF16),
            vm((2, width, width), BF16),
            vm((cols, rows, 1), F32),
            vm(token, F32),
            vm((cols * nb // 2, 2 * rows, width), BF16),
            vm((cols, nb, rows, width), BF16),
            vm((cols, nb, rows, width), BF16),
            vm(token, F32),
            vm((cols * ff_blocks, rows, width), BF16),
            vm((cols * ff_blocks * rows // CHUNK, CHUNK, width), BF16),
            vm((2 * cols, rows, width), BF16),
            vm(token, BF16),
            vm((3, width, width), F32),
            vm((nb, rows, HEAD), BF16),
            vm(token, BF16),
            vm(token, F32),
            vm((2 * ff_blocks + 4, width, width), BF16),
            vm((11, 16, width), F32),
            dma((5,)),
            dma((7,)),
            dma((4,)),
            dma((16,)),
            dma((nb,)),
            dma((nb,)),
            dma((cols, 5)),
            dma((cols, nb)),
            dma((cols,)),
            dma((cols, nb)),
            dma((cols, nb)),
            dma((4, 19)),
            dma((4, 19)),
            dma((6,)),
            dma((6,)),
            pltpu.SemaphoreType.REGULAR,
            pltpu.SemaphoreType.REGULAR((4,)),
        ],
        compiler_params=pltpu.CompilerParams(
            collective_id=0, has_side_effects=True, vmem_limit_bytes=64 * 1024 * 1024
        ),
    )(
        cells_t,
        cot_t,
        jnp.transpose(missing[0], (1, 0)),
        context,
        vec,
        feat_qkv,
        feat_out,
        row_qkv,
        row_out,
        ff_in,
        ff_out.reshape(ff // 128, 128, width),
    )
    act, igrad = results[0], results[1]
    sums = [g.astype(F32) for g in results[2:8]] + [results[8]]
    if not fused:
        sums = lax.psum(sums, ("tab", "blk"))
    g_fqkv, g_fout, g_rqkv, g_rout, g_fin, g_fdn, gvec = sums
    return (
        jnp.transpose(act, (1, 0, 2))[None],
        jnp.transpose(igrad, (1, 0, 2))[None],
        gvec[EMBED],
        gvec[GAIN1],
        gvec[SHIFT1],
        g_fqkv,
        g_fout,
        gvec[GAIN2],
        gvec[SHIFT2],
        g_rqkv,
        g_rout,
        gvec[GAIN3],
        gvec[SHIFT3],
        g_fin,
        gvec[IN_BIAS : IN_BIAS + ff_blocks].reshape(ff),
        g_fdn,
        gvec[OUT_BIAS],
    )


def solution(mesh):
    split = (
        P("tab", "blk", None, None),
        P("tab", "blk", None),
        P("tab", "blk"),
        P("tab", "blk", None, None),
    )
    return jax.shard_map(
        per_device,
        mesh=mesh,
        in_specs=split + (P(),) * 15,
        out_specs=(P("tab", "blk", None, None),) * 2 + (P(),) * 15,
        check_vma=False,
    )
```

```python
import functools
import math

import jax
import jax.numpy as jnp
from jax import lax
from jax.experimental import pallas as pl
from jax.experimental.pallas import tpu as pltpu
from jax.sharding import PartitionSpec as P

HEADS = 4
HEAD = 128
EPS = 1e-05
SCALE = 1.0 / math.sqrt(HEAD)
MESH = pl.DeviceIdType.MESH
F32 = jnp.float32
BF16 = jnp.bfloat16
EMBED, GAIN1, SHIFT1, GAIN2, SHIFT2, GAIN3, SHIFT3, OUT_BIAS, IN_BIAS = range(9)
CHUNK = 64
PUMPS = {
    "head3": ((0, 0),),
    "columns": ((1, 0),),
    "row_q": ((0, 1),),
    "norm2_2": ((0, 2), (1, 1), (2, 0)),
    "scores0": ((3, 0),),
    "scores1": ((1, 2),),
    "scores2": ((6, 0),),
    "queries": ((0, 3),),
    "keys": ((2, 1),),
    "normed1": ((3, 1), (4, 0), (6, 1)),
    "norm1_0": ((5, 0),),
    "norm1_1": ((2, 2), (1, 3)),
    "norm1_2": ((3, 2),),
    "end0": ((4, 1), (6, 2), (5, 1), (4, 2)),
    "end1": ((0, 4), (5, 2), (2, 3), (0, 5)),
    "end2": ((1, 4), (3, 3), (0, 6), (6, 3)),
    "end3": ((4, 3), (5, 3), (0, 7), (1, 5)),
    "end4": ((2, 4), (3, 4), (6, 4), (4, 4), (1, 6), (5, 4), (2, 5), (3, 5), (6, 5), (4, 5), (1, 7), (5, 5), (2, 6), (3, 6), (6, 6), (2, 7), (3, 7), (4, 6), (6, 7), (5, 6), (4, 7), (5, 7)),
}
HALF = 256
STAGES = 8


def dot(a, b):
    return jnp.dot(a, b, preferred_element_type=F32)


def dot_rt(a, b):
    return lax.dot_general(a, b, (((1,), (1,)), ((), ())), preferred_element_type=F32)


def dot_lt(a, b):
    return lax.dot_general(a, b, (((0,), (0,)), ((), ())), preferred_element_type=F32)


def stats(x):
    center = x - jnp.mean(x, axis=-1, keepdims=True)
    rstd = lax.rsqrt(jnp.mean(center * center, axis=-1, keepdims=True) + EPS)
    return center * rstd, rstd


def norm_back(x, gain, dy):
    xhat, rstd = stats(x)
    dxh = dy * gain
    dx = rstd * (
        dxh
        - jnp.mean(dxh, axis=-1, keepdims=True)
        - xhat * jnp.mean(dxh * xhat, axis=-1, keepdims=True)
    )
    dgain = jnp.sum(dy * xhat, axis=0, keepdims=True)
    dshift = jnp.sum(dy, axis=0, keepdims=True)
    return dx, dgain, dshift


def layer_kernel(
    nb,
    fused,
    cells_h,
    cot_h,
    missing,
    context,
    *rest,
):
    vectors, rest = rest[:9], rest[9:]
    (
    wfqkv_h,
    wfout_h,
    wrqkv_h,
    wrout_h,
    wfin_h,
    wfdn_h,
    act_h,
    igrad_h,
    gfqkv_h,
    gfout_h,
    grqkv_h,
    grout_h,
    gfin_h,
    gfdn_h,
    gvec,
    n1_h,
    fqkv_h,
    fp_h,
    fo_h,
    cot,
    wrqkv,
    wrout,
    wfin,
    wfdn,
    wkvt,
    absent,
    af,
    n2,
    rss,
    rsr,
    g2,
    hid,
    gin,
    nro,
    gy2,
    dkv,
    dq,
    ctxa,
    act,
    dn2,
    gb,
    vland,
    vec,
    load_sem,
    feat_sem,
    stash_sem,
    out_sem,
    ctx_send,
    ctx_recv,
    ag_send,
    ag_recv,
    rs_send,
    rs_recv,
    ar_send,
    ar_recv,
    vec_send,
    vec_recv,
    ready,
    free,
    ) = rest
    cols, rows, width = g2.shape
    seg = width
    ff_blocks = wfin.shape[1] // seg
    quarter = rows // CHUNK
    ro_at = cols
    t = lax.axis_index("tab")
    z = lax.axis_index("blk")
    core, xbit, ybit = lax.rem(t, 2), lax.rem(lax.div(t, 2), 2), lax.rem(lax.div(t, 4), 2)
    on_core = (t + 1 - 2 * core, z)
    on_x = (t + 2 - 4 * xbit, z)
    on_y = (t + 4 - 8 * ybit, z)
    along = [(t, lax.rem(z + d, nb)) for d in range(1, nb)]
    partners = along + ([on_core, on_x, on_y] if fused else [])

    def load_all(pairs, sem):
        copies = [
            pltpu.make_async_copy(a, b, sem.at[i]) for i, (a, b) in enumerate(pairs)
        ]
        for copy in copies:
            copy.start()
        return copies

    def signal_all(sem):
        for device in partners:
            pl.semaphore_signal(sem, inc=1, device_id=device, device_id_type=MESH)

    def await_all(sem):
        pl.semaphore_wait(sem, len(partners))

    def remote(source, dest, send, recv, device):
        return pltpu.make_async_remote_copy(
            src_ref=source,
            dst_ref=dest,
            send_sem=send,
            recv_sem=recv,
            device_id=device,
            device_id_type=MESH,
        )

    def block(c, s):
        return n2.at[c * (nb // 2) + s // 2, pl.ds(pl.multiple_of((s % 2) * rows, rows), rows)]

    own_hi, own_lo = lax.div(z, 2), pl.multiple_of(lax.rem(z, 2) * rows, rows)

    def own_block(c):
        return n2.at[c * (nb // 2) + own_hi, pl.ds(own_lo, rows)]

    def on_each(run, devices=None):
        for me in range(nb) if devices is None else devices:

            @pl.when(z == me)
            def _():
                run(me)

    ends, middle = (0, nb - 1), tuple(range(1, nb - 1))

    def pass_on(c, s, me, step):
        return remote(
            block(c, s),
            block(c, s),
            ag_send.at[c, s, (step + 1) // 2],
            ag_recv.at[c, s],
            (t, me + step),
        )

    def await_block(c, s):
        pltpu.make_async_copy(block(c, s), block(c, s), ag_recv.at[c, s]).wait()

    def gather_sends(c, me, far):
        out = []
        for step in (-1, 1):
            if 0 <= me + step < nb and 0 <= me - far * step < nb:
                out.append((me - far * step, pass_on(c, me - far * step, me, step)))
        return out

    def start_gather(c, devices=None):
        def run(me):
            for _, copy in gather_sends(c, me, 0):
                copy.start()

        on_each(run, devices)

    def hop(c, far):
        def run(me):
            for s, copy in gather_sends(c, me, far):
                await_block(c, s)
                copy.start()

        on_each(run, middle)

    def await_gather(c):
        def run(me):
            for s in range(nb):
                if s != me:
                    await_block(c, s)

        on_each(run, ends)

    def await_gather_sends(c):
        def run(me):
            for far in range(nb - 1):
                for _, copy in gather_sends(c, me, far):
                    copy.wait_send()

        on_each(run)

    def slot_of(owner, me):
        return nb if owner == me else owner

    def rs_copy(c, owner, me):
        step = 1 if owner > me else -1
        there = owner if step < 0 else slot_of(owner, me + step)
        return remote(
            rss.at[c, owner],
            rsr.at[c, there],
            rs_send.at[c, owner],
            rs_recv.at[c, there],
            (t, me + step),
        )

    def start_scatter(c):
        def run(me):
            for owner in sorted((o for o in range(nb) if o != me), key=lambda o: -abs(o - me)):
                rs_copy(c, owner, me).start()

        on_each(run, ends)

    def await_slot(c, s):
        pltpu.make_async_copy(rsr.at[c, s], rsr.at[c, s], rs_recv.at[c, s]).wait()

    def combine(c, part):
        def run(me):
            low = me == 1
            owner = (nb - 1, nb - 2, 0)[part] if low else (0, 1, nb - 1)[part]
            await_slot(c, owner)
            rss[c, owner] = (rss[c, owner].astype(F32) + rsr[c, owner].astype(F32)).astype(BF16)
            rs_copy(c, owner, me).start()

        on_each(run, middle)

    def own_slots(me):
        return [] if me == nb - 1 else [me], [] if me == 0 else [nb]

    def await_scatter_sends(c):
        def run(me):
            for owner in range(nb):
                if owner != me:
                    rs_copy(c, owner, me).wait_send()

        on_each(run)

    groups = [
        (gb, 0, 4, 0, (hid, 0)),
        (gb, 4, 5, 4, (hid, 4)),
        (gb, 9, 3, 9, (hid, 9)),
        (n2, 0, 1, 12, (nro, 0)),
        (n2, 1, 1, 13, (nro, 1)),
        (n2, 2, 1, 14, (nro, 2)),
        (n2, 3, 1, 15, (nro, 3)),
    ]
    reached = [0] * len(groups)

    def pump(point):
        for g, stage in PUMPS.get(point, ()):
            next_sum(g, stage)

    lanes_a, lanes_b = pl.ds(0, HALF), pl.ds(HALF, HALF)

    def at16(v):
        return pl.multiple_of(v, 16)

    row_core = core * 256
    paths = [(lanes_a, xbit, ybit, on_x, on_y), (lanes_b, ybit, xbit, on_y, on_x)]

    def landing(g, stage):
        _, _, n, place, (land, land_at) = groups[g]
        if stage == 0:
            return land, pl.ds(land_at, n)
        if stage == 1:
            return wfdn, pl.ds(place, n)
        return gin, pl.ds(place + (16 if stage == 3 else 0), n)

    def sum_copies(g, stage):
        ref, base, n, _, _ = groups[g]
        whole = pl.ds(0, width)

        def final(row, count, lanes):
            return ref.at[pl.ds(base, n), pl.ds(at16(row), count), lanes]

        out = []
        if stage < 4:
            land, at = landing(g, stage)
            if stage > 0:
                last, last_at = landing(g, stage - 1)
        if stage == 0:
            out.append((final((1 - core) * 256, 256, whole), land.at[at], on_core))
        elif stage == 1:
            for lanes, bit, _, device, _ in paths:
                away = last.at[last_at, pl.ds(at16((1 - bit) * 128), 128), lanes]
                out.append((away, land.at[at, :, lanes], device))
        elif stage == 2:
            for lanes, _, bit, _, device in paths:
                away = last.at[last_at, pl.ds(at16((1 - bit) * 64), 64), lanes]
                out.append((away, land.at[at, :, lanes], device))
        elif stage == 3:
            for d in range(1, nb):
                away = last.at[last_at, pl.ds(at16(lax.rem(z + d, nb) * 16), 16), :]
                out.append((away, land.at[at, pl.ds((d - 1) * 16, 16), :], along[d - 1]))
        elif stage == 4:
            last, last_at = landing(g, 3)
            for d in range(1, nb):
                for lanes, bit1, bit2, _, _ in paths:
                    row = row_core + bit1 * 128 + bit2 * 64 + z * 16
                    mine = last.at[last_at, pl.ds(0, 16), lanes]
                    out.append((mine, final(row, 16, lanes), along[d - 1]))
        elif stage == 5:
            for lanes, bit1, bit2, _, device in paths:
                mine = final(row_core + bit1 * 128 + bit2 * 64, 64, lanes)
                out.append((mine, mine, device))
        elif stage == 6:
            for lanes, bit1, _, device, _ in paths:
                mine = final(row_core + bit1 * 128, 128, lanes)
                out.append((mine, mine, device))
        else:
            mine = final(row_core, 256, whole)
            out.append((mine, mine, on_core))
        first = (0, 1, 3, 5, 8, 14, 16, 18)[stage]
        return [
            remote(a, b, ar_send.at[g, first + i], ar_recv.at[g, first + i], device)
            for i, (a, b, device) in enumerate(out)
        ]

    def start_sum(g, stage=0):
        if fused:
            if stage == STAGES - 1:
                pl.semaphore_wait(free.at[g], 1)
            for copy in sum_copies(g, stage):
                copy.start()

    def add_landed(g, stage):
        ref, base, n, _, _ = groups[g]
        blocks = pl.ds(base, n)
        land, at = landing(g, stage)
        if stage == 0:
            mine = ref[blocks, pl.ds(at16(row_core), 256), :]
            land[at] = (mine.astype(F32) + land[at].astype(F32)).astype(BF16)
            return
        last, last_at = landing(g, stage - 1)
        if stage == 3:
            total = last[last_at, pl.ds(at16(z * 16), 16), :].astype(F32)
            for d in range(1, nb):
                total = total + land[at, pl.ds((d - 1) * 16, 16), :].astype(F32)
            total = total.astype(BF16)
            land[at, pl.ds(0, 16), :] = total
            for i, (lanes, bit1, bit2, _, _) in enumerate(paths):
                row = at16(row_core + bit1 * 128 + bit2 * 64 + z * 16)
                ref[blocks, pl.ds(row, 16), lanes] = total[:, :, i * HALF : (i + 1) * HALF]
            return
        count = 128 if stage == 1 else 64
        for lanes, bit1, bit2, _, _ in paths:
            row = at16((bit1 if stage == 1 else bit2) * count)
            mine = last[last_at, pl.ds(row, count), lanes]
            land[at, :, lanes] = (
                mine.astype(F32) + land[at, :, lanes].astype(F32)
            ).astype(BF16)

    def next_sum(g, stage):
        if not fused:
            return
        assert reached[g] == stage
        reached[g] += 1
        for copy in sum_copies(g, stage):
            copy.wait_recv()
        if stage < 4:
            add_landed(g, stage)
        if stage == 0:
            for copy in sum_copies(g, stage):
                copy.wait_send()
            pl.semaphore_signal(free.at[g], inc=1, device_id=on_core, device_id_type=MESH)
        if stage + 1 < STAGES:
            start_sum(g, stage + 1)
        else:
            start_out(g)

    def out_copies(g):
        if g == 0:
            pairs = [
                (gb.at[f], gfdn_h.at[pl.ds(f * seg, seg)]) for f in range(ff_blocks)
            ]
            first = 0
        elif g == 1:
            pairs = [
                (gb.at[4 + f], gfin_h.at[:, pl.ds(f * seg, seg)]) for f in range(ff_blocks)
            ] + [(gb.at[8], grout_h)]
            first = 4
        elif g == 2:
            pairs = [(gb.at[9 + b], grqkv_h.at[:, pl.ds(b * seg, seg)]) for b in range(3)]
            first = 9
        elif g == 3:
            pairs = [(n2.at[0], gfout_h)]
            first = 12
        else:
            pairs = [(n2.at[g - 3], gfqkv_h.at[:, pl.ds((g - 4) * seg, seg)])]
            first = 9 + g
        return [
            pltpu.make_async_copy(a, b, out_sem.at[first + i]) for i, (a, b) in enumerate(pairs)
        ]

    def start_out(g):
        for copy in out_copies(g):
            copy.start()

    barrier = pltpu.get_barrier_semaphore()
    signal_all(barrier)
    marks = jnp.concatenate(
        [missing[:, 0, :].astype(F32), jnp.zeros((8 - cols, rows), F32)], axis=0
    ).T
    for c in range(cols):
        absent[c] = marks[:, c : c + 1]
    ctxa[z] = jnp.broadcast_to(context[...].astype(F32), (HEAD, rows)).T.astype(BF16)
    gvec[...] = jnp.zeros_like(gvec)

    for i, vector in enumerate(vectors):
        count = vector.shape[0] // width
        vec[i : i + count, :] = vector[...].astype(F32).reshape(count, width)

    def row(i):
        return vec[i : i + 1, :]

    ones = (
        lax.broadcasted_iota(jnp.int32, (width, HEAD), 0) // HEAD
        == lax.broadcasted_iota(jnp.int32, (width, HEAD), 1)
    ).astype(BF16)
    ones_t = (
        lax.broadcasted_iota(jnp.int32, (HEAD, width), 1) // HEAD
        == lax.broadcasted_iota(jnp.int32, (HEAD, width), 0)
    ).astype(BF16)

    def base_of(cells, c, r):
        return jnp.where(
            absent[c, pl.ds(r, CHUNK), :] > 0, row(EMBED), cells[c, pl.ds(r, CHUNK), :].astype(F32)
        )

    ctx_copies = [
        remote(ctxa.at[z], ctxa.at[z], ctx_send.at[d], ctx_recv.at[z], along[d])
        for d in range(nb - 1)
    ]

    weights = [(wrqkv_h, wrqkv), (wrout_h, wrout), (wfin_h, wfin), (wfdn_h, wfdn), (cot_h, cot)]
    loads = [
        pltpu.make_async_copy(a, b, load_sem.at[i]) for i, (a, b) in enumerate(weights)
    ]

    def feature_forward(cells, wfqkv, wfout, n1, fqkv, fp, fo, hi, lo, spread):
        feat_loads = load_all(
            [(cells_h, cells), (wfqkv_h, wfqkv), (wfout_h, wfout)], feat_sem
        )
        for copy in loads:
            copy.start()
        feat_loads[0].wait()
        for c in range(cols):
            for r in range(0, rows, CHUNK):
                xhat, _ = stats(base_of(cells, c, r))
                n1[c, pl.ds(r, CHUNK), :] = (xhat * row(GAIN1) + row(SHIFT1)).astype(BF16)
        await_all(barrier)
        for copy in ctx_copies:
            copy.start()
        feat_loads[1].wait()
        n1_all = n1[...].reshape(cols * rows, width)
        for b in range(3):
            fqkv[b] = (
                dot(n1_all, wfqkv[:, b * seg : (b + 1) * seg])
                .astype(BF16)
                .reshape(cols, rows, width)
            )
        stash = [(n1, n1_h), (fqkv, fqkv_h)]
        for i in range(cols):
            for j in range(cols):
                for r in range(0, rows, CHUNK):
                    prod = fqkv[0, i, pl.ds(r, CHUNK), :].astype(F32) * fqkv[
                        1, j, pl.ds(r, CHUNK), :
                    ].astype(F32)
                    top = prod.astype(BF16)
                    hi[pl.ds(j * rows + r, CHUNK), :] = top
                    lo[pl.ds(j * rows + r, CHUNK), :] = (prod - top.astype(F32)).astype(BF16)
            scores = (dot(hi[...], ones) + dot(lo[...], ones)) * SCALE
            parts = [scores[j * rows : (j + 1) * rows] for j in range(cols)]
            top = functools.reduce(jnp.maximum, parts)
            parts = [jnp.exp(part - top) for part in parts]
            inv = 1.0 / functools.reduce(jnp.add, parts)
            for j in range(cols):
                fp[i, j] = parts[j] * inv
            spread[...] = dot(fp[i].reshape(cols * rows, HEAD).astype(BF16), ones_t)
            weigh(spread, fqkv, 2, fo, None, i, 1.0)
            if i == 0:
                feat_loads[2].wait()
            spread[0:rows, :] = dot(fo[i], wfout[...])
            for r in range(0, rows, CHUNK):
                after = base_of(cells, i, r) + spread[pl.ds(r, CHUNK), :]
                af[i, pl.ds(r, CHUNK), :] = after
                xhat, _ = stats(after)
                n2[i * (nb // 2) + own_hi, pl.ds(pl.multiple_of(own_lo + r, CHUNK), CHUNK), :] = (
                    xhat * row(GAIN2) + row(SHIFT2)
                ).astype(BF16)
            start_gather(i, None if i == 0 else ends)
        for copy in load_all(stash + [(fp, fp_h), (fo, fo_h)], stash_sem):
            copy.wait()

    def weigh(spread, source, part, dest, dest_part, i, scale):
        for r in range(0, rows, CHUNK):
            rr = pl.ds(r, CHUNK)
            total = functools.reduce(
                jnp.add,
                [
                    spread[pl.ds(j * rows + r, CHUNK), :]
                    * (source[j, rr, :] if part is None else source[part, j, rr, :]).astype(F32)
                    for j in range(cols)
                ],
            )
            total = (total * scale).astype(BF16)
            if dest_part is None:
                dest[i, rr, :] = total
            else:
                dest[dest_part, i, rr, :] = total

    token = (cols, rows, width)
    vm = pltpu.VMEM
    feature_scratch = [
        vm(token, BF16),
        vm(wfqkv_h.shape, BF16),
        vm(wfout_h.shape, BF16),
        vm(token, BF16),
        vm((3,) + token, BF16),
        vm((cols, cols, rows, HEAD), F32),
        vm(token, BF16),
        vm((cols * rows, width), BF16),
        vm((cols * rows, width), BF16),
        vm((cols * rows, width), F32),
    ]
    pl.run_scoped(feature_forward, *feature_scratch)
    hop(0, 1)

    loads[0].wait()
    for b in range(2):
        wkvt[b] = wrqkv[:, (b + 1) * seg : (b + 2) * seg].astype(F32).T.astype(BF16)
    for load in loads[1:]:
        load.wait()
    for s in range(nb):

        @pl.when(z != s)
        def _():
            pltpu.make_async_copy(ctxa.at[s], ctxa.at[s], ctx_recv.at[s]).wait()

    hop(0, 2)
    start_gather(1, middle)

    def ff_weight(f):
        return wfdn[pl.ds(f * (seg // 128), seg // 128)].reshape(seg, width)

    def gin_block(c, f):
        return pl.ds((c * ff_blocks + f) * quarter, quarter)

    def ff_weights():
        cot_all = cot[...].reshape(cols * rows, width)
        n3_all = nro[0:cols].reshape(cols * rows, width)
        for f in range(ff_blocks):
            hid_all = jnp.concatenate([hid[c * ff_blocks + f] for c in range(cols)], axis=0)
            gb[f] = dot_lt(hid_all, cot_all).astype(BF16)
            gin_all = jnp.concatenate(
                [gin[gin_block(c, f)].reshape(rows, seg) for c in range(cols)], axis=0
            )
            gb[ff_blocks + f] = dot_lt(n3_all, gin_all).astype(BF16)
        gb[2 * ff_blocks] = dot_lt(
            nro[ro_at : ro_at + cols].reshape(cols * rows, width),
            gy2[...].reshape(cols * rows, width),
        ).astype(BF16)
        if fused:
            signal_all(ready)
            await_all(ready)
        start_sum(0)
        start_sum(1)

    def columns_stage(bias, q, kv, kvt, p, ot, dgel, ar):
        for s in range(nb):
            b = (ctxa[s].astype(F32) - 1.0) * 1e30
            for lane in range(0, rows, HEAD):
                bias[pl.ds(s * rows, rows), lane : lane + HEAD] = b

        def on_last(c, point):
            if fused and PUMPS.get(point):

                @pl.when(c == cols - 1)
                def _():
                    pump(point)

        def column(c, _):
            await_gather(c)
            x = n2[pl.ds(c * (nb // 2), nb // 2)].reshape(nb * rows, width)
            own = n2[c * (nb // 2) + own_hi, pl.ds(own_lo, rows), :]
            q[...] = dot(own, wrqkv[:, 0:seg]).astype(BF16)
            kv[0] = dot(x, wrqkv[:, seg : 2 * seg]).astype(BF16)
            kvt[1] = dot_rt(wkvt[1], x).astype(BF16)
            for h in range(HEADS):
                hs = slice(h * HEAD, (h + 1) * HEAD)
                s = dot_rt(kv[0, :, hs], q[:, hs]) + bias[...]
                top = jnp.max(s, axis=0, keepdims=True)
                e = jnp.exp((s - top) * SCALE)
                p[h] = (e * (1.0 / jnp.sum(e, axis=0, keepdims=True))).astype(BF16)
                ot[hs, :] = dot(kvt[1, hs, :], p[h])
            nro[ro_at + c] = ot[...].T.astype(BF16)

            @pl.when(c + 1 < cols)
            def _():
                hop(c + 1, 1)

            kv[1] = dot(x, wrqkv[:, 2 * seg : 3 * seg]).astype(BF16)
            kvt[0] = dot_rt(wkvt[0], x).astype(BF16)

            ar[...] = dot(nro[ro_at + c], wrout[...])
            for r in range(0, rows, CHUNK):
                rr = pl.ds(r, CHUNK)
                after = af[c, rr, :] + ar[rr, :]
                ar[rr, :] = after
                xhat, _ = stats(after)
                nro[c, rr, :] = (xhat * row(GAIN3) + row(SHIFT3)).astype(BF16)
            for f in range(ff_blocks):
                fs = slice(f * seg, (f + 1) * seg)
                dgel[f] = dot(nro[c], wfin[:, fs])
                for r in range(0, rows, CHUNK):
                    rr = pl.ds(r, CHUNK)
                    u = dgel[f, rr, :] + row(IN_BIAS + f)
                    c0 = math.sqrt(2.0 / math.pi)
                    sq = u * u
                    th = jnp.tanh(u * (c0 + (c0 * 0.044715) * sq))
                    half = 0.5 * (1.0 + th)
                    hid[c * ff_blocks + f, rr, :] = (u * half).astype(BF16)
                    dgel[f, rr, :] = half + 0.5 * u * (1.0 - th * th) * (
                        c0 + (3.0 * c0 * 0.044715) * sq
                    )
            total = ar[...] + row(OUT_BIAS)
            for f in range(ff_blocks):
                total = total + dot(hid[c * ff_blocks + f], ff_weight(f))
            act[c] = total.astype(BF16)

            @pl.when(c > 0)
            def _():
                combine(c - 1, 0)

            pltpu.make_async_copy(act.at[c], act_h.at[c], stash_sem.at[c]).start()
            back = jnp.zeros((rows, width), F32)
            for f in range(ff_blocks):
                fs = slice(f * seg, (f + 1) * seg)
                gi = (dot_rt(cot[c], ff_weight(f)) * dgel[f]).astype(BF16)
                gin[gin_block(c, f)] = gi.reshape(quarter, CHUNK, seg)
                gvec[IN_BIAS + f : IN_BIAS + f + 1, :] += jnp.sum(
                    gi.astype(F32), axis=0, keepdims=True
                )
                back = back + dot_rt(gi, wfin[:, fs])
            dgel[0] = back
            for r in range(0, rows, CHUNK):
                rr = pl.ds(r, CHUNK)
                dx, dgain, dshift = norm_back(ar[rr, :], row(GAIN3), dgel[0, rr, :])
                g3 = cot[c, rr, :].astype(F32)
                g = g3 + dx
                g2[c, rr, :] = g
                gy2[c, rr, :] = g.astype(BF16)
                gvec[GAIN3 : GAIN3 + 1, :] += dgain
                gvec[SHIFT3 : SHIFT3 + 1, :] += dshift
                gvec[OUT_BIAS : OUT_BIAS + 1, :] += jnp.sum(g3, axis=0, keepdims=True)

            ar[...] = dot_rt(gy2[c], wrout[...])

            @pl.when(c + 1 < cols)
            def _():
                hop(c + 1, 2)

            @pl.when(c + 2 < cols)
            def _():
                start_gather(c + 2, middle)

            @pl.when(c == cols - 1)
            def _():
                ff_weights()

            gro = ar[...].astype(BF16)
            table = pl.ds(pl.multiple_of(c * nb * rows, nb * rows), nb * rows)
            for h in range(HEADS):
                hs = slice(h * HEAD, (h + 1) * HEAD)
                vs = slice(width + h * HEAD, width + (h + 1) * HEAD)
                dp = dot_rt(kv[1, :, hs], gro[:, hs])
                pr = p[h].astype(F32)
                ds = (pr * (dp - jnp.sum(pr * dp, axis=0, keepdims=True))).astype(BF16)
                dkv[table, hs] = (dot(ds, q[:, hs]) * SCALE).astype(BF16)
                dkv[table, vs] = dot(p[h], gro[:, hs]).astype(BF16)
                ot[hs, :] = dot(kvt[0, hs, :], ds)
                on_last(c, f"head{h}")
            dq[c] = (ot[...].T * SCALE).astype(BF16)

            @pl.when(c > 0)
            def _():
                combine(c - 1, 1)

            for o in range(nb):
                part = pl.ds(pl.multiple_of((c * nb + o) * rows, rows), rows)
                rss[c, o] = dot_rt(dkv[part, :], wrqkv[:, seg : 3 * seg]).astype(BF16)
            start_scatter(c)

            @pl.when(c > 0)
            def _():
                combine(c - 1, 2)

            on_last(c, "scatter")
            dn2[c] = dot_rt(dq[c], wrqkv[:, 0:seg])
            return 0

        lax.fori_loop(0, cols, column, 0)

    pl.run_scoped(
        columns_stage,
        vm((nb * rows, rows), F32),
        vm((rows, width), BF16),
        vm((2, nb * rows, width), BF16),
        vm((2, width, nb * rows), BF16),
        vm((HEADS, nb * rows, rows), BF16),
        vm((width, rows), F32),
        vm((ff_blocks, rows, width), F32),
        vm((rows, width), F32),
    )

    def feature_backward(cells, wfqkv, wfout, n1, fqkv, fp, fo, hi, lo, spread, gfo, dqkv, dsl):
        again = load_all(
            [
                (cells_h, cells),
                (wfqkv_h, wfqkv),
                (wfout_h, wfout),
                (n1_h, n1),
                (fqkv_h, fqkv),
                (fp_h, fp),
                (fo_h, fo),
            ],
            feat_sem,
        )
        pump("columns")
        x_all = n2[...].reshape(cols * nb * rows, width)
        half = width // 2
        for i in range(2):
            at = slice(i * half, (i + 1) * half)
            got = dot_lt(x_all[:, at], dkv[...]).astype(BF16)
            gb[10, at, :] = got[:, 0:seg]
            gb[11, at, :] = got[:, seg:]
            pump(f"row_kv{i}")
        own = jnp.concatenate(
            [n2[c * (nb // 2) + own_hi, pl.ds(own_lo, rows), :] for c in range(cols)], axis=0
        )
        gb[9] = dot_lt(own, dq[...].reshape(cols * rows, width)).astype(BF16)
        start_sum(2)
        pump("row_q")
        for part in range(3):
            combine(cols - 1, part)
        for c in range(cols):
            await_gather_sends(c)
        pump("combine")
        for c in range(cols):
            def arrived(me):
                above, below = own_slots(me)
                for s in above + below:
                    await_slot(c, s)
                    dn2[c] += rsr[c, s].astype(F32)

            on_each(arrived)
            for r in range(0, rows, CHUNK):
                rr = pl.ds(r, CHUNK)
                dy = dn2[c, rr, :] + rss[c, z, rr, :].astype(F32)
                dx, dgain, dshift = norm_back(af[c, rr, :], row(GAIN2), dy)
                g = g2[c, rr, :] + dx
                g2[c, rr, :] = g
                gy2[c, rr, :] = g.astype(BF16)
                gvec[GAIN2 : GAIN2 + 1, :] += dgain
                gvec[SHIFT2 : SHIFT2 + 1, :] += dshift
            pump(f"norm2_{c}")
        for copy in again:
            copy.wait()
        gy1 = gy2[...].reshape(cols * rows, width)
        gfo[...] = dot_rt(gy1, wfout[...]).astype(BF16).reshape(cols, rows, width)
        n2[0] = dot_lt(fo[...].reshape(cols * rows, width), gy1).astype(BF16)
        start_sum(3)
        pump("feat_out")
        n1_flat = n1[...].reshape(cols * rows, width)

        def part_done(b):
            n2[1 + b] = dot_lt(n1_flat, dqkv[b].reshape(cols * rows, width)).astype(BF16)
            start_sum(4 + b)

        for i in range(cols):
            spread[...] = dot(
                jnp.concatenate([fp[j, i].astype(BF16) for j in range(cols)], axis=0), ones_t
            )
            weigh(spread, gfo, None, dqkv, 2, i, 1.0)
        part_done(2)
        pump("values")
        for i in range(cols):
            for j in range(cols):
                for r in range(0, rows, CHUNK):
                    prod = gfo[i, pl.ds(r, CHUNK), :].astype(F32) * fqkv[
                        2, j, pl.ds(r, CHUNK), :
                    ].astype(F32)
                    top = prod.astype(BF16)
                    hi[pl.ds(j * rows + r, CHUNK), :] = top
                    lo[pl.ds(j * rows + r, CHUNK), :] = (prod - top.astype(F32)).astype(BF16)
            dp = dot(hi[...], ones) + dot(lo[...], ones)
            parts = [dp[j * rows : (j + 1) * rows] for j in range(cols)]
            mean = functools.reduce(jnp.add, [fp[i, j] * parts[j] for j in range(cols)])
            for j in range(cols):
                dsl[i, j] = (fp[i, j] * (parts[j] - mean)).astype(BF16)
            pump(f"scores{i}")
        for i in range(cols):
            spread[...] = dot(dsl[i].reshape(cols * rows, HEAD), ones_t)
            weigh(spread, fqkv, 1, dqkv, 0, i, SCALE)
        part_done(0)
        pump("queries")
        for i in range(cols):
            spread[...] = dot(jnp.concatenate([dsl[j, i] for j in range(cols)], axis=0), ones_t)
            weigh(spread, fqkv, 0, dqkv, 1, i, SCALE)
        part_done(1)
        pump("keys")
        spread[...] = functools.reduce(
            jnp.add,
            [
                dot_rt(dqkv[b].reshape(cols * rows, width), wfqkv[:, b * seg : (b + 1) * seg])
                for b in range(3)
            ],
        )
        pump("normed1")
        for c in range(cols):
            for r in range(0, rows, CHUNK):
                rr = pl.ds(r, CHUNK)
                dx, dgain, dshift = norm_back(
                    base_of(cells, c, r), row(GAIN1), spread[pl.ds(c * rows + r, CHUNK), :]
                )
                g = g2[c, rr, :] + dx
                gone = absent[c, rr, :] > 0
                g2[c, rr, :] = jnp.where(gone, 0.0, g)
                gvec[GAIN1 : GAIN1 + 1, :] += dgain
                gvec[SHIFT1 : SHIFT1 + 1, :] += dshift
                gvec[EMBED : EMBED + 1, :] += jnp.sum(
                    jnp.where(gone, g, 0.0), axis=0, keepdims=True
                )
            pump(f"norm1_{c}")

    pl.run_scoped(
        feature_backward,
        *feature_scratch,
        vm(token, BF16),
        vm((3,) + token, BF16),
        vm((cols, cols, rows, HEAD), BF16),
    )
    igrad_copy = pltpu.make_async_copy(g2, igrad_h, stash_sem.at[cols])
    igrad_copy.start()

    vec_copies = []

    def vec_step(k, devices):
        copies = [
            remote(
                vland.at[k],
                vland.at[4 + k + i],
                vec_send.at[k + i],
                vec_recv.at[k + i],
                device,
            )
            for i, device in enumerate(devices)
        ]
        vland[k] = gvec[...]
        for copy in copies:
            copy.start()
        vec_copies.extend(copies)
        return copies

    def vec_add(copies, k):
        for copy in copies:
            copy.wait_recv()
        if len(copies) == 1:
            gvec[...] = gvec[...] + vland[4 + k]
        else:
            vland[4 + k + nb - 1] = gvec[...]
            total = jnp.zeros_like(gvec)
            for s in range(nb):
                total = total + vland[4 + k + lax.rem(z + nb - s + nb - 1, nb)]
            gvec[...] = total

    if fused:
        step = vec_step(0, [on_core])
        pump("end0")
        vec_add(step, 0)
        step = vec_step(1, [on_x])
        pump("end1")
        vec_add(step, 1)
        step = vec_step(2, [on_y])
        pump("end2")
        vec_add(step, 2)
        step = vec_step(3, along)
        pump("end3")
        vec_add(step, 3)
        pump("end4")
        assert all(stage == STAGES for stage in reached)
    else:
        for g in range(len(groups)):
            start_out(g)

    for c in range(cols):
        pltpu.make_async_copy(act.at[c], act_h.at[c], stash_sem.at[c]).wait()
        await_scatter_sends(c)

    for copy in ctx_copies + vec_copies:
        copy.wait_send()
    if fused:
        for g in range(len(groups)):
            for stage in range(1, STAGES):
                for copy in sum_copies(g, stage):
                    copy.wait_send()
    igrad_copy.wait()
    for g in range(len(groups)):
        for copy in out_copies(g):
            copy.wait()


def finish_kernel(*refs):
    ins, gvec, outs, vectors = refs[0:8], refs[8], refs[9:17], refs[17:26]
    low, high, same = refs[26:32], refs[32:38], refs[38:40]
    in_sem, out_sem = refs[40:]
    width = gvec.shape[1]
    loads = [
        pltpu.make_async_copy(a, b, in_sem.at[i]) for i, (a, b) in enumerate(zip(ins, same + low))
    ]
    stores = [
        pltpu.make_async_copy(a, b, out_sem.at[i])
        for i, (a, b) in enumerate(zip(same + high, outs))
    ]
    for copy in loads:
        copy.start()
    for i, vector in enumerate(vectors):
        count = vector.shape[0] // width
        vector[...] = gvec[i : i + count, :].reshape(vector.shape)
    for load, store in zip(loads[:2], stores[:2]):
        load.wait()
        store.start()
    for source, dest, load, store in zip(low, high, loads[2:], stores[2:]):
        load.wait()

        def convert(i, _):
            at = pl.ds(pl.multiple_of(i * CHUNK, CHUNK), CHUNK)
            dest[at, :] = source[at, :].astype(F32)
            return 0

        lax.fori_loop(0, source.shape[0] // CHUNK, convert, 0)
        store.start()
    for copy in stores:
        copy.wait()


def per_device(
    cells,
    missing,
    context,
    cotangent,
    miss_embed,
    norm1_gain,
    norm1_shift,
    feat_qkv,
    feat_out,
    norm2_gain,
    norm2_shift,
    row_qkv,
    row_out,
    norm3_gain,
    norm3_shift,
    ff_in,
    ff_in_bias,
    ff_out,
    ff_out_bias,
):
    _, rows, cols, width = cells.shape
    nb = lax.axis_size("blk")
    fused = lax.axis_size("tab") == 8
    ff = ff_in.shape[1]
    ff_blocks = ff // width

    cells_t = jnp.transpose(cells[0], (1, 0, 2))
    cot_t = jnp.transpose(cotangent[0], (1, 0, 2))
    any_spec = pl.BlockSpec(memory_space=pl.ANY)
    vmem_spec = pl.BlockSpec(memory_space=pltpu.VMEM)
    token = (cols, rows, width)
    vm = pltpu.VMEM
    dma = pltpu.SemaphoreType.DMA
    shape = jax.ShapeDtypeStruct
    results = pl.pallas_call(
        functools.partial(layer_kernel, nb, fused),
        out_shape=(
            shape(token, BF16),
            shape(token, F32),
            shape(feat_qkv.shape, BF16),
            shape(feat_out.shape, BF16),
            shape(row_qkv.shape, BF16),
            shape(row_out.shape, BF16),
            shape(ff_in.shape, BF16),
            shape(ff_out.shape, BF16),
            shape((16, width), F32),
            shape(token, BF16),
            shape((3,) + token, BF16),
            shape((cols, cols, rows, HEAD), F32),
            shape(token, BF16),
        ),
        in_specs=[any_spec] * 2 + [vmem_spec] * 11 + [any_spec] * 6,
        out_specs=(any_spec,) * 8 + (vmem_spec,) + (any_spec,) * 4,
        scratch_shapes=[
            vm(token, BF16),
            vm(row_qkv.shape, BF16),
            vm(row_out.shape, BF16),
            vm(ff_in.shape, BF16),
            vm((ff // 128, 128, width), BF16),
            vm((2, width, width), BF16),
            vm((cols, rows, 1), F32),
            vm(token, F32),
            vm((cols * nb // 2, 2 * rows, width), BF16),
            vm((cols, nb, rows, width), BF16),
            vm((cols, nb + 1, rows, width), BF16),
            vm(token, F32),
            vm((cols * ff_blocks, rows, width), BF16),
            vm((cols * ff_blocks * rows // CHUNK, CHUNK, width), BF16),
            vm((2 * cols, rows, width), BF16),
            vm(token, BF16),
            vm((cols * nb * rows, 2 * width), BF16),
            vm(token, BF16),
            vm((nb, rows, HEAD), BF16),
            vm(token, BF16),
            vm(token, F32),
            vm((2 * ff_blocks + 4, width, width), BF16),
            vm((11, 16, width), F32),
            vm((8 + ff_blocks, width), F32),
            dma((5,)),
            dma((7,)),
            dma((4,)),
            dma((16,)),
            dma((nb,)),
            dma((nb,)),
            dma((cols, nb, 2)),
            dma((cols, nb)),
            dma((cols, nb)),
            dma((cols, nb + 1)),
            dma((7, 19)),
            dma((7, 19)),
            dma((6,)),
            dma((6,)),
            pltpu.SemaphoreType.REGULAR,
            pltpu.SemaphoreType.REGULAR((7,)),
        ],
        compiler_params=pltpu.CompilerParams(
            collective_id=0, has_side_effects=True, vmem_limit_bytes=64 * 1024 * 1024
        ),
    )(
        cells_t,
        cot_t,
        jnp.transpose(missing, (2, 0, 1)),
        context,
        miss_embed,
        norm1_gain,
        norm1_shift,
        norm2_gain,
        norm2_shift,
        norm3_gain,
        norm3_shift,
        ff_out_bias,
        ff_in_bias,
        feat_qkv,
        feat_out,
        row_qkv,
        row_out,
        ff_in,
        ff_out.reshape(ff // 128, 128, width),
    )
    *results, gvec = results[:9]
    if not fused:
        results[2:], gvec = lax.psum(
            ([g.astype(F32) for g in results[2:]], gvec), ("tab", "blk")
        )
        results[2:] = [g.astype(BF16) for g in results[2:]]
    wide = [shape(g.shape, F32) for g in results[2:]]
    vectors = [shape((width,), F32)] * 8 + [shape((ff,), F32)]
    done = pl.pallas_call(
        finish_kernel,
        out_shape=(shape(token, BF16), shape(token, F32), *wide, *vectors),
        in_specs=[any_spec] * 8 + [vmem_spec],
        out_specs=(any_spec,) * 8 + (vmem_spec,) * 9,
        scratch_shapes=[vm(g.shape, BF16) for g in results[2:]]
        + [vm(g.shape, F32) for g in results[2:]]
        + [vm(token, BF16), vm(token, F32)]
        + [dma((8,)), dma((8,))],
        compiler_params=pltpu.CompilerParams(vmem_limit_bytes=64 * 1024 * 1024),
    )(*results, gvec)
    act, igrad, g_fqkv, g_fout, g_rqkv, g_rout, g_fin, g_fdn, *vectors = done
    embed, gain1, shift1, gain2, shift2, gain3, shift3, out_bias, in_bias = vectors
    return (
        jnp.transpose(act, (1, 0, 2))[None],
        jnp.transpose(igrad, (1, 0, 2))[None],
        embed,
        gain1,
        shift1,
        g_fqkv,
        g_fout,
        gain2,
        shift2,
        g_rqkv,
        g_rout,
        gain3,
        shift3,
        g_fin,
        in_bias,
        g_fdn,
        out_bias,
    )


def solution(mesh):
    split = (
        P("tab", "blk", None, None),
        P("tab", "blk", None),
        P("tab", "blk"),
        P("tab", "blk", None, None),
    )
    return jax.shard_map(
        per_device,
        mesh=mesh,
        in_specs=split + (P(),) * 15,
        out_specs=(P("tab", "blk", None, None),) * 2 + (P(),) * 15,
        check_vma=False,
    )
```

```python
import functools
import math

import jax
import jax.numpy as jnp
from jax import lax
from jax.experimental import pallas as pl
from jax.experimental.pallas import tpu as pltpu
from jax.sharding import PartitionSpec as P

HEADS = 4
HEAD = 128
EPS = 1e-05
SCALE = 1.0 / math.sqrt(HEAD)
MESH = pl.DeviceIdType.MESH
F32 = jnp.float32
BF16 = jnp.bfloat16
EMBED, GAIN1, SHIFT1, GAIN2, SHIFT2, GAIN3, SHIFT3, OUT_BIAS, IN_BIAS = range(9)
CHUNK = 64
GROUPS = ((0, 1), (2, 3), (4, 5), (6, 7), (8, 9, 10, 11), (12, 13), (14,), (15,))
PUMPS = {
    "head3": ((0, 0), (1, 0)),
    "row_kv0": ((0, 1),),
    "row_kv1": ((2, 0), (3, 0), (1, 1)),
    "norm2_0": ((0, 2),),
    "earlier": ((2, 1), (4, 0)),
    "window": ((3, 1),),
    "norm2_2": ((1, 2),),
    "keys": ((0, 3), (2, 2)),
    "norm1_0": ((4, 1), (6, 0), (7, 0), (1, 3), (3, 2)),
    "norm1_1": ((5, 0), (0, 4)),
    "end0": ((2, 3), (4, 2), (1, 4), (6, 1), (7, 1), (3, 3)),
    "end1": ((5, 1), (2, 4), (0, 5), (1, 5), (6, 2), (7, 2), (5, 2), (4, 3), (2, 5), (3, 4)),
    "end2": ((0, 6), (6, 3), (7, 3), (1, 6), (0, 7), (5, 3), (2, 6), (1, 7), (3, 5), (2, 7), (4, 4)),
    "end3": ((3, 6), (6, 4), (7, 4), (3, 7), (4, 5), (5, 4), (6, 5), (7, 5), (4, 6), (5, 5), (6, 6)),
    "end4": ((4, 7), (7, 6), (6, 7), (5, 6), (7, 7), (5, 7)),
}
HALF = 256
STAGES = 8


def dot(a, b):
    return jnp.dot(a, b, preferred_element_type=F32)


def dot_rt(a, b):
    return lax.dot_general(a, b, (((1,), (1,)), ((), ())), preferred_element_type=F32)


def dot_lt(a, b):
    return lax.dot_general(a, b, (((0,), (0,)), ((), ())), preferred_element_type=F32)


def stats(x):
    center = x - jnp.mean(x, axis=-1, keepdims=True)
    rstd = lax.rsqrt(jnp.mean(center * center, axis=-1, keepdims=True) + EPS)
    return center * rstd, rstd


def norm_back(x, gain, dy):
    xhat, rstd = stats(x)
    dxh = dy * gain
    dx = rstd * (
        dxh
        - jnp.mean(dxh, axis=-1, keepdims=True)
        - xhat * jnp.mean(dxh * xhat, axis=-1, keepdims=True)
    )
    dgain = jnp.sum(dy * xhat, axis=0, keepdims=True)
    dshift = jnp.sum(dy, axis=0, keepdims=True)
    return dx, dgain, dshift


def layer_kernel(
    nb,
    fused,
    cells_h,
    cot_h,
    missing,
    context,
    *rest,
):
    vectors, rest = rest[:9], rest[9:]
    (
    wfqkv_h,
    wfout_h,
    wrqkv_h,
    wrout_h,
    wfin_h,
    wfdn_h,
    act_h,
    igrad_h,
    gfqkv_h,
    gfout_h,
    grqkv_h,
    grout_h,
    gfin_h,
    gfdn_h,
    gvec,
    n1_h,
    fqkv_h,
    fp_h,
    fo_h,
    cot,
    wrqkv,
    wrout,
    wfin,
    wfdn,
    wkvt,
    absent,
    af,
    n2,
    rss,
    rsr,
    g2,
    hid,
    gin,
    nro,
    gy2,
    dkv,
    dq,
    ctxa,
    act,
    dn2,
    gb,
    vland,
    vec,
    load_sem,
    feat_sem,
    stash_sem,
    out_sem,
    ctx_send,
    ctx_recv,
    ag_send,
    ag_recv,
    rs_send,
    rs_recv,
    ar_send,
    ar_recv,
    vec_send,
    vec_recv,
    ready,
    free,
    ) = rest
    cols, rows, width = g2.shape
    seg = width
    ff_blocks = wfin.shape[1] // seg
    quarter = rows // CHUNK
    ro_at = cols
    t = lax.axis_index("tab")
    z = lax.axis_index("blk")
    core, xbit, ybit = lax.rem(t, 2), lax.rem(lax.div(t, 2), 2), lax.rem(lax.div(t, 4), 2)
    on_core = (t + 1 - 2 * core, z)
    on_x = (t + 2 - 4 * xbit, z)
    on_y = (t + 4 - 8 * ybit, z)
    along = [(t, lax.rem(z + d, nb)) for d in range(1, nb)]
    partners = along + ([on_core, on_x, on_y] if fused else [])

    def load_all(pairs, sem):
        copies = [
            pltpu.make_async_copy(a, b, sem.at[i]) for i, (a, b) in enumerate(pairs)
        ]
        for copy in copies:
            copy.start()
        return copies

    def signal_all(sem):
        for device in partners:
            pl.semaphore_signal(sem, inc=1, device_id=device, device_id_type=MESH)

    def await_all(sem):
        pl.semaphore_wait(sem, len(partners))

    def remote(source, dest, send, recv, device):
        return pltpu.make_async_remote_copy(
            src_ref=source,
            dst_ref=dest,
            send_sem=send,
            recv_sem=recv,
            device_id=device,
            device_id_type=MESH,
        )

    def block(c, s):
        return n2.at[c * (nb // 2) + s // 2, pl.ds(pl.multiple_of((s % 2) * rows, rows), rows)]

    own_hi, own_lo = lax.div(z, 2), pl.multiple_of(lax.rem(z, 2) * rows, rows)

    def own_block(c):
        return n2.at[c * (nb // 2) + own_hi, pl.ds(own_lo, rows)]

    def on_each(run, devices=None):
        for me in range(nb) if devices is None else devices:

            @pl.when(z == me)
            def _():
                run(me)

    ends, middle = (0, nb - 1), tuple(range(1, nb - 1))

    def pass_on(c, s, me, step):
        return remote(
            block(c, s),
            block(c, s),
            ag_send.at[c, s, (step + 1) // 2],
            ag_recv.at[c, s],
            (t, me + step),
        )

    def await_block(c, s):
        pltpu.make_async_copy(block(c, s), block(c, s), ag_recv.at[c, s]).wait()

    def gather_sends(c, me, far):
        out = []
        for step in (-1, 1):
            if 0 <= me + step < nb and 0 <= me - far * step < nb:
                out.append((me - far * step, pass_on(c, me - far * step, me, step)))
        return out

    def start_gather(c, devices=None):
        def run(me):
            for _, copy in gather_sends(c, me, 0):
                copy.start()

        on_each(run, devices)

    def hop(c, far):
        def run(me):
            for s, copy in gather_sends(c, me, far):
                await_block(c, s)
                copy.start()

        on_each(run, middle)

    def await_gather(c):
        def run(me):
            for s in range(nb):
                if s != me:
                    await_block(c, s)

        on_each(run, ends)

    def await_gather_sends(c):
        def run(me):
            for far in range(nb - 1):
                for _, copy in gather_sends(c, me, far):
                    copy.wait_send()

        on_each(run)

    def slot_of(owner, me):
        return nb if owner == me else owner

    def rs_copy(c, owner, me):
        step = 1 if owner > me else -1
        there = owner if step < 0 else slot_of(owner, me + step)
        return remote(
            rss.at[c, owner],
            rsr.at[c, there],
            rs_send.at[c, owner],
            rs_recv.at[c, there],
            (t, me + step),
        )

    def scatter(c, part):
        def run(me):
            order = sorted((o for o in range(nb) if o != me), key=lambda o: -abs(o - me))
            if part > 0:
                rs_copy(c, order[part - 1], me).wait_send()
            rs_copy(c, order[part], me).start()

        on_each(run, ends)

    def await_slot(c, s):
        pltpu.make_async_copy(rsr.at[c, s], rsr.at[c, s], rs_recv.at[c, s]).wait()

    def combine(c, part):
        def run(me):
            low = me == 1
            owner = (nb - 1, nb - 2, 0)[part] if low else (0, 1, nb - 1)[part]
            await_slot(c, owner)
            rss[c, owner] = (rss[c, owner].astype(F32) + rsr[c, owner].astype(F32)).astype(BF16)
            rs_copy(c, owner, me).start()

        on_each(run, middle)

    def own_slots(me):
        return [] if me == nb - 1 else [me], [] if me == 0 else [nb]

    def await_scatter_sends(c):
        def run(me):
            for owner in range(nb):
                if owner != me and (me in middle or abs(owner - me) == 1):
                    rs_copy(c, owner, me).wait_send()

        on_each(run)

    groups = []
    for members in GROUPS:
        first, count = members[0], len(members)
        if first < 4:
            land = rss.at[0, pl.ds(first, count)]
        else:
            land = hid.at[pl.ds(first - 4, count)]
        array, place = (gb, first) if first < 12 else (n2, first - 12)
        groups.append((array, place, count, first, land))

    reached = [0] * len(GROUPS)
    started = set()

    def pump(point):
        for g, stage in PUMPS.get(point, ()):
            next_sum(g, stage)

    lanes_a, lanes_b = pl.ds(0, HALF), pl.ds(HALF, HALF)

    def at16(v):
        return pl.multiple_of(v, 16)

    row_core = core * 256
    paths = [(lanes_a, xbit, ybit, on_x, on_y), (lanes_b, ybit, xbit, on_y, on_x)]

    def landing(g, stage):
        _, _, n, first, land = groups[g]
        if stage == 0:
            return land
        if stage == 1:
            return wfdn.at[pl.ds(first, n)]
        return gin.at[pl.ds(first + (16 if stage == 3 else 0), n)]

    def sum_copies(g, stage):
        ref, place, n, _, _ = groups[g]
        whole = pl.ds(0, width)

        def final(row, count, lanes):
            return ref.at[pl.ds(place, n), pl.ds(at16(row), count), lanes]

        out = []
        if stage == 0:
            out.append((final((1 - core) * 256, 256, whole), landing(g, 0), on_core))
        elif stage == 1:
            for lanes, bit, _, device, _ in paths:
                away = landing(g, 0).at[:, pl.ds(at16((1 - bit) * 128), 128), lanes]
                out.append((away, landing(g, 1).at[:, :, lanes], device))
        elif stage == 2:
            for lanes, _, bit, _, device in paths:
                away = landing(g, 1).at[:, pl.ds(at16((1 - bit) * 64), 64), lanes]
                out.append((away, landing(g, 2).at[:, :, lanes], device))
        elif stage == 3:
            for d in range(1, nb):
                away = landing(g, 2).at[:, pl.ds(at16(lax.rem(z + d, nb) * 16), 16), :]
                out.append((away, landing(g, 3).at[:, pl.ds((d - 1) * 16, 16), :], along[d - 1]))
        elif stage == 4:
            for d in range(1, nb):
                for lanes, bit1, bit2, _, _ in paths:
                    row = row_core + bit1 * 128 + bit2 * 64 + z * 16
                    mine = landing(g, 3).at[:, pl.ds(0, 16), lanes]
                    out.append((mine, final(row, 16, lanes), along[d - 1]))
        elif stage == 5:
            for lanes, bit1, bit2, _, device in paths:
                mine = final(row_core + bit1 * 128 + bit2 * 64, 64, lanes)
                out.append((mine, mine, device))
        elif stage == 6:
            for lanes, bit1, _, device, _ in paths:
                mine = final(row_core + bit1 * 128, 128, lanes)
                out.append((mine, mine, device))
        else:
            mine = final(row_core, 256, whole)
            out.append((mine, mine, on_core))
        first = (0, 1, 3, 5, 8, 14, 16, 18)[stage]
        return [
            remote(a, b, ar_send.at[g, first + i], ar_recv.at[g, first + i], device)
            for i, (a, b, device) in enumerate(out)
        ]

    def start_stage(g, stage):
        if stage == STAGES - 1:
            pl.semaphore_wait(free.at[g], 1)
        for copy in sum_copies(g, stage):
            copy.start()

    def start_sum(*done):
        if not fused:
            return
        for group, members in enumerate(GROUPS):
            if any(b in done for b in members):
                started.update(b for b in done if b in members)
                if started.issuperset(members):
                    start_stage(group, 0)

    def add_landed(g, stage):
        ref, place, n, _, _ = groups[g]
        land = landing(g, stage)
        if stage == 0:
            for i in range(n):
                mine = ref[place + i, pl.ds(at16(row_core), 256), :]
                land[i] = (mine.astype(F32) + land[i].astype(F32)).astype(BF16)
            return
        last = landing(g, stage - 1)
        if stage == 3:
            total = last[:, pl.ds(at16(z * 16), 16), :].astype(F32)
            for d in range(1, nb):
                total = total + land[:, pl.ds((d - 1) * 16, 16), :].astype(F32)
            total = total.astype(BF16)
            land[:, pl.ds(0, 16), :] = total
            for i, (lanes, bit1, bit2, _, _) in enumerate(paths):
                row = at16(row_core + bit1 * 128 + bit2 * 64 + z * 16)
                ref[pl.ds(place, n), pl.ds(row, 16), lanes] = total[
                    :, :, i * HALF : (i + 1) * HALF
                ]
            return
        count = 128 if stage == 1 else 64
        for lanes, bit1, bit2, _, _ in paths:
            row = at16((bit1 if stage == 1 else bit2) * count)
            mine = last[:, pl.ds(row, count), lanes]
            land[:, :, lanes] = (mine.astype(F32) + land[:, :, lanes].astype(F32)).astype(BF16)

    def next_sum(g, stage):
        if not fused:
            return
        assert reached[g] == stage
        reached[g] += 1
        if stage == 1 and not any(later > 1 for later in reached[:g] + reached[g + 1 :]):
            await_all(ready.at[2])
        copies = sum_copies(g, stage)
        for copy in copies:
            copy.wait_recv()
        if stage < 4:
            add_landed(g, stage)
        if stage + 1 < STAGES:
            start_stage(g, stage + 1)
        else:
            for b in GROUPS[g]:
                start_out(b)
        if stage == 0:
            for copy in copies:
                copy.wait_send()
            pl.semaphore_signal(free.at[g], inc=1, device_id=on_core, device_id_type=MESH)

    def out_copies(g):
        if g < 4:
            dest = gfdn_h.at[pl.ds(g * seg, seg)]
        elif g in (8, 12):
            dest = grout_h if g == 8 else gfout_h
        else:
            dest = gfin_h if g < 8 else grqkv_h if g < 12 else gfqkv_h
            part = g - 4 if g < 8 else g - 9 if g < 12 else (2, 0, 1)[g - 13]
            dest = dest.at[:, pl.ds(part * seg, seg)]
        ref, place = (gb, g) if g < 12 else (n2, g - 12)
        return [pltpu.make_async_copy(ref.at[place], dest, out_sem.at[g])]

    def start_out(g):
        for copy in out_copies(g):
            copy.start()

    barrier = pltpu.get_barrier_semaphore()
    signal_all(barrier)
    marks = jnp.concatenate(
        [missing[:, 0, :].astype(F32), jnp.zeros((8 - cols, rows), F32)], axis=0
    ).T
    for c in range(cols):
        absent[c] = marks[:, c : c + 1]
    ctxa[z] = jnp.broadcast_to(context[...].astype(F32), (HEAD, rows)).T.astype(BF16)
    gvec[...] = jnp.zeros_like(gvec)

    for i, vector in enumerate(vectors):
        count = vector.shape[0] // width
        vec[i : i + count, :] = vector[...].astype(F32).reshape(count, width)

    def row(i):
        return vec[i : i + 1, :]

    ones = (
        lax.broadcasted_iota(jnp.int32, (width, HEAD), 0) // HEAD
        == lax.broadcasted_iota(jnp.int32, (width, HEAD), 1)
    ).astype(BF16)
    ones_t = (
        lax.broadcasted_iota(jnp.int32, (HEAD, width), 1) // HEAD
        == lax.broadcasted_iota(jnp.int32, (HEAD, width), 0)
    ).astype(BF16)

    def base_of(cells, c, r):
        return jnp.where(
            absent[c, pl.ds(r, CHUNK), :] > 0, row(EMBED), cells[c, pl.ds(r, CHUNK), :].astype(F32)
        )

    ctx_copies = [
        remote(ctxa.at[z], ctxa.at[z], ctx_send.at[d], ctx_recv.at[z], along[d])
        for d in range(nb - 1)
    ]

    weights = [(wrqkv_h, wrqkv), (wrout_h, wrout), (wfin_h, wfin), (wfdn_h, wfdn), (cot_h, cot)]
    loads = [
        pltpu.make_async_copy(a, b, load_sem.at[i]) for i, (a, b) in enumerate(weights)
    ]

    def feature_forward(cells, wfqkv, wfout, n1, fqkv, fp, fo, hi, lo, spread):
        feat_loads = load_all(
            [(cells_h, cells), (wfqkv_h, wfqkv), (wfout_h, wfout)], feat_sem
        )
        for copy in loads:
            copy.start()
        feat_loads[0].wait()
        for c in range(cols):
            for r in range(0, rows, CHUNK):
                xhat, _ = stats(base_of(cells, c, r))
                n1[c, pl.ds(r, CHUNK), :] = (xhat * row(GAIN1) + row(SHIFT1)).astype(BF16)
        await_all(barrier)
        for copy in ctx_copies:
            copy.start()
        feat_loads[1].wait()
        n1_all = n1[...].reshape(cols * rows, width)
        for b in range(3):
            fqkv[b] = (
                dot(n1_all, wfqkv[:, b * seg : (b + 1) * seg])
                .astype(BF16)
                .reshape(cols, rows, width)
            )
        stash = [(n1, n1_h), (fqkv, fqkv_h)]
        for i in range(cols):
            for j in range(cols):
                for r in range(0, rows, CHUNK):
                    prod = fqkv[0, i, pl.ds(r, CHUNK), :].astype(F32) * fqkv[
                        1, j, pl.ds(r, CHUNK), :
                    ].astype(F32)
                    top = prod.astype(BF16)
                    hi[pl.ds(j * rows + r, CHUNK), :] = top
                    lo[pl.ds(j * rows + r, CHUNK), :] = (prod - top.astype(F32)).astype(BF16)
            scores = (dot(hi[...], ones) + dot(lo[...], ones)) * SCALE
            parts = [scores[j * rows : (j + 1) * rows] for j in range(cols)]
            top = functools.reduce(jnp.maximum, parts)
            parts = [jnp.exp(part - top) for part in parts]
            inv = 1.0 / functools.reduce(jnp.add, parts)
            for j in range(cols):
                fp[i, j] = parts[j] * inv
            spread[...] = dot(fp[i].reshape(cols * rows, HEAD).astype(BF16), ones_t)
            weigh(spread, fqkv, 2, fo, None, i, 1.0)
            if i == 0:
                feat_loads[2].wait()
            spread[0:rows, :] = dot(fo[i], wfout[...])
            for r in range(0, rows, CHUNK):
                after = base_of(cells, i, r) + spread[pl.ds(r, CHUNK), :]
                af[i, pl.ds(r, CHUNK), :] = after
                xhat, _ = stats(after)
                n2[i * (nb // 2) + own_hi, pl.ds(pl.multiple_of(own_lo + r, CHUNK), CHUNK), :] = (
                    xhat * row(GAIN2) + row(SHIFT2)
                ).astype(BF16)
            if i == 0:
                start_gather(0)
        for copy in load_all(stash + [(fp, fp_h), (fo, fo_h)], stash_sem):
            copy.wait()

    def weigh(spread, source, part, dest, dest_part, i, scale):
        for r in range(0, rows, CHUNK):
            rr = pl.ds(r, CHUNK)
            total = functools.reduce(
                jnp.add,
                [
                    spread[pl.ds(j * rows + r, CHUNK), :]
                    * (source[j, rr, :] if part is None else source[part, j, rr, :]).astype(F32)
                    for j in range(cols)
                ],
            )
            total = (total * scale).astype(BF16)
            if dest_part is None:
                dest[i, rr, :] = total
            else:
                dest[dest_part, i, rr, :] = total

    token = (cols, rows, width)
    vm = pltpu.VMEM
    feature_scratch = [
        vm(token, BF16),
        vm(wfqkv_h.shape, BF16),
        vm(wfout_h.shape, BF16),
        vm(token, BF16),
        vm((3,) + token, BF16),
        vm((cols, cols, rows, HEAD), F32),
        vm(token, BF16),
        vm((cols * rows, width), BF16),
        vm((cols * rows, width), BF16),
        vm((cols * rows, width), F32),
    ]
    pl.run_scoped(feature_forward, *feature_scratch)
    hop(0, 1)

    loads[0].wait()
    for b in range(2):
        wkvt[b] = wrqkv[:, (b + 1) * seg : (b + 2) * seg].astype(F32).T.astype(BF16)
    for load in loads[1:]:
        load.wait()
    for s in range(nb):

        @pl.when(z != s)
        def _():
            pltpu.make_async_copy(ctxa.at[s], ctxa.at[s], ctx_recv.at[s]).wait()

    hop(0, 2)
    start_gather(1)

    def ff_weight(f):
        return wfdn[pl.ds(f * (seg // 128), seg // 128)].reshape(seg, width)

    def gin_block(c, f):
        return pl.ds((c * ff_blocks + f) * quarter, quarter)

    def ff_out_weights():
        await_scatter_sends(0)
        if fused:
            signal_all(ready.at[0])
        cot_all = cot[...].reshape(cols * rows, width)
        for f in range(ff_blocks):
            hid_all = jnp.concatenate([hid[c * ff_blocks + f] for c in range(cols)], axis=0)
            gb[f] = dot_lt(hid_all, cot_all).astype(BF16)
            if fused and f == 0:
                await_all(ready.at[0])
            start_sum(f)
        if fused:
            signal_all(ready.at[1])
        pump("ff_out")

    def ff_in_weights():
        if fused:
            await_all(ready.at[1])
        n3_all = nro[0:cols].reshape(cols * rows, width)
        for f in range(ff_blocks):
            gin_all = jnp.concatenate(
                [gin[gin_block(c, f)].reshape(rows, seg) for c in range(cols)], axis=0
            )
            gb[ff_blocks + f] = dot_lt(n3_all, gin_all).astype(BF16)
            start_sum(4 + f)
        pump("ff_in")
        gb[8] = dot_lt(
            nro[ro_at : ro_at + cols].reshape(cols * rows, width),
            gy2[...].reshape(cols * rows, width),
        ).astype(BF16)
        if fused:
            signal_all(ready.at[2])
        start_sum(8)
        pump("row_out")

    def columns_stage(q, kv, kvt, gro, p, scores, dsb, ot, rof, dgel, ar):
        def wide(ref, value):
            for h in range(HEADS):
                ref[:, h * 2 * HEAD : h * 2 * HEAD + HEAD] = value[:, h * HEAD : (h + 1) * HEAD]

        def extra(ref, rr, value):
            for h in range(HEADS):
                ref[rr, h * 2 * HEAD + HEAD : (h + 1) * 2 * HEAD] = value

        def lanes_of(count):
            return lax.broadcasted_iota(jnp.int32, (count, HEAD), 1)

        first = lanes_of(rows) == 0
        extra(q, slice(None), first.astype(BF16))
        for s in range(nb):
            rr = slice(s * rows, (s + 1) * rows)
            mask = jnp.where(first, (ctxa[s].astype(F32) - 1.0) * 1e30, 0.0)
            extra(kv.at[0], rr, mask.astype(BF16))
            extra(kv.at[1], rr, (lanes_of(rows) < 2).astype(BF16))
        keys_in = nb * rows
        step = 2 * CHUNK

        def fold(part, op):
            return op(part.reshape(step // 8, 8, part.shape[-1]), axis=0)

        exponent = SCALE * math.log2(math.e)

        def act_copy(c):
            return pltpu.make_async_copy(act, act_h.at[c], stash_sem.at[c])

        def on_last(c, point):
            if fused and PUMPS.get(point):

                @pl.when(c == cols - 1)
                def _():
                    pump(point)

        def column(c, _):
            await_gather(c)
            x = n2[pl.ds(c * (nb // 2), nb // 2)].reshape(nb * rows, width)
            own = n2[c * (nb // 2) + own_hi, pl.ds(own_lo, rows), :]
            wide(q, dot(own, wrqkv[:, 0:seg]).astype(BF16))
            wide(kv.at[0], dot(x, wrqkv[:, seg : 2 * seg]).astype(BF16))
            kvt[1] = dot_rt(wkvt[1], x).astype(BF16)
            for h in range(HEADS):
                hs = slice(h * HEAD, (h + 1) * HEAD)
                hw = slice(h * 2 * HEAD, (h + 1) * 2 * HEAD)
                sh = scores.at[h % 2]
                sh[...] = dot_rt(kv[0, :, hw], q[:, hw])
                top = functools.reduce(
                    jnp.maximum,
                    [fold(sh[r : r + step, :], jnp.max) for r in range(0, keys_in, step)],
                )
                top = jnp.max(top, axis=0, keepdims=True) * exponent
                total = jnp.zeros((8, rows), F32)
                for r in range(0, keys_in, step):
                    e = jnp.exp2(sh[r : r + step, :] * exponent - top)
                    sh[r : r + step, :] = e
                    total = total + fold(e, jnp.sum)
                inv = 1.0 / jnp.sum(total, axis=0, keepdims=True)
                for r in range(0, keys_in, step):
                    p[h, r : r + step, :] = (sh[r : r + step, :] * inv).astype(BF16)
                ot[hs, :] = dot(kvt[1, hs, :], p[h])
            rof[...] = ot[...].T
            nro[ro_at + c] = rof[...].astype(BF16)

            @pl.when(c + 1 < cols)
            def _():
                hop(c + 1, 1)

            @pl.when(c > 0)
            def _():
                scatter(c - 1, 1)

            ar[...] = dot(nro[ro_at + c], wrout[...])
            for r in range(0, rows, CHUNK):
                rr = pl.ds(r, CHUNK)
                after = af[c, rr, :] + ar[rr, :]
                ar[rr, :] = after
                xhat, _ = stats(after)
                nro[c, rr, :] = (xhat * row(GAIN3) + row(SHIFT3)).astype(BF16)
            for f in range(ff_blocks):
                fs = slice(f * seg, (f + 1) * seg)
                dgel[f] = dot(nro[c], wfin[:, fs])
                for r in range(0, rows, CHUNK // 2):
                    rr = pl.ds(r, CHUNK // 2)
                    u = dgel[f, rr, :] + row(IN_BIAS + f)
                    c0 = math.sqrt(2.0 / math.pi)
                    c1 = c0 * 0.044715
                    sq = u * u
                    half = 0.5 + 0.5 * jnp.tanh(u * (c0 + c1 * sq))
                    out = u * half
                    hid[c * ff_blocks + f, rr, :] = out.astype(BF16)
                    dgel[f, rr, :] = half + out * (1.0 - half) * (2.0 * c0 + (6.0 * c1) * sq)
            total = ar[...] + row(OUT_BIAS)
            for f in range(ff_blocks):
                total = total + dot(hid[c * ff_blocks + f], ff_weight(f))

            @pl.when(c > 0)
            def _():
                act_copy(c - 1).wait()

            act[...] = total.astype(BF16)

            @pl.when(c >= 0)
            def _():
                act_copy(c).start()


            back = jnp.zeros((rows, width), F32)
            for f in range(ff_blocks):
                fs = slice(f * seg, (f + 1) * seg)
                gi = (dot_rt(cot[c], ff_weight(f)) * dgel[f]).astype(BF16)
                gin[gin_block(c, f)] = gi.reshape(quarter, CHUNK, seg)
                gvec[IN_BIAS + f : IN_BIAS + f + 1, :] += jnp.sum(
                    gi.astype(F32), axis=0, keepdims=True
                )
                back = back + dot_rt(gi, wfin[:, fs])
            dgel[0] = back
            for r in range(0, rows, CHUNK):
                rr = pl.ds(r, CHUNK)
                dx, dgain, dshift = norm_back(ar[rr, :], row(GAIN3), dgel[0, rr, :])
                g3 = cot[c, rr, :].astype(F32)
                g = g3 + dx
                g2[c, rr, :] = g
                gy2[c, rr, :] = g.astype(BF16)
                gvec[GAIN3 : GAIN3 + 1, :] += dgain
                gvec[SHIFT3 : SHIFT3 + 1, :] += dshift
                gvec[OUT_BIAS : OUT_BIAS + 1, :] += jnp.sum(g3, axis=0, keepdims=True)


            @pl.when(c + 1 < cols)
            def _():
                hop(c + 1, 2)

            @pl.when(c + 2 < cols)
            def _():
                start_gather(c + 2)

            @pl.when(c == cols - 1)
            def _():
                ff_out_weights()

            @pl.when(c > 0)
            def _():
                scatter(c - 1, 2)

            wide(gro, dot_rt(gy2[c], wrout[...]).astype(BF16))
            for h in range(HEADS):
                hs = slice(h * HEAD, (h + 1) * HEAD)
                mean = jnp.sum(
                    rof[:, hs] * gro[:, h * 2 * HEAD : h * 2 * HEAD + HEAD].astype(F32),
                    axis=1,
                    keepdims=True,
                )
                high = mean.astype(BF16).astype(F32)
                gro[:, h * 2 * HEAD + HEAD : (h + 1) * 2 * HEAD] = jnp.where(
                    first, -high, jnp.where(lanes_of(rows) == 1, high - mean, 0.0)
                ).astype(BF16)
            wide(kv.at[1], dot(x, wrqkv[:, 2 * seg : 3 * seg]).astype(BF16))
            kvt[0] = dot_rt(wkvt[0], x).astype(BF16)
            on_last(c, "values_again")
            table = pl.ds(pl.multiple_of(c * nb * rows, nb * rows), nb * rows)
            for h in range(HEADS):
                hs = slice(h * HEAD, (h + 1) * HEAD)
                hw = slice(h * 2 * HEAD, (h + 1) * 2 * HEAD)
                hn = slice(h * 2 * HEAD, h * 2 * HEAD + HEAD)
                vs = slice(width + h * HEAD, width + (h + 1) * HEAD)
                sh, dh = scores.at[h % 2], dsb.at[h % 2]
                sh[...] = dot_rt(kv[1, :, hw], gro[:, hw])
                for r in range(0, keys_in, step):
                    dh[r : r + step, :] = (
                        p[h, r : r + step, :].astype(F32) * sh[r : r + step, :]
                    ).astype(BF16)
                dkv[table, hs] = (dot(dh[...], q[:, hn]) * SCALE).astype(BF16)
                dkv[table, vs] = dot(p[h], gro[:, hn]).astype(BF16)
                ot[hs, :] = dot(kvt[0, hs, :], dh[...])
                on_last(c, f"head{h}")
            dq[c] = (ot[...].T * SCALE).astype(BF16)

            @pl.when(c > 0)
            def _():
                combine(c - 1, 0)


            for o in range(nb):
                part = pl.ds(pl.multiple_of((c * nb + o) * rows, rows), rows)
                rss[c, o] = dot_rt(dkv[part, :], wrqkv[:, seg : 3 * seg]).astype(BF16)
            scatter(c, 0)

            on_last(c, "scatter")
            @pl.when(c == cols - 1)
            def _():
                ff_in_weights()

            dn2[c] = dot_rt(dq[c], wrqkv[:, 0:seg]) + rss[c, z].astype(F32)

            @pl.when(c > 0)
            def _():
                combine(c - 1, 1)
                combine(c - 1, 2)

            return 0

        lax.fori_loop(0, cols, column, 0)
        act_copy(cols - 1).wait()

    pl.run_scoped(
        columns_stage,
        vm((rows, 2 * width), BF16),
        vm((2, nb * rows, 2 * width), BF16),
        vm((2, width, nb * rows), BF16),
        vm((rows, 2 * width), BF16),
        vm((HEADS, nb * rows, rows), BF16),
        vm((2, nb * rows, rows), F32),
        vm((2, nb * rows, rows), BF16),
        vm((width, rows), F32),
        vm((rows, width), F32),
        vm((ff_blocks, rows, width), F32),
        vm((rows, width), F32),
    )

    def feature_backward(
        cells, wfqkv, wfout, n1, fqkv, fp, fo, hi, lo, spread, gfo, dqkv, dsl, more
    ):
        again = load_all(
            [
                (cells_h, cells),
                (wfqkv_h, wfqkv),
                (wfout_h, wfout),
                (n1_h, n1),
                (fqkv_h, fqkv),
                (fp_h, fp),
                (fo_h, fo),
            ],
            feat_sem,
        )
        pump("columns")
        x_all = n2[...].reshape(cols * nb * rows, width)
        half = width // 2
        for i in range(2):
            at = slice(i * half, (i + 1) * half)
            got = dot_lt(x_all[:, at], dkv[...]).astype(BF16)
            gb[10, at, :] = got[:, 0:seg]
            gb[11, at, :] = got[:, seg:]
            if i == 1:
                start_sum(10, 11)
            if i == 0:
                scatter(cols - 1, 1)
                combine(cols - 1, 0)
            pump(f"row_kv{i}")
        own = jnp.concatenate(
            [n2[c * (nb // 2) + own_hi, pl.ds(own_lo, rows), :] for c in range(cols)], axis=0
        )
        gb[9] = dot_lt(own, dq[...].reshape(cols * rows, width)).astype(BF16)
        start_sum(9)
        pump("row_q")
        for copy in again:
            copy.wait()
        for c in range(cols):
            await_gather_sends(c)

        def column_back(c):
            def arrived(me):
                above, below = own_slots(me)
                for s in above + below:
                    await_slot(c, s)
                    dn2[c] += rsr[c, s].astype(F32)

            on_each(arrived)
            for r in range(0, rows, CHUNK):
                rr = pl.ds(r, CHUNK)
                dy = dn2[c, rr, :]
                dx, dgain, dshift = norm_back(af[c, rr, :], row(GAIN2), dy)
                g = g2[c, rr, :] + dx
                g2[c, rr, :] = g
                gy2[c, rr, :] = g.astype(BF16)
                gvec[GAIN2 : GAIN2 + 1, :] += dgain
                gvec[SHIFT2 : SHIFT2 + 1, :] += dshift
            gfo[c] = dot_rt(gy2[c], wfout[...]).astype(BF16)
            for j in range(cols):
                for r in range(0, rows, CHUNK):
                    prod = gfo[c, pl.ds(r, CHUNK), :].astype(F32) * fqkv[
                        2, j, pl.ds(r, CHUNK), :
                    ].astype(F32)
                    top = prod.astype(BF16)
                    hi[pl.ds(j * rows + r, CHUNK), :] = top
                    lo[pl.ds(j * rows + r, CHUNK), :] = (prod - top.astype(F32)).astype(BF16)
            dp = dot(hi[...], ones) + dot(lo[...], ones)
            parts = [dp[j * rows : (j + 1) * rows] for j in range(cols)]
            mean = functools.reduce(jnp.add, [fp[c, j] * parts[j] for j in range(cols)])
            for j in range(cols):
                dsl[c, j] = (fp[c, j] * (parts[j] - mean)).astype(BF16)
            spread[...] = dot(dsl[c].reshape(cols * rows, HEAD), ones_t)
            weigh(spread, fqkv, 1, dqkv, 0, c, SCALE)

        def earlier(terms, source, part, sums):
            for j in range(cols):
                spread[0 : (cols - 1) * rows, :] = dot(
                    jnp.concatenate([terms[i, j].astype(BF16) for i in range(cols - 1)], axis=0),
                    ones_t,
                )
                for r in range(0, rows, CHUNK):
                    rr = pl.ds(r, CHUNK)
                    sums[j][rr, :] = functools.reduce(
                        jnp.add,
                        [
                            spread[pl.ds(i * rows + r, CHUNK), :]
                            * (source[i, rr, :] if part is None else source[part, i, rr, :]).astype(
                                F32
                            )
                            for i in range(cols - 1)
                        ],
                    )

        def finish(source, part, sums, dest_part, scale):
            last = cols - 1
            for j in range(cols):
                for r in range(0, rows, CHUNK):
                    rr = pl.ds(r, CHUNK)
                    mine = source[last, rr, :] if part is None else source[part, last, rr, :]
                    total = sums[j][rr, :] + spread[pl.ds(j * rows + r, CHUNK), :] * mine.astype(F32)
                    dqkv[dest_part, j, rr, :] = (total * scale).astype(BF16)

        n1_flat = n1[...].reshape(cols * rows, width)

        def part_done(b):
            at = (1, 2, 0)[b]
            n2[1 + at] = dot_lt(n1_flat, dqkv[b].reshape(cols * rows, width)).astype(BF16)
            start_sum(13 + at)

        sums_k = [af.at[0], af.at[1], more.at[0]]
        sums_v = [dn2.at[0], dn2.at[1], more.at[1]]
        column_back(0)
        scatter(cols - 1, 2)
        combine(cols - 1, 1)
        pump("norm2_0")
        for c in range(1, cols - 1):
            column_back(c)
        combine(cols - 1, 2)
        pump("norm2_1")
        earlier(dsl, fqkv, 0, sums_k)
        pump("earlier")
        earlier(fp, gfo, None, sums_v)
        pump("window")
        column_back(cols - 1)
        pump("norm2_2")
        finish(fqkv, 0, sums_k, 1, SCALE)
        part_done(0)
        part_done(1)
        pump("keys")
        spread[...] = dot(fp[cols - 1].reshape(cols * rows, HEAD).astype(BF16), ones_t)
        finish(gfo, None, sums_v, 2, 1.0)
        n2[0] = dot_lt(
            fo[...].reshape(cols * rows, width), gy2[...].reshape(cols * rows, width)
        ).astype(BF16)
        start_sum(12)
        part_done(2)
        pump("values")
        spread[...] = functools.reduce(
            jnp.add,
            [
                dot_rt(dqkv[b].reshape(cols * rows, width), wfqkv[:, b * seg : (b + 1) * seg])
                for b in range(3)
            ],
        )
        pump("normed1")
        for c in range(cols):
            for r in range(0, rows, CHUNK):
                rr = pl.ds(r, CHUNK)
                dx, dgain, dshift = norm_back(
                    base_of(cells, c, r), row(GAIN1), spread[pl.ds(c * rows + r, CHUNK), :]
                )
                g = g2[c, rr, :] + dx
                gone = absent[c, rr, :] > 0
                g2[c, rr, :] = jnp.where(gone, 0.0, g)
                gvec[GAIN1 : GAIN1 + 1, :] += dgain
                gvec[SHIFT1 : SHIFT1 + 1, :] += dshift
                gvec[EMBED : EMBED + 1, :] += jnp.sum(
                    jnp.where(gone, g, 0.0), axis=0, keepdims=True
                )
            pump(f"norm1_{c}")

    pl.run_scoped(
        feature_backward,
        *feature_scratch,
        vm(token, BF16),
        vm((3,) + token, BF16),
        vm((cols, cols, rows, HEAD), BF16),
        vm((2, rows, width), F32),
    )
    igrad_copy = pltpu.make_async_copy(g2, igrad_h, stash_sem.at[cols])
    igrad_copy.start()

    vec_copies = []

    def vec_step(k, devices):
        copies = [
            remote(
                vland.at[k],
                vland.at[4 + k + i],
                vec_send.at[k + i],
                vec_recv.at[k + i],
                device,
            )
            for i, device in enumerate(devices)
        ]
        vland[k] = gvec[...]
        for copy in copies:
            copy.start()
        vec_copies.extend(copies)
        return copies

    def vec_add(copies, k):
        for copy in copies:
            copy.wait_recv()
        if len(copies) == 1:
            gvec[...] = gvec[...] + vland[4 + k]
        else:
            vland[4 + k + nb - 1] = gvec[...]
            total = jnp.zeros_like(gvec)
            for s in range(nb):
                total = total + vland[4 + k + lax.rem(z + nb - s + nb - 1, nb)]
            gvec[...] = total

    if fused:
        step = vec_step(0, [on_core])
        pump("end0")
        vec_add(step, 0)
        step = vec_step(1, [on_x])
        pump("end1")
        vec_add(step, 1)
        step = vec_step(2, [on_y])
        pump("end2")
        vec_add(step, 2)
        step = vec_step(3, along)
        pump("end3")
        vec_add(step, 3)
        pump("end4")
        assert all(stage == STAGES for stage in reached)
    else:
        for g in range(16):
            start_out(g)

    for c in range(cols):
        if c > 0:
            await_scatter_sends(c)

    for copy in ctx_copies + vec_copies:
        copy.wait_send()
    if fused:
        for g in range(len(groups)):
            for stage in range(1, STAGES):
                for copy in sum_copies(g, stage):
                    copy.wait_send()
    igrad_copy.wait()
    for g in range(16):
        for copy in out_copies(g):
            copy.wait()


def finish_kernel(*refs):
    ins, gvec, outs, vectors = refs[0:8], refs[8], refs[9:17], refs[17:26]
    low, high, same = refs[26:32], refs[32:38], refs[38:40]
    in_sem, out_sem = refs[40:]
    width = gvec.shape[1]
    loads = [
        pltpu.make_async_copy(a, b, in_sem.at[i]) for i, (a, b) in enumerate(zip(ins, same + low))
    ]
    stores = [
        pltpu.make_async_copy(a, b, out_sem.at[i])
        for i, (a, b) in enumerate(zip(same + high, outs))
    ]
    for copy in loads:
        copy.start()
    for i, vector in enumerate(vectors):
        count = vector.shape[0] // width
        vector[...] = gvec[i : i + count, :].reshape(vector.shape)
    for load, store in zip(loads[:2], stores[:2]):
        load.wait()
        store.start()
    for source, dest, load, store in zip(low, high, loads[2:], stores[2:]):
        load.wait()

        def convert(i, _):
            at = pl.ds(pl.multiple_of(i * CHUNK, CHUNK), CHUNK)
            dest[at, :] = source[at, :].astype(F32)
            return 0

        lax.fori_loop(0, source.shape[0] // CHUNK, convert, 0)
        store.start()
    for copy in stores:
        copy.wait()


def per_device(
    cells,
    missing,
    context,
    cotangent,
    miss_embed,
    norm1_gain,
    norm1_shift,
    feat_qkv,
    feat_out,
    norm2_gain,
    norm2_shift,
    row_qkv,
    row_out,
    norm3_gain,
    norm3_shift,
    ff_in,
    ff_in_bias,
    ff_out,
    ff_out_bias,
):
    _, rows, cols, width = cells.shape
    nb = lax.axis_size("blk")
    fused = lax.axis_size("tab") == 8
    ff = ff_in.shape[1]
    ff_blocks = ff // width

    cells_t = jnp.transpose(cells[0], (1, 0, 2))
    cot_t = jnp.transpose(cotangent[0], (1, 0, 2))
    any_spec = pl.BlockSpec(memory_space=pl.ANY)
    vmem_spec = pl.BlockSpec(memory_space=pltpu.VMEM)
    token = (cols, rows, width)
    vm = pltpu.VMEM
    dma = pltpu.SemaphoreType.DMA
    shape = jax.ShapeDtypeStruct
    results = pl.pallas_call(
        functools.partial(layer_kernel, nb, fused),
        out_shape=(
            shape(token, BF16),
            shape(token, F32),
            shape(feat_qkv.shape, BF16),
            shape(feat_out.shape, BF16),
            shape(row_qkv.shape, BF16),
            shape(row_out.shape, BF16),
            shape(ff_in.shape, BF16),
            shape(ff_out.shape, BF16),
            shape((16, width), F32),
            shape(token, BF16),
            shape((3,) + token, BF16),
            shape((cols, cols, rows, HEAD), F32),
            shape(token, BF16),
        ),
        in_specs=[any_spec] * 2 + [vmem_spec] * 11 + [any_spec] * 6,
        out_specs=(any_spec,) * 8 + (vmem_spec,) + (any_spec,) * 4,
        scratch_shapes=[
            vm(token, BF16),
            vm(row_qkv.shape, BF16),
            vm(row_out.shape, BF16),
            vm(ff_in.shape, BF16),
            vm((ff // 128, 128, width), BF16),
            vm((2, width, width), BF16),
            vm((cols, rows, 1), F32),
            vm(token, F32),
            vm((cols * nb // 2, 2 * rows, width), BF16),
            vm((cols, nb, rows, width), BF16),
            vm((cols, nb + 1, rows, width), BF16),
            vm(token, F32),
            vm((cols * ff_blocks, rows, width), BF16),
            vm((cols * ff_blocks * rows // CHUNK, CHUNK, width), BF16),
            vm((2 * cols, rows, width), BF16),
            vm(token, BF16),
            vm((cols * nb * rows, 2 * width), BF16),
            vm(token, BF16),
            vm((nb, rows, HEAD), BF16),
            vm((rows, width), BF16),
            vm(token, F32),
            vm((2 * ff_blocks + 4, width, width), BF16),
            vm((11, 16, width), F32),
            vm((8 + ff_blocks, width), F32),
            dma((5,)),
            dma((7,)),
            dma((4,)),
            dma((16,)),
            dma((nb,)),
            dma((nb,)),
            dma((cols, nb, 2)),
            dma((cols, nb)),
            dma((cols, nb)),
            dma((cols, nb + 1)),
            dma((len(GROUPS), 19)),
            dma((len(GROUPS), 19)),
            dma((6,)),
            dma((6,)),
            pltpu.SemaphoreType.REGULAR((3,)),
            pltpu.SemaphoreType.REGULAR((len(GROUPS),)),
        ],
        compiler_params=pltpu.CompilerParams(
            collective_id=0, has_side_effects=True, vmem_limit_bytes=64 * 1024 * 1024
        ),
    )(
        cells_t,
        cot_t,
        jnp.transpose(missing, (2, 0, 1)),
        context,
        miss_embed,
        norm1_gain,
        norm1_shift,
        norm2_gain,
        norm2_shift,
        norm3_gain,
        norm3_shift,
        ff_out_bias,
        ff_in_bias,
        feat_qkv,
        feat_out,
        row_qkv,
        row_out,
        ff_in,
        ff_out.reshape(ff // 128, 128, width),
    )
    *results, gvec = results[:9]
    if not fused:
        results[2:], gvec = lax.psum(
            ([g.astype(F32) for g in results[2:]], gvec), ("tab", "blk")
        )
        results[2:] = [g.astype(BF16) for g in results[2:]]
    wide = [shape(g.shape, F32) for g in results[2:]]
    vectors = [shape((width,), F32)] * 8 + [shape((ff,), F32)]
    done = pl.pallas_call(
        finish_kernel,
        out_shape=(shape(token, BF16), shape(token, F32), *wide, *vectors),
        in_specs=[any_spec] * 8 + [vmem_spec],
        out_specs=(any_spec,) * 8 + (vmem_spec,) * 9,
        scratch_shapes=[vm(g.shape, BF16) for g in results[2:]]
        + [vm(g.shape, F32) for g in results[2:]]
        + [vm(token, BF16), vm(token, F32)]
        + [dma((8,)), dma((8,))],
        compiler_params=pltpu.CompilerParams(vmem_limit_bytes=64 * 1024 * 1024),
    )(*results, gvec)
    act, igrad, g_fqkv, g_fout, g_rqkv, g_rout, g_fin, g_fdn, *vectors = done
    embed, gain1, shift1, gain2, shift2, gain3, shift3, out_bias, in_bias = vectors
    return (
        jnp.transpose(act, (1, 0, 2))[None],
        jnp.transpose(igrad, (1, 0, 2))[None],
        embed,
        gain1,
        shift1,
        g_fqkv,
        g_fout,
        gain2,
        shift2,
        g_rqkv,
        g_rout,
        gain3,
        shift3,
        g_fin,
        in_bias,
        g_fdn,
        out_bias,
    )


def solution(mesh):
    split = (
        P("tab", "blk", None, None),
        P("tab", "blk", None),
        P("tab", "blk"),
        P("tab", "blk", None, None),
    )
    return jax.shard_map(
        per_device,
        mesh=mesh,
        in_specs=split + (P(),) * 15,
        out_specs=(P("tab", "blk", None, None),) * 2 + (P(),) * 15,
        check_vma=False,
    )
```

```python
import functools
import math

import jax
import jax.numpy as jnp
from jax import lax
from jax.experimental import pallas as pl
from jax.experimental.pallas import tpu as pltpu
from jax.sharding import PartitionSpec as P

HEADS = 4
HEAD = 128
EPS = 1e-05
SCALE = 1.0 / math.sqrt(HEAD)
MESH = pl.DeviceIdType.MESH
F32 = jnp.float32
BF16 = jnp.bfloat16
EMBED, GAIN1, SHIFT1, GAIN2, SHIFT2, GAIN3, SHIFT3, OUT_BIAS, IN_BIAS = range(9)
CHUNK = 64
GROUPS = ((0, 1), (2, 3), (4, 5), (6, 7), (8, 9, 10, 11), (12, 13), (14,), (15,))
PUMPS = {
    "head2": ((0, 0),),
    "head3": ((1, 0),),
    "row_kv0": ((0, 1), (2, 0)),
    "row_kv1": ((1, 1), (3, 0)),
    "norm2_1": ((2, 1),),
    "earlier": ((4, 0),),
    "window": ((0, 2), (1, 2), (3, 1), (2, 2), (0, 3)),
    "keys": ((4, 1), (1, 3), (3, 2)),
    "values": ((2, 3),),
    "normed1": ((6, 0), (7, 0)),
    "norm1_0": ((0, 4),),
    "norm1_1": ((4, 2), (5, 0), (1, 4)),
    "end0": ((6, 1), (3, 3), (7, 1), (0, 5), (2, 4), (5, 1)),
    "end1": ((1, 5), (6, 2), (7, 2), (4, 3), (0, 6), (3, 4), (2, 5), (6, 3), (5, 2)),
    "end2": ((0, 7), (7, 3), (1, 6), (3, 5), (1, 7), (4, 4), (2, 6), (6, 4), (3, 6), (2, 7)),
    "end3": ((5, 3), (7, 4), (4, 5), (3, 7), (6, 5), (7, 5), (5, 4), (4, 6), (6, 6), (7, 6), (4, 7)),
    "end4": ((5, 5), (6, 7), (7, 7), (5, 6), (5, 7)),
}
HALF = 256
STAGES = 8


def dot(a, b):
    return jnp.dot(a, b, preferred_element_type=F32)


def dot_rt(a, b):
    return lax.dot_general(a, b, (((1,), (1,)), ((), ())), preferred_element_type=F32)


def dot_lt(a, b):
    return lax.dot_general(a, b, (((0,), (0,)), ((), ())), preferred_element_type=F32)


def stats(x):
    center = x - jnp.mean(x, axis=-1, keepdims=True)
    rstd = lax.rsqrt(jnp.mean(center * center, axis=-1, keepdims=True) + EPS)
    return center * rstd, rstd


def norm_back(x, gain, dy):
    xhat, rstd = stats(x)
    dxh = dy * gain
    dx = rstd * (
        dxh
        - jnp.mean(dxh, axis=-1, keepdims=True)
        - xhat * jnp.mean(dxh * xhat, axis=-1, keepdims=True)
    )
    dgain = jnp.sum(dy * xhat, axis=0, keepdims=True)
    dshift = jnp.sum(dy, axis=0, keepdims=True)
    return dx, dgain, dshift


def layer_kernel(
    nb,
    fused,
    cells_h,
    cot_h,
    missing,
    context,
    *rest,
):
    vectors, rest = rest[:9], rest[9:]
    (
    wfqkv_h,
    wfout_h,
    wrqkv_h,
    wrout_h,
    wfin_h,
    wfdn_h,
    act_h,
    igrad_h,
    gfqkv_h,
    gfout_h,
    grqkv_h,
    grout_h,
    gfin_h,
    gfdn_h,
    gvec,
    n1_h,
    fqkv_h,
    fp_h,
    fo_h,
    cot,
    wrqkv,
    wrout,
    wfin,
    wfdn,
    wkvt,
    absent,
    af,
    n2,
    rss,
    rsr,
    g2,
    hid,
    gin,
    nro,
    gy2,
    dkv,
    dq,
    ctxa,
    act,
    dn2,
    gb,
    vland,
    vec,
    load_sem,
    feat_sem,
    stash_sem,
    out_sem,
    ctx_send,
    ctx_recv,
    ag_send,
    ag_recv,
    rs_send,
    rs_recv,
    ar_send,
    ar_recv,
    vec_send,
    vec_recv,
    ready,
    free,
    ) = rest
    cols, rows, width = g2.shape
    seg = width
    ff_blocks = wfin.shape[1] // seg
    quarter = rows // CHUNK
    ro_at = cols
    t = lax.axis_index("tab")
    z = lax.axis_index("blk")
    core, xbit, ybit = lax.rem(t, 2), lax.rem(lax.div(t, 2), 2), lax.rem(lax.div(t, 4), 2)
    on_core = (t + 1 - 2 * core, z)
    on_x = (t + 2 - 4 * xbit, z)
    on_y = (t + 4 - 8 * ybit, z)
    along = [(t, lax.rem(z + d, nb)) for d in range(1, nb)]
    partners = along + ([on_core, on_x, on_y] if fused else [])

    def load_all(pairs, sem):
        copies = [
            pltpu.make_async_copy(a, b, sem.at[i]) for i, (a, b) in enumerate(pairs)
        ]
        for copy in copies:
            copy.start()
        return copies

    def signal_all(sem):
        for device in partners:
            pl.semaphore_signal(sem, inc=1, device_id=device, device_id_type=MESH)

    def await_all(sem):
        pl.semaphore_wait(sem, len(partners))

    def remote(source, dest, send, recv, device):
        return pltpu.make_async_remote_copy(
            src_ref=source,
            dst_ref=dest,
            send_sem=send,
            recv_sem=recv,
            device_id=device,
            device_id_type=MESH,
        )

    def block(c, s):
        return n2.at[c * (nb // 2) + s // 2, pl.ds(pl.multiple_of((s % 2) * rows, rows), rows)]

    own_hi, own_lo = lax.div(z, 2), pl.multiple_of(lax.rem(z, 2) * rows, rows)

    def own_block(c):
        return n2.at[c * (nb // 2) + own_hi, pl.ds(own_lo, rows)]

    def on_each(run, devices=None):
        for me in range(nb) if devices is None else devices:

            @pl.when(z == me)
            def _():
                run(me)

    ends, middle = (0, nb - 1), tuple(range(1, nb - 1))

    def pass_on(c, s, me, step):
        return remote(
            block(c, s),
            block(c, s),
            ag_send.at[c, s, (step + 1) // 2],
            ag_recv.at[c, s],
            (t, me + step),
        )

    def await_block(c, s):
        pltpu.make_async_copy(block(c, s), block(c, s), ag_recv.at[c, s]).wait()

    def gather_sends(c, me, far):
        out = []
        for step in (-1, 1):
            if 0 <= me + step < nb and 0 <= me - far * step < nb:
                out.append((me - far * step, pass_on(c, me - far * step, me, step)))
        return out

    def start_gather(c, devices=None):
        def run(me):
            for _, copy in gather_sends(c, me, 0):
                copy.start()

        on_each(run, devices)

    def hop(c, far):
        def run(me):
            for s, copy in gather_sends(c, me, far):
                await_block(c, s)
                copy.start()

        on_each(run, middle)

    def await_gather(c):
        def run(me):
            for s in range(nb):
                if s != me:
                    await_block(c, s)

        on_each(run, ends)

    def await_gather_sends(c):
        def run(me):
            for far in range(nb - 1):
                for _, copy in gather_sends(c, me, far):
                    copy.wait_send()

        on_each(run)

    def slot_of(owner, me):
        return nb if owner == me else owner

    def rs_copy(c, owner, me):
        step = 1 if owner > me else -1
        there = owner if step < 0 else slot_of(owner, me + step)
        return remote(
            rss.at[c, owner],
            rsr.at[c, there],
            rs_send.at[c, owner],
            rs_recv.at[c, there],
            (t, me + step),
        )

    def scatter(c, part):
        def run(me):
            order = sorted((o for o in range(nb) if o != me), key=lambda o: -abs(o - me))
            if part > 0:
                rs_copy(c, order[part - 1], me).wait_send()
            rs_copy(c, order[part], me).start()

        on_each(run, ends)

    def await_slot(c, s):
        pltpu.make_async_copy(rsr.at[c, s], rsr.at[c, s], rs_recv.at[c, s]).wait()

    def combine(c, part):
        def run(me):
            low = me == 1
            owner = (nb - 1, nb - 2, 0)[part] if low else (0, 1, nb - 1)[part]
            await_slot(c, owner)
            rss[c, owner] = (rss[c, owner].astype(F32) + rsr[c, owner].astype(F32)).astype(BF16)
            rs_copy(c, owner, me).start()

        on_each(run, middle)

    def own_slots(me):
        return [] if me == nb - 1 else [me], [] if me == 0 else [nb]

    def await_scatter_sends(c):
        def run(me):
            for owner in range(nb):
                if owner != me and (me in middle or abs(owner - me) == 1):
                    rs_copy(c, owner, me).wait_send()

        on_each(run)

    groups = []
    for members in GROUPS:
        first, count = members[0], len(members)
        if first < 4:
            land = rss.at[0, pl.ds(first, count)]
        else:
            land = hid.at[pl.ds(first - 4, count)]
        array, place = (gb, first) if first < 12 else (n2, first - 12)
        groups.append((array, place, count, first, land))

    reached = [0] * len(GROUPS)
    started = set()

    def pump(point):
        for g, stage in PUMPS.get(point, ()):
            next_sum(g, stage)

    lanes_a, lanes_b = pl.ds(0, HALF), pl.ds(HALF, HALF)

    def at16(v):
        return pl.multiple_of(v, 16)

    row_core = core * 256
    paths = [(lanes_a, xbit, ybit, on_x, on_y), (lanes_b, ybit, xbit, on_y, on_x)]

    def landing(g, stage):
        _, _, n, first, land = groups[g]
        if stage == 0:
            return land
        if stage == 1:
            return wfdn.at[pl.ds(first, n)]
        return gin.at[pl.ds(first + (16 if stage == 3 else 0), n)]

    def sum_copies(g, stage):
        ref, place, n, _, _ = groups[g]
        whole = pl.ds(0, width)

        def final(row, count, lanes):
            return ref.at[pl.ds(place, n), pl.ds(at16(row), count), lanes]

        out = []
        if stage == 0:
            out.append((final((1 - core) * 256, 256, whole), landing(g, 0), on_core))
        elif stage == 1:
            for lanes, bit, _, device, _ in paths:
                away = landing(g, 0).at[:, pl.ds(at16((1 - bit) * 128), 128), lanes]
                out.append((away, landing(g, 1).at[:, :, lanes], device))
        elif stage == 2:
            for lanes, _, bit, _, device in paths:
                away = landing(g, 1).at[:, pl.ds(at16((1 - bit) * 64), 64), lanes]
                out.append((away, landing(g, 2).at[:, :, lanes], device))
        elif stage == 3:
            for d in range(1, nb):
                away = landing(g, 2).at[:, pl.ds(at16(lax.rem(z + d, nb) * 16), 16), :]
                out.append((away, landing(g, 3).at[:, pl.ds((d - 1) * 16, 16), :], along[d - 1]))
        elif stage == 4:
            for d in range(1, nb):
                for lanes, bit1, bit2, _, _ in paths:
                    row = row_core + bit1 * 128 + bit2 * 64 + z * 16
                    mine = landing(g, 3).at[:, pl.ds(0, 16), lanes]
                    out.append((mine, final(row, 16, lanes), along[d - 1]))
        elif stage == 5:
            for lanes, bit1, bit2, _, device in paths:
                mine = final(row_core + bit1 * 128 + bit2 * 64, 64, lanes)
                out.append((mine, mine, device))
        elif stage == 6:
            for lanes, bit1, _, device, _ in paths:
                mine = final(row_core + bit1 * 128, 128, lanes)
                out.append((mine, mine, device))
        else:
            mine = final(row_core, 256, whole)
            out.append((mine, mine, on_core))
        first = (0, 1, 3, 5, 8, 14, 16, 18)[stage]
        return [
            remote(a, b, ar_send.at[g, first + i], ar_recv.at[g, first + i], device)
            for i, (a, b, device) in enumerate(out)
        ]

    def start_stage(g, stage):
        if stage == STAGES - 1:
            pl.semaphore_wait(free.at[g], 1)
        for copy in sum_copies(g, stage):
            copy.start()

    def start_sum(*done):
        if not fused:
            return
        for group, members in enumerate(GROUPS):
            if any(b in done for b in members):
                started.update(b for b in done if b in members)
                if started.issuperset(members):
                    start_stage(group, 0)

    def add_landed(g, stage):
        ref, place, n, _, _ = groups[g]
        land = landing(g, stage)
        if stage == 0:
            for i in range(n):
                mine = ref[place + i, pl.ds(at16(row_core), 256), :]
                land[i] = (mine.astype(F32) + land[i].astype(F32)).astype(BF16)
            return
        last = landing(g, stage - 1)
        if stage == 3:
            total = last[:, pl.ds(at16(z * 16), 16), :].astype(F32)
            for d in range(1, nb):
                total = total + land[:, pl.ds((d - 1) * 16, 16), :].astype(F32)
            total = total.astype(BF16)
            land[:, pl.ds(0, 16), :] = total
            for i, (lanes, bit1, bit2, _, _) in enumerate(paths):
                row = at16(row_core + bit1 * 128 + bit2 * 64 + z * 16)
                ref[pl.ds(place, n), pl.ds(row, 16), lanes] = total[
                    :, :, i * HALF : (i + 1) * HALF
                ]
            return
        count = 128 if stage == 1 else 64
        for lanes, bit1, bit2, _, _ in paths:
            row = at16((bit1 if stage == 1 else bit2) * count)
            mine = last[:, pl.ds(row, count), lanes]
            land[:, :, lanes] = (mine.astype(F32) + land[:, :, lanes].astype(F32)).astype(BF16)

    def next_sum(g, stage):
        if not fused:
            return
        assert reached[g] == stage
        reached[g] += 1
        if stage == 1 and not any(later > 1 for later in reached[:g] + reached[g + 1 :]):
            await_all(ready.at[2])
        copies = sum_copies(g, stage)
        for copy in copies:
            copy.wait_recv()
        if stage < 4:
            add_landed(g, stage)
        if stage + 1 < STAGES:
            start_stage(g, stage + 1)
        else:
            for b in GROUPS[g]:
                start_out(b)
        if stage == 0:
            for copy in copies:
                copy.wait_send()
            pl.semaphore_signal(free.at[g], inc=1, device_id=on_core, device_id_type=MESH)

    def out_copies(g):
        if g < 4:
            dest = gfdn_h.at[pl.ds(g * seg, seg)]
        elif g in (8, 12):
            dest = grout_h if g == 8 else gfout_h
        else:
            dest = gfin_h if g < 8 else grqkv_h if g < 12 else gfqkv_h
            part = g - 4 if g < 8 else g - 9 if g < 12 else (2, 0, 1)[g - 13]
            dest = dest.at[:, pl.ds(part * seg, seg)]
        ref, place = (gb, g) if g < 12 else (n2, g - 12)
        return [pltpu.make_async_copy(ref.at[place], dest, out_sem.at[g])]

    def start_out(g):
        for copy in out_copies(g):
            copy.start()

    barrier = pltpu.get_barrier_semaphore()
    signal_all(barrier)
    marks = jnp.concatenate(
        [missing[:, 0, :].astype(F32), jnp.zeros((8 - cols, rows), F32)], axis=0
    ).T
    for c in range(cols):
        absent[c] = marks[:, c : c + 1]
    ctxa[z] = jnp.broadcast_to(context[...].astype(F32), (HEAD, rows)).T.astype(BF16)
    gvec[...] = jnp.zeros_like(gvec)

    for i, vector in enumerate(vectors):
        count = vector.shape[0] // width
        vec[i : i + count, :] = vector[...].astype(F32).reshape(count, width)

    def row(i):
        return vec[i : i + 1, :]

    ones = (
        lax.broadcasted_iota(jnp.int32, (width, HEAD), 0) // HEAD
        == lax.broadcasted_iota(jnp.int32, (width, HEAD), 1)
    ).astype(BF16)
    ones_t = (
        lax.broadcasted_iota(jnp.int32, (HEAD, width), 1) // HEAD
        == lax.broadcasted_iota(jnp.int32, (HEAD, width), 0)
    ).astype(BF16)

    def base_of(cells, c, r):
        return jnp.where(
            absent[c, pl.ds(r, CHUNK), :] > 0, row(EMBED), cells[c, pl.ds(r, CHUNK), :].astype(F32)
        )

    ctx_copies = [
        remote(ctxa.at[z], ctxa.at[z], ctx_send.at[d], ctx_recv.at[z], along[d])
        for d in range(nb - 1)
    ]

    weights = [(wrqkv_h, wrqkv), (wrout_h, wrout), (wfin_h, wfin), (wfdn_h, wfdn), (cot_h, cot)]
    loads = [
        pltpu.make_async_copy(a, b, load_sem.at[i]) for i, (a, b) in enumerate(weights)
    ]

    def feature_forward(cells, wfqkv, wfout, n1, fqkv, fp, fo, hi, lo, spread):
        feat_loads = load_all(
            [(cells_h, cells), (wfqkv_h, wfqkv), (wfout_h, wfout)], feat_sem
        )
        for copy in loads:
            copy.start()
        feat_loads[0].wait()
        for c in range(cols):
            for r in range(0, rows, CHUNK):
                xhat, _ = stats(base_of(cells, c, r))
                n1[c, pl.ds(r, CHUNK), :] = (xhat * row(GAIN1) + row(SHIFT1)).astype(BF16)
        await_all(barrier)
        for copy in ctx_copies:
            copy.start()
        feat_loads[1].wait()
        n1_all = n1[...].reshape(cols * rows, width)
        for b in range(3):
            fqkv[b] = (
                dot(n1_all, wfqkv[:, b * seg : (b + 1) * seg])
                .astype(BF16)
                .reshape(cols, rows, width)
            )
        stash = [(n1, n1_h), (fqkv, fqkv_h)]
        for i in range(cols):
            for j in range(cols):
                for r in range(0, rows, CHUNK):
                    prod = fqkv[0, i, pl.ds(r, CHUNK), :].astype(F32) * fqkv[
                        1, j, pl.ds(r, CHUNK), :
                    ].astype(F32)
                    top = prod.astype(BF16)
                    hi[pl.ds(j * rows + r, CHUNK), :] = top
                    lo[pl.ds(j * rows + r, CHUNK), :] = (prod - top.astype(F32)).astype(BF16)
            scores = (dot(hi[...], ones) + dot(lo[...], ones)) * SCALE
            parts = [scores[j * rows : (j + 1) * rows] for j in range(cols)]
            top = functools.reduce(jnp.maximum, parts)
            parts = [jnp.exp(part - top) for part in parts]
            inv = 1.0 / functools.reduce(jnp.add, parts)
            for j in range(cols):
                fp[i, j] = parts[j] * inv
            spread[...] = dot(fp[i].reshape(cols * rows, HEAD).astype(BF16), ones_t)
            weigh(spread, fqkv, 2, fo, None, i, 1.0)
            if i == 0:
                feat_loads[2].wait()
            spread[0:rows, :] = dot(fo[i], wfout[...])
            for r in range(0, rows, CHUNK):
                after = base_of(cells, i, r) + spread[pl.ds(r, CHUNK), :]
                af[i, pl.ds(r, CHUNK), :] = after
                xhat, _ = stats(after)
                n2[i * (nb // 2) + own_hi, pl.ds(pl.multiple_of(own_lo + r, CHUNK), CHUNK), :] = (
                    xhat * row(GAIN2) + row(SHIFT2)
                ).astype(BF16)
            if i == 0:
                start_gather(0)
        for copy in load_all(stash + [(fp, fp_h), (fo, fo_h)], stash_sem):
            copy.wait()

    def weigh(spread, source, part, dest, dest_part, i, scale):
        for r in range(0, rows, CHUNK):
            rr = pl.ds(r, CHUNK)
            total = functools.reduce(
                jnp.add,
                [
                    spread[pl.ds(j * rows + r, CHUNK), :]
                    * (source[j, rr, :] if part is None else source[part, j, rr, :]).astype(F32)
                    for j in range(cols)
                ],
            )
            total = (total * scale).astype(BF16)
            if dest_part is None:
                dest[i, rr, :] = total
            else:
                dest[dest_part, i, rr, :] = total

    token = (cols, rows, width)
    vm = pltpu.VMEM
    feature_scratch = [
        vm(token, BF16),
        vm(wfqkv_h.shape, BF16),
        vm(wfout_h.shape, BF16),
        vm(token, BF16),
        vm((3,) + token, BF16),
        vm((cols, cols, rows, HEAD), F32),
        vm(token, BF16),
        vm((cols * rows, width), BF16),
        vm((cols * rows, width), BF16),
        vm((cols * rows, width), F32),
    ]
    pl.run_scoped(feature_forward, *feature_scratch)
    hop(0, 1)
    start_gather(1, ends)

    loads[0].wait()
    for b in range(2):
        wkvt[b] = wrqkv[:, (b + 1) * seg : (b + 2) * seg].astype(F32).T.astype(BF16)
    for load in loads[1:]:
        load.wait()
    for s in range(nb):

        @pl.when(z != s)
        def _():
            pltpu.make_async_copy(ctxa.at[s], ctxa.at[s], ctx_recv.at[s]).wait()

    hop(0, 2)
    start_gather(1, middle)

    def ff_weight(f):
        return wfdn[pl.ds(f * (seg // 128), seg // 128)].reshape(seg, width)

    def gin_block(c, f):
        return pl.ds((c * ff_blocks + f) * quarter, quarter)

    def ff_out_weights():
        cot_all = cot[...].reshape(cols * rows, width)
        for f in range(ff_blocks):
            hid_all = jnp.concatenate([hid[c * ff_blocks + f] for c in range(cols)], axis=0)
            gb[f] = dot_lt(hid_all, cot_all).astype(BF16)
            if fused and f == 0:
                await_all(ready.at[0])
            start_sum(f)
        if fused:
            signal_all(ready.at[1])
        pump("ff_out")

    def ff_in_weights():
        if fused:
            await_all(ready.at[1])
        n3_all = nro[0:cols].reshape(cols * rows, width)
        for f in range(ff_blocks):
            gin_all = jnp.concatenate(
                [gin[gin_block(c, f)].reshape(rows, seg) for c in range(cols)], axis=0
            )
            gb[ff_blocks + f] = dot_lt(n3_all, gin_all).astype(BF16)
            start_sum(4 + f)
        pump("ff_in")
        gb[8] = dot_lt(
            nro[ro_at : ro_at + cols].reshape(cols * rows, width),
            gy2[...].reshape(cols * rows, width),
        ).astype(BF16)
        if fused:
            signal_all(ready.at[2])
        start_sum(8)
        pump("row_out")

    def columns_stage(q, kv, kvt, gro, p, scores, dsb, ot, rof, dgel, ar):
        def wide(ref, value):
            for h in range(HEADS):
                ref[:, h * 2 * HEAD : h * 2 * HEAD + HEAD] = value[:, h * HEAD : (h + 1) * HEAD]

        def extra(ref, rr, value):
            for h in range(HEADS):
                ref[rr, h * 2 * HEAD + HEAD : (h + 1) * 2 * HEAD] = value

        def lanes_of(count):
            return lax.broadcasted_iota(jnp.int32, (count, HEAD), 1)

        first = lanes_of(rows) == 0
        extra(q, slice(None), first.astype(BF16))
        for s in range(nb):
            rr = slice(s * rows, (s + 1) * rows)
            mask = jnp.where(first, (ctxa[s].astype(F32) - 1.0) * 1e30, 0.0)
            extra(kv.at[0], rr, mask.astype(BF16))
            extra(kv.at[1], rr, (lanes_of(rows) < 2).astype(BF16))
        keys_in = nb * rows
        step = 2 * CHUNK

        def fold(part, op):
            return op(part.reshape(step // 8, 8, part.shape[-1]), axis=0)

        exponent = SCALE * math.log2(math.e)

        def act_copy(c):
            return pltpu.make_async_copy(act, act_h.at[c], stash_sem.at[c])

        def on_last(c, point):
            if fused and PUMPS.get(point):

                @pl.when(c == cols - 1)
                def _():
                    pump(point)

        def column(c, _):
            await_gather(c)
            x = n2[pl.ds(c * (nb // 2), nb // 2)].reshape(nb * rows, width)
            own = n2[c * (nb // 2) + own_hi, pl.ds(own_lo, rows), :]
            wide(q, dot(own, wrqkv[:, 0:seg]).astype(BF16))
            wide(kv.at[0], dot(x, wrqkv[:, seg : 2 * seg]).astype(BF16))
            kvt[1] = dot_rt(wkvt[1], x).astype(BF16)
            for h in range(HEADS):
                hs = slice(h * HEAD, (h + 1) * HEAD)
                hw = slice(h * 2 * HEAD, (h + 1) * 2 * HEAD)
                sh = scores.at[h % 2]
                sh[...] = dot_rt(kv[0, :, hw], q[:, hw])
                top = functools.reduce(
                    jnp.maximum,
                    [fold(sh[r : r + step, :], jnp.max) for r in range(0, keys_in, step)],
                )
                top = jnp.max(top, axis=0, keepdims=True) * exponent
                total = jnp.zeros((8, rows), F32)
                for r in range(0, keys_in, step):
                    e = jnp.exp2(sh[r : r + step, :] * exponent - top)
                    sh[r : r + step, :] = e
                    total = total + fold(e, jnp.sum)
                inv = 1.0 / jnp.sum(total, axis=0, keepdims=True)
                for r in range(0, keys_in, step):
                    p[h, r : r + step, :] = (sh[r : r + step, :] * inv).astype(BF16)
                ot[hs, :] = dot(kvt[1, hs, :], p[h])
            rof[...] = ot[...].T
            nro[ro_at + c] = rof[...].astype(BF16)

            @pl.when(c + 1 < cols)
            def _():
                hop(c + 1, 1)

            @pl.when(c > 0)
            def _():
                scatter(c - 1, 1)

            ar[...] = dot(nro[ro_at + c], wrout[...])
            for r in range(0, rows, CHUNK):
                rr = pl.ds(r, CHUNK)
                after = af[c, rr, :] + ar[rr, :]
                ar[rr, :] = after
                xhat, _ = stats(after)
                nro[c, rr, :] = (xhat * row(GAIN3) + row(SHIFT3)).astype(BF16)
            for f in range(ff_blocks):
                fs = slice(f * seg, (f + 1) * seg)
                dgel[f] = dot(nro[c], wfin[:, fs])
                for r in range(0, rows, CHUNK // 2):
                    rr = pl.ds(r, CHUNK // 2)
                    u = dgel[f, rr, :] + row(IN_BIAS + f)
                    c0 = math.sqrt(2.0 / math.pi)
                    c1 = c0 * 0.044715
                    sq = u * u
                    half = 0.5 + 0.5 * jnp.tanh(u * (c0 + c1 * sq))
                    out = u * half
                    hid[c * ff_blocks + f, rr, :] = out.astype(BF16)
                    dgel[f, rr, :] = half + out * (1.0 - half) * (2.0 * c0 + (6.0 * c1) * sq)
            total = ar[...] + row(OUT_BIAS)
            for f in range(ff_blocks):
                total = total + dot(hid[c * ff_blocks + f], ff_weight(f))

            @pl.when(c > 0)
            def _():
                act_copy(c - 1).wait()

            act[...] = total.astype(BF16)

            @pl.when(c >= 0)
            def _():
                act_copy(c).start()


            back = jnp.zeros((rows, width), F32)
            for f in range(ff_blocks):
                fs = slice(f * seg, (f + 1) * seg)
                gi = (dot_rt(cot[c], ff_weight(f)) * dgel[f]).astype(BF16)
                gin[gin_block(c, f)] = gi.reshape(quarter, CHUNK, seg)
                gvec[IN_BIAS + f : IN_BIAS + f + 1, :] += jnp.sum(
                    gi.astype(F32), axis=0, keepdims=True
                )
                back = back + dot_rt(gi, wfin[:, fs])

            @pl.when(c == cols - 1)
            def _():
                await_scatter_sends(0)
                if fused:
                    signal_all(ready.at[0])

            dgel[0] = back
            for r in range(0, rows, CHUNK):
                rr = pl.ds(r, CHUNK)
                dx, dgain, dshift = norm_back(ar[rr, :], row(GAIN3), dgel[0, rr, :])
                g3 = cot[c, rr, :].astype(F32)
                g = g3 + dx
                g2[c, rr, :] = g
                gy2[c, rr, :] = g.astype(BF16)
                gvec[GAIN3 : GAIN3 + 1, :] += dgain
                gvec[SHIFT3 : SHIFT3 + 1, :] += dshift
                gvec[OUT_BIAS : OUT_BIAS + 1, :] += jnp.sum(g3, axis=0, keepdims=True)


            @pl.when(c + 1 < cols)
            def _():
                hop(c + 1, 2)

            @pl.when(c + 2 < cols)
            def _():
                start_gather(c + 2)

            @pl.when(c == cols - 1)
            def _():
                ff_out_weights()

            @pl.when(c > 0)
            def _():
                scatter(c - 1, 2)

            wide(gro, dot_rt(gy2[c], wrout[...]).astype(BF16))
            for h in range(HEADS):
                hs = slice(h * HEAD, (h + 1) * HEAD)
                mean = jnp.sum(
                    rof[:, hs] * gro[:, h * 2 * HEAD : h * 2 * HEAD + HEAD].astype(F32),
                    axis=1,
                    keepdims=True,
                )
                high = mean.astype(BF16).astype(F32)
                gro[:, h * 2 * HEAD + HEAD : (h + 1) * 2 * HEAD] = jnp.where(
                    first, -high, jnp.where(lanes_of(rows) == 1, high - mean, 0.0)
                ).astype(BF16)
            wide(kv.at[1], dot(x, wrqkv[:, 2 * seg : 3 * seg]).astype(BF16))
            kvt[0] = dot_rt(wkvt[0], x).astype(BF16)
            on_last(c, "values_again")
            table = pl.ds(pl.multiple_of(c * nb * rows, nb * rows), nb * rows)
            for h in range(HEADS):
                hs = slice(h * HEAD, (h + 1) * HEAD)
                hw = slice(h * 2 * HEAD, (h + 1) * 2 * HEAD)
                hn = slice(h * 2 * HEAD, h * 2 * HEAD + HEAD)
                vs = slice(width + h * HEAD, width + (h + 1) * HEAD)
                sh, dh = scores.at[h % 2], dsb.at[h % 2]
                sh[...] = dot_rt(kv[1, :, hw], gro[:, hw])
                for r in range(0, keys_in, step):
                    dh[r : r + step, :] = (
                        p[h, r : r + step, :].astype(F32) * sh[r : r + step, :]
                    ).astype(BF16)
                dkv[table, hs] = (dot(dh[...], q[:, hn]) * SCALE).astype(BF16)
                dkv[table, vs] = dot(p[h], gro[:, hn]).astype(BF16)
                ot[hs, :] = dot(kvt[0, hs, :], dh[...])
                on_last(c, f"head{h}")
            dq[c] = (ot[...].T * SCALE).astype(BF16)

            @pl.when(c > 0)
            def _():
                combine(c - 1, 0)


            for o in range(nb):
                part = pl.ds(pl.multiple_of((c * nb + o) * rows, rows), rows)
                rss[c, o] = dot_rt(dkv[part, :], wrqkv[:, seg : 3 * seg]).astype(BF16)
            scatter(c, 0)

            on_last(c, "scatter")
            @pl.when(c == cols - 1)
            def _():
                ff_in_weights()

            dn2[c] = dot_rt(dq[c], wrqkv[:, 0:seg]) + rss[c, z].astype(F32)

            @pl.when(c > 0)
            def _():
                combine(c - 1, 1)
                combine(c - 1, 2)

            return 0

        lax.fori_loop(0, cols, column, 0)
        act_copy(cols - 1).wait()

    pl.run_scoped(
        columns_stage,
        vm((rows, 2 * width), BF16),
        vm((2, nb * rows, 2 * width), BF16),
        vm((2, width, nb * rows), BF16),
        vm((rows, 2 * width), BF16),
        vm((HEADS, nb * rows, rows), BF16),
        vm((2, nb * rows, rows), F32),
        vm((2, nb * rows, rows), BF16),
        vm((width, rows), F32),
        vm((rows, width), F32),
        vm((ff_blocks, rows, width), F32),
        vm((rows, width), F32),
    )

    def feature_backward(
        cells, wfqkv, wfout, n1, fqkv, fp, fo, hi, lo, spread, gfo, dqkv, dsl, more
    ):
        again = load_all(
            [
                (cells_h, cells),
                (wfqkv_h, wfqkv),
                (wfout_h, wfout),
                (n1_h, n1),
                (fqkv_h, fqkv),
                (fp_h, fp),
                (fo_h, fo),
            ],
            feat_sem,
        )
        pump("columns")
        x_all = n2[...].reshape(cols * nb * rows, width)
        half = width // 2
        for i in range(2):
            at = slice(i * half, (i + 1) * half)
            got = dot_lt(x_all[:, at], dkv[...]).astype(BF16)
            gb[10, at, :] = got[:, 0:seg]
            gb[11, at, :] = got[:, seg:]
            if i == 1:
                start_sum(10, 11)
            if i == 0:
                scatter(cols - 1, 1)
                combine(cols - 1, 0)
            pump(f"row_kv{i}")
        own = jnp.concatenate(
            [n2[c * (nb // 2) + own_hi, pl.ds(own_lo, rows), :] for c in range(cols)], axis=0
        )
        gb[9] = dot_lt(own, dq[...].reshape(cols * rows, width)).astype(BF16)
        start_sum(9)
        pump("row_q")
        for copy in again:
            copy.wait()
        for c in range(cols):
            await_gather_sends(c)

        def column_back(c):
            def arrived(me):
                above, below = own_slots(me)
                for s in above + below:
                    await_slot(c, s)
                    dn2[c] += rsr[c, s].astype(F32)

            on_each(arrived)
            for r in range(0, rows, CHUNK):
                rr = pl.ds(r, CHUNK)
                dy = dn2[c, rr, :]
                dx, dgain, dshift = norm_back(af[c, rr, :], row(GAIN2), dy)
                g = g2[c, rr, :] + dx
                g2[c, rr, :] = g
                gy2[c, rr, :] = g.astype(BF16)
                gvec[GAIN2 : GAIN2 + 1, :] += dgain
                gvec[SHIFT2 : SHIFT2 + 1, :] += dshift
            gfo[c] = dot_rt(gy2[c], wfout[...]).astype(BF16)
            for j in range(cols):
                for r in range(0, rows, CHUNK):
                    prod = gfo[c, pl.ds(r, CHUNK), :].astype(F32) * fqkv[
                        2, j, pl.ds(r, CHUNK), :
                    ].astype(F32)
                    top = prod.astype(BF16)
                    hi[pl.ds(j * rows + r, CHUNK), :] = top
                    lo[pl.ds(j * rows + r, CHUNK), :] = (prod - top.astype(F32)).astype(BF16)
            dp = dot(hi[...], ones) + dot(lo[...], ones)
            parts = [dp[j * rows : (j + 1) * rows] for j in range(cols)]
            mean = functools.reduce(jnp.add, [fp[c, j] * parts[j] for j in range(cols)])
            for j in range(cols):
                dsl[c, j] = (fp[c, j] * (parts[j] - mean)).astype(BF16)
            spread[...] = dot(dsl[c].reshape(cols * rows, HEAD), ones_t)
            weigh(spread, fqkv, 1, dqkv, 0, c, SCALE)

        def earlier(terms, source, part, sums):
            for j in range(cols):
                spread[0 : (cols - 1) * rows, :] = dot(
                    jnp.concatenate([terms[i, j].astype(BF16) for i in range(cols - 1)], axis=0),
                    ones_t,
                )
                for r in range(0, rows, CHUNK):
                    rr = pl.ds(r, CHUNK)
                    sums[j][rr, :] = functools.reduce(
                        jnp.add,
                        [
                            spread[pl.ds(i * rows + r, CHUNK), :]
                            * (source[i, rr, :] if part is None else source[part, i, rr, :]).astype(
                                F32
                            )
                            for i in range(cols - 1)
                        ],
                    )

        def finish(source, part, sums, dest_part, scale):
            last = cols - 1
            for j in range(cols):
                for r in range(0, rows, CHUNK):
                    rr = pl.ds(r, CHUNK)
                    mine = source[last, rr, :] if part is None else source[part, last, rr, :]
                    total = sums[j][rr, :] + spread[pl.ds(j * rows + r, CHUNK), :] * mine.astype(F32)
                    dqkv[dest_part, j, rr, :] = (total * scale).astype(BF16)

        n1_flat = n1[...].reshape(cols * rows, width)

        def part_done(b):
            at = (1, 2, 0)[b]
            n2[1 + at] = dot_lt(n1_flat, dqkv[b].reshape(cols * rows, width)).astype(BF16)
            start_sum(13 + at)

        sums_k = [af.at[0], af.at[1], more.at[0]]
        sums_v = [dn2.at[0], dn2.at[1], more.at[1]]
        column_back(0)
        scatter(cols - 1, 2)
        combine(cols - 1, 1)
        pump("norm2_0")
        for c in range(1, cols - 1):
            column_back(c)
        combine(cols - 1, 2)
        pump("norm2_1")
        earlier(dsl, fqkv, 0, sums_k)
        pump("earlier")
        earlier(fp, gfo, None, sums_v)
        pump("window")
        column_back(cols - 1)
        pump("norm2_2")
        finish(fqkv, 0, sums_k, 1, SCALE)
        part_done(0)
        part_done(1)
        pump("keys")
        spread[...] = dot(fp[cols - 1].reshape(cols * rows, HEAD).astype(BF16), ones_t)
        finish(gfo, None, sums_v, 2, 1.0)
        n2[0] = dot_lt(
            fo[...].reshape(cols * rows, width), gy2[...].reshape(cols * rows, width)
        ).astype(BF16)
        start_sum(12)
        part_done(2)
        pump("values")
        spread[...] = functools.reduce(
            jnp.add,
            [
                dot_rt(dqkv[b].reshape(cols * rows, width), wfqkv[:, b * seg : (b + 1) * seg])
                for b in range(3)
            ],
        )
        pump("normed1")
        for c in range(cols):
            for r in range(0, rows, CHUNK):
                rr = pl.ds(r, CHUNK)
                dx, dgain, dshift = norm_back(
                    base_of(cells, c, r), row(GAIN1), spread[pl.ds(c * rows + r, CHUNK), :]
                )
                g = g2[c, rr, :] + dx
                gone = absent[c, rr, :] > 0
                g2[c, rr, :] = jnp.where(gone, 0.0, g)
                gvec[GAIN1 : GAIN1 + 1, :] += dgain
                gvec[SHIFT1 : SHIFT1 + 1, :] += dshift
                gvec[EMBED : EMBED + 1, :] += jnp.sum(
                    jnp.where(gone, g, 0.0), axis=0, keepdims=True
                )
            pump(f"norm1_{c}")

    pl.run_scoped(
        feature_backward,
        *feature_scratch,
        vm(token, BF16),
        vm((3,) + token, BF16),
        vm((cols, cols, rows, HEAD), BF16),
        vm((2, rows, width), F32),
    )
    igrad_copy = pltpu.make_async_copy(g2, igrad_h, stash_sem.at[cols])
    igrad_copy.start()

    vec_copies = []

    def vec_step(k, devices):
        copies = [
            remote(
                vland.at[k],
                vland.at[4 + k + i],
                vec_send.at[k + i],
                vec_recv.at[k + i],
                device,
            )
            for i, device in enumerate(devices)
        ]
        vland[k] = gvec[...]
        for copy in copies:
            copy.start()
        vec_copies.extend(copies)
        return copies

    def vec_add(copies, k):
        for copy in copies:
            copy.wait_recv()
        if len(copies) == 1:
            gvec[...] = gvec[...] + vland[4 + k]
        else:
            vland[4 + k + nb - 1] = gvec[...]
            total = jnp.zeros_like(gvec)
            for s in range(nb):
                total = total + vland[4 + k + lax.rem(z + nb - s + nb - 1, nb)]
            gvec[...] = total

    if fused:
        step = vec_step(0, [on_core])
        pump("end0")
        vec_add(step, 0)
        step = vec_step(1, [on_x])
        pump("end1")
        vec_add(step, 1)
        step = vec_step(2, [on_y])
        pump("end2")
        vec_add(step, 2)
        step = vec_step(3, along)
        pump("end3")
        vec_add(step, 3)
        pump("end4")
        assert all(stage == STAGES for stage in reached)
    else:
        for g in range(16):
            start_out(g)

    for c in range(cols):
        if c > 0:
            await_scatter_sends(c)

    for copy in ctx_copies + vec_copies:
        copy.wait_send()
    if fused:
        for g in range(len(groups)):
            for stage in range(1, STAGES):
                for copy in sum_copies(g, stage):
                    copy.wait_send()
    igrad_copy.wait()
    for g in range(16):
        for copy in out_copies(g):
            copy.wait()


def finish_kernel(*refs):
    ins, gvec, outs, vectors = refs[0:8], refs[8], refs[9:17], refs[17:26]
    low, high, same = refs[26:32], refs[32:38], refs[38:40]
    in_sem, out_sem = refs[40:]
    width = gvec.shape[1]
    part = 4 * CHUNK

    def parts(sources, dests, sems):
        out = []
        for source, dest in zip(sources, dests):
            for r in range(0, source.shape[0], part):
                rr = pl.ds(r, part)
                out.append(
                    pltpu.make_async_copy(source.at[rr], dest.at[rr], sems.at[2 + len(out)])
                )
        return out

    moves_in = [pltpu.make_async_copy(ins[i], same[i], in_sem.at[i]) for i in range(2)]
    moves_out = [pltpu.make_async_copy(same[i], outs[i], out_sem.at[i]) for i in range(2)]
    loads = parts(ins[2:], low, in_sem)
    stores = parts(high, outs[2:], out_sem)
    for copy in loads + moves_in:
        copy.start()
    for i, vector in enumerate(vectors):
        count = vector.shape[0] // width
        vector[...] = gvec[i : i + count, :].reshape(vector.shape)
    place = 0
    for source, dest in zip(low, high):
        for first in range(0, source.shape[0], part):
            loads[place].wait()

            def convert(i, _):
                at = pl.ds(pl.multiple_of(first + i * CHUNK, CHUNK), CHUNK)
                dest[at, :] = source[at, :].astype(F32)
                return 0

            lax.fori_loop(0, part // CHUNK, convert, 0)
            stores[place].start()
            place += 1
    for copy in moves_in:
        copy.wait()
    for copy in moves_out:
        copy.start()
    for copy in stores + moves_out:
        copy.wait()


def per_device(
    cells,
    missing,
    context,
    cotangent,
    miss_embed,
    norm1_gain,
    norm1_shift,
    feat_qkv,
    feat_out,
    norm2_gain,
    norm2_shift,
    row_qkv,
    row_out,
    norm3_gain,
    norm3_shift,
    ff_in,
    ff_in_bias,
    ff_out,
    ff_out_bias,
):
    _, rows, cols, width = cells.shape
    nb = lax.axis_size("blk")
    fused = lax.axis_size("tab") == 8
    ff = ff_in.shape[1]
    ff_blocks = ff // width

    cells_t = jnp.transpose(cells[0], (1, 0, 2))
    cot_t = jnp.transpose(cotangent[0], (1, 0, 2))
    any_spec = pl.BlockSpec(memory_space=pl.ANY)
    vmem_spec = pl.BlockSpec(memory_space=pltpu.VMEM)
    token = (cols, rows, width)
    vm = pltpu.VMEM
    dma = pltpu.SemaphoreType.DMA
    shape = jax.ShapeDtypeStruct
    results = pl.pallas_call(
        functools.partial(layer_kernel, nb, fused),
        out_shape=(
            shape(token, BF16),
            shape(token, F32),
            shape(feat_qkv.shape, BF16),
            shape(feat_out.shape, BF16),
            shape(row_qkv.shape, BF16),
            shape(row_out.shape, BF16),
            shape(ff_in.shape, BF16),
            shape(ff_out.shape, BF16),
            shape((16, width), F32),
            shape(token, BF16),
            shape((3,) + token, BF16),
            shape((cols, cols, rows, HEAD), F32),
            shape(token, BF16),
        ),
        in_specs=[any_spec] * 2 + [vmem_spec] * 11 + [any_spec] * 6,
        out_specs=(any_spec,) * 8 + (vmem_spec,) + (any_spec,) * 4,
        scratch_shapes=[
            vm(token, BF16),
            vm(row_qkv.shape, BF16),
            vm(row_out.shape, BF16),
            vm(ff_in.shape, BF16),
            vm((ff // 128, 128, width), BF16),
            vm((2, width, width), BF16),
            vm((cols, rows, 1), F32),
            vm(token, F32),
            vm((cols * nb // 2, 2 * rows, width), BF16),
            vm((cols, nb, rows, width), BF16),
            vm((cols, nb + 1, rows, width), BF16),
            vm(token, F32),
            vm((cols * ff_blocks, rows, width), BF16),
            vm((cols * ff_blocks * rows // CHUNK, CHUNK, width), BF16),
            vm((2 * cols, rows, width), BF16),
            vm(token, BF16),
            vm((cols * nb * rows, 2 * width), BF16),
            vm(token, BF16),
            vm((nb, rows, HEAD), BF16),
            vm((rows, width), BF16),
            vm(token, F32),
            vm((2 * ff_blocks + 4, width, width), BF16),
            vm((11, 16, width), F32),
            vm((8 + ff_blocks, width), F32),
            dma((5,)),
            dma((7,)),
            dma((4,)),
            dma((16,)),
            dma((nb,)),
            dma((nb,)),
            dma((cols, nb, 2)),
            dma((cols, nb)),
            dma((cols, nb)),
            dma((cols, nb + 1)),
            dma((len(GROUPS), 19)),
            dma((len(GROUPS), 19)),
            dma((6,)),
            dma((6,)),
            pltpu.SemaphoreType.REGULAR((3,)),
            pltpu.SemaphoreType.REGULAR((len(GROUPS),)),
        ],
        compiler_params=pltpu.CompilerParams(
            collective_id=0, has_side_effects=True, vmem_limit_bytes=64 * 1024 * 1024
        ),
    )(
        cells_t,
        cot_t,
        jnp.transpose(missing, (2, 0, 1)),
        context,
        miss_embed,
        norm1_gain,
        norm1_shift,
        norm2_gain,
        norm2_shift,
        norm3_gain,
        norm3_shift,
        ff_out_bias,
        ff_in_bias,
        feat_qkv,
        feat_out,
        row_qkv,
        row_out,
        ff_in,
        ff_out.reshape(ff // 128, 128, width),
    )
    *results, gvec = results[:9]
    if not fused:
        results[2:], gvec = lax.psum(
            ([g.astype(F32) for g in results[2:]], gvec), ("tab", "blk")
        )
        results[2:] = [g.astype(BF16) for g in results[2:]]
    wide = [shape(g.shape, F32) for g in results[2:]]
    vectors = [shape((width,), F32)] * 8 + [shape((ff,), F32)]
    done = pl.pallas_call(
        finish_kernel,
        out_shape=(shape(token, BF16), shape(token, F32), *wide, *vectors),
        in_specs=[any_spec] * 8 + [vmem_spec],
        out_specs=(any_spec,) * 8 + (vmem_spec,) * 9,
        scratch_shapes=[vm(g.shape, BF16) for g in results[2:]]
        + [vm(g.shape, F32) for g in results[2:]]
        + [vm(token, BF16), vm(token, F32)]
        + [dma((2 + sum(g.shape[0] for g in results[2:]) // (4 * CHUNK),))] * 2,
        compiler_params=pltpu.CompilerParams(vmem_limit_bytes=64 * 1024 * 1024),
    )(*results, gvec)
    act, igrad, g_fqkv, g_fout, g_rqkv, g_rout, g_fin, g_fdn, *vectors = done
    embed, gain1, shift1, gain2, shift2, gain3, shift3, out_bias, in_bias = vectors
    return (
        jnp.transpose(act, (1, 0, 2))[None],
        jnp.transpose(igrad, (1, 0, 2))[None],
        embed,
        gain1,
        shift1,
        g_fqkv,
        g_fout,
        gain2,
        shift2,
        g_rqkv,
        g_rout,
        gain3,
        shift3,
        g_fin,
        in_bias,
        g_fdn,
        out_bias,
    )


def solution(mesh):
    split = (
        P("tab", "blk", None, None),
        P("tab", "blk", None),
        P("tab", "blk"),
        P("tab", "blk", None, None),
    )
    return jax.shard_map(
        per_device,
        mesh=mesh,
        in_specs=split + (P(),) * 15,
        out_specs=(P("tab", "blk", None, None),) * 2 + (P(),) * 15,
        check_vma=False,
    )
```
